32 devices in a mesh: fsdp: 2 (over x), ctx: 4 (over z), tp: 4 (over y, core).
Axes of the slice: x: 2, y: 2, z: 4, core: 2. Of those that a mesh axis runs over, the one named last changes fastest.
Arguments:
- hidden: bfloat16 [2, 3072, 2560], P('fsdp', 'ctx'), may hold values from -6 to 6
- lengths: int32 [2], replicated, may hold values from 1024 to 3072, as said below
- teacher: bfloat16 [2, 3072, 2560], P('fsdp', ('ctx', 'tp')), may hold values from -6 to 6
- attn_gain: bfloat16 [2560], P(('fsdp', 'ctx', 'tp')), may hold values from 0.5 to 1.5
- query_weight: bfloat16 [2560, 2560], P(('fsdp', 'ctx', 'tp')), may hold values from -0.125 to 0.125
- kv_weight: bfloat16 [2560, 512], P(('fsdp', 'ctx', 'tp')), may hold values from -0.125 to 0.125
- out_weight: bfloat16 [2560, 2560], P(('fsdp', 'ctx', 'tp')), may hold values from -2.5 to 2.5
- mlp_gain: bfloat16 [2560], P(('fsdp', 'ctx', 'tp')), may hold values from 0.5 to 1.5
- gate_weight: bfloat16 [2560, 7680], P(('fsdp', 'ctx'), 'tp'), may hold values from -0.125 to 0.125
- up_weight: bfloat16 [2560, 7680], P(('fsdp', 'ctx'), 'tp'), may hold values from -0.125 to 0.125
- down_weight: bfloat16 [7680, 2560], P('tp', ('fsdp', 'ctx')), may hold values from -0.0625 to 0.0625
Outputs:
- output: bfloat16 [2, 3072, 2560], P('fsdp', ('ctx', 'tp'))
- loss: float32 [], replicated
- input_grad: float32 [2, 3072, 2560], P('fsdp', ('ctx', 'tp'))
- attn_gain_grad: float32 [2560], P(('fsdp', 'ctx', 'tp'))
- query_weight_grad: float32 [2560, 2560], P(('fsdp', 'ctx', 'tp'))
- kv_weight_grad: float32 [2560, 512], P(('fsdp', 'ctx', 'tp'))
- out_weight_grad: float32 [2560, 2560], P(('fsdp', 'ctx', 'tp'))
- mlp_gain_grad: float32 [2560], P(('fsdp', 'ctx', 'tp'))
- gate_weight_grad: float32 [2560, 7680], P(('fsdp', 'ctx'), 'tp')
- up_weight_grad: float32 [2560, 7680], P(('fsdp', 'ctx'), 'tp')
- down_weight_grad: float32 [7680, 2560], P('tp', ('fsdp', 'ctx'))
The draws below stay inside these ranges and needn't reach their ends.
Inputs may be any that keep to these rules, and one draw needn't show every extreme that they name: `lengths`: each sequence holds at least 1024 real tokens at its start; in every draw one sequence, chosen by the seed, fills all 3072 slots.
All inputs are finite; a program needn't handle non-finite values.
Results may differ from the reference program's by a relative error of at most 0.013.
Values may be sent and summed in bfloat16 or wider, within the bound.
No kernel may reach another device: no remote copies, remote signals or barrier semaphores. Data moves between devices by JAX's collectives and lax.ppermute only.
A program may use at most 320 MiB of HBM per device.

```python
import jax
import jax.numpy as jnp
from jax import lax

D = 2560
H = 10
HD = 256
FF = 7680
W = 2048
SEQ = 3072
NSEQ = 2


def draw_lengths(key, part):
    key = jax.random.fold_in(key, 7)
    pick_key, value_key = jax.random.split(key)
    drawn = jax.random.randint(value_key, (NSEQ,), SEQ // 3, SEQ + 1)
    chosen = jax.random.randint(pick_key, (), 0, NSEQ)
    return jnp.where(jnp.arange(NSEQ) == chosen, SEQ, drawn).astype(jnp.int32)


def steps_of(own_key, extent, shards, low, top_value):
    def one(axis_at, parts):
        draws = jax.random.uniform(jax.random.fold_in(jax.random.fold_in(own_key, 6), axis_at), (parts,), jnp.float32, low / len(shards), top_value / len(shards))
        return jnp.repeat(jnp.exp(draws), extent[axis_at] // parts).reshape((-1,) + (1,) * (len(extent) - axis_at - 1))

    level = one(*shards[0])
    for cut in shards[1:]:
        level = level * one(*cut)
    return level


def bell_draw(stream_key, shape, spread, reach, cuts=(), held_as=jnp.bfloat16):
    level = steps_of(stream_key, shape, cuts, -0.22, 0.18) if cuts else 1.0
    values = jax.random.normal(stream_key, shape, jnp.float32) * spread * level
    return jnp.minimum(jnp.maximum(values, -reach), reach).astype(held_as)


def setup_inputs(seed: int = 0) -> dict:
    seeds = jax.random.split(jax.random.key(seed), 12)
    return {
        "hidden": bell_draw(seeds[0], (NSEQ, SEQ, D), 1.0, 6.0, ((0, 2), (1, 4))),
        "lengths": draw_lengths(jax.random.fold_in(seeds[11], 71), 0),
        "teacher": bell_draw(seeds[2], (NSEQ, SEQ, D), 1.0, 6.0, ((0, 2), (1, 16))),
        "attn_gain": jnp.clip(1.0 + 0.1 * jax.random.normal(seeds[3], (D,), jnp.float32), 0.5, 1.5).astype(jnp.bfloat16),
        "query_weight": bell_draw(seeds[4], (D, H * HD), D ** -0.5, 0.125, ((0, 32),)),
        "kv_weight": bell_draw(seeds[5], (D, 2 * HD), D ** -0.5, 0.125, ((0, 32),)),
        "out_weight": bell_draw(seeds[6], (D, H * HD), (H * HD * 4 // W) ** -0.5, 2.5, ((0, 32),)),
        "mlp_gain": jnp.clip(1.0 + 0.1 * jax.random.normal(seeds[7], (D,), jnp.float32), 0.5, 1.5).astype(jnp.bfloat16),
        "gate_weight": bell_draw(seeds[8], (D, FF), D ** -0.5, 0.125, ((0, 8), (1, 4))),
        "up_weight": bell_draw(seeds[9], (D, FF), D ** -0.5, 0.125, ((0, 8), (1, 4))),
        "down_weight": bell_draw(seeds[10], (FF, D), FF ** -0.5, 0.0625, ((0, 4), (1, 8))),
    }


@jax.custom_vjp
def low(v):
    return lax.optimization_barrier(v.astype(jnp.bfloat16)).astype(jnp.float32)

@jax.custom_vjp
def low_back(v):
    return v

def low_keep(v):
    return (low(v), None)

def low_pass(kept, grad):
    return (grad,)

def back_keep(v):
    return (v, None)

def back_low(kept, grad):
    return (low(grad),)
low.defvjp(low_keep, low_pass)
low_back.defvjp(back_keep, back_low)
epsilon = 1e-06
lowest = -1e+30
highest = lax.Precision.HIGHEST

def rms_norm(values, scaling):
    return values * lax.rsqrt(lax.optimization_barrier(jnp.mean(values * values, axis=-1, keepdims=True)) + epsilon) * scaling

def rotary_tables(positions, head_size):
    quarter = head_size // 4
    frequency = 10000.0 ** (-(jnp.arange(quarter).astype(jnp.float32) * 4.0 / head_size))
    angle = positions.astype(jnp.float32)[:, None] * frequency[None, :]
    return (jnp.cos(angle), jnp.sin(angle))

def turn(values, cosine, sine):
    quarter = cosine.shape[-1]
    first_half = values[..., :quarter]
    second_half = values[..., quarter:2 * quarter]
    return jnp.concatenate([first_half * cosine - second_half * sine, second_half * cosine + first_half * sine, values[..., 2 * quarter:]], axis=-1)

def sequence_pass(inputs, length, target_rows, weights):
    attn_gain, query_weight, kv_weight, out_weight, mlp_gain, gate_weight, up_weight, down_weight = weights
    positions = jnp.arange(SEQ)
    cosine, sine = rotary_tables(positions, HD)
    normed = low(rms_norm(inputs, attn_gain))
    query_raw = low_back(jnp.dot(normed, query_weight, precision=highest))
    kv_raw = low_back(jnp.dot(normed, kv_weight, precision=highest))
    queries = low(turn(query_raw.reshape(SEQ, H, HD), cosine[:, None, :], sine[:, None, :]) * HD ** (-0.5))
    key_rows = low(turn(kv_raw[:, :HD], cosine, sine))
    value_rows = low(kv_raw[:, HD:])
    block_rows = min(512, SEQ)
    query_blocks = queries.reshape(SEQ // block_rows, block_rows, H, HD)

    def one_block(block_in):
        query_part, block_start = block_in
        query_pos = block_start + jnp.arange(block_rows)
        scores = low_back(jnp.einsum('qhd,kd->hqk', query_part, key_rows, precision=highest))
        allowed = (positions[None, :] <= query_pos[:, None]) & (positions[None, :] > query_pos[:, None] - W)
        scores = jnp.where(allowed[None], scores, lowest)
        row_max = lax.optimization_barrier(jnp.max(scores, axis=-1, keepdims=True))
        shifted = jnp.exp(scores - row_max)
        weights_soft = low(shifted / lax.optimization_barrier(jnp.sum(shifted, axis=-1, keepdims=True)))
        return jnp.einsum('hqk,kd->qhd', weights_soft, value_rows, precision=highest)
    block_starts = jnp.arange(SEQ // block_rows) * block_rows
    attended = lax.map(jax.checkpoint(one_block), (query_blocks, block_starts))
    attended = low(low_back(attended.reshape(SEQ, H * HD)))
    attn_out = low_back(lax.dot_general(attended, out_weight, (((1,), (1,)), ((), ())), precision=highest))
    residual = inputs + attn_out
    normed_two = low(rms_norm(residual, mlp_gain))
    gate_proj = low_back(jnp.dot(normed_two, gate_weight, precision=highest))
    up_proj = low_back(jnp.dot(normed_two, up_weight, precision=highest))
    hidden_act = low(jax.nn.gelu(gate_proj, approximate=True) * up_proj)
    ffn_out = low_back(jnp.dot(hidden_act, down_weight, precision=highest))
    valid_rows = (positions < length).astype(jnp.float32)[:, None]
    output = (residual + ffn_out) * valid_rows
    mismatch = output - target_rows
    return (output, jnp.sum(valid_rows * mismatch * mismatch))

def reference(hidden, lengths, teacher, attn_gain, query_weight, kv_weight, out_weight, mlp_gain, gate_weight, up_weight, down_weight):
    count = jnp.sum(lengths).astype(jnp.float32)
    target_all = teacher.astype(jnp.float32)

    def objective(inputs_all, *weights):

        def step(running, item):
            inputs, length, target_rows = item
            output, err_sum = jax.checkpoint(sequence_pass)(inputs, length, target_rows, weights)
            return (running + err_sum, output)
        total_err, outputs = lax.scan(step, jnp.zeros((), jnp.float32), (inputs_all, lengths, target_all))
        return (total_err * (NSEQ * SEQ) / (2.0 * count), (outputs, total_err))
    primals = (hidden.astype(jnp.float32), attn_gain.astype(jnp.float32), query_weight.astype(jnp.float32), kv_weight.astype(jnp.float32), out_weight.astype(jnp.float32), mlp_gain.astype(jnp.float32), gate_weight.astype(jnp.float32), up_weight.astype(jnp.float32), down_weight.astype(jnp.float32))
    value, backward, extras = jax.vjp(objective, *primals, has_aux=True)
    outputs, total_err = extras
    grads = backward(jnp.ones((), jnp.float32))
    loss = total_err / (count * D)
    return (outputs.astype(jnp.bfloat16), loss, grads[0], grads[1], grads[2], grads[3], grads[4], grads[5], grads[6], grads[7], grads[8])
```

```python
import jax
import jax.numpy as jnp
from jax import lax
from jax.experimental import pallas as pl
from jax.experimental.pallas import tpu as pltpu
from jax.sharding import PartitionSpec as P

W = 2048

epsilon = 1e-06
lowest = -1e30
ROWS = 256
VMEM_BYTES = 40 * 1024 * 1024


def flip(array, axis, bit):
    return lax.ppermute(array, axis, [(i, i ^ bit) for i in range(lax.axis_size(axis))])


def ring(array, axis, by=1):
    count = lax.axis_size(axis)
    return lax.ppermute(array, axis, [(i, (i + by) % count) for i in range(count)])


def shifted(array, axis, by):
    count = lax.axis_size(axis)
    pairs = [(i, i + by) for i in range(count) if 0 <= i + by < count]
    return lax.ppermute(array, axis, pairs)


def low(values):
    return values.astype(jnp.bfloat16)


def wide(values):
    return values.astype(jnp.float32)


def take(array, index, axis=0):
    return lax.dynamic_index_in_dim(array, index, axis, keepdims=False)


def swapped(blocks, rank):
    if len(blocks) == 2:
        odd = rank == 1
        return [jnp.where(odd, blocks[1], blocks[0]), jnp.where(odd, blocks[0], blocks[1])]
    first = swapped(blocks[:2], rank % 2) + swapped(blocks[2:], rank % 2)
    outer = rank // 2 == 1
    return [jnp.where(outer, first[i ^ 2], first[i]) for i in range(4)]


def place(pieces, slots):
    count = len(pieces)
    shape = pieces[0].shape

    def body(slots_ref, *refs):
        out_ref, held, came, left = refs[count:]
        into = [pltpu.make_async_copy(refs[k], held.at[k], came.at[k]) for k in range(count)]
        out_of = [
            pltpu.make_async_copy(held.at[k], out_ref.at[slots_ref[k]], left.at[k])
            for k in range(count)
        ]
        for copy in into:
            copy.start()
        for first, second in zip(into, out_of):
            first.wait()
            second.start()
        for copy in out_of:
            copy.wait()

    return pl.pallas_call(
        body,
        out_shape=jax.ShapeDtypeStruct((count,) + shape, pieces[0].dtype),
        grid_spec=pltpu.PrefetchScalarGridSpec(
            num_scalar_prefetch=1,
            grid=(1,),
            in_specs=[pl.BlockSpec(memory_space=pl.ANY)] * count,
            out_specs=pl.BlockSpec(memory_space=pl.ANY),
            scratch_shapes=[
                pltpu.VMEM((count,) + shape, pieces[0].dtype),
                pltpu.SemaphoreType.DMA((count,)),
                pltpu.SemaphoreType.DMA((count,)),
            ],
        ),
        compiler_params=pltpu.CompilerParams(vmem_limit_bytes=VMEM_BYTES),
        name="place",
    )(jnp.stack(slots).astype(jnp.int32), *pieces)


def nn(first, second):
    return lax.dot_general(
        first, second, (((1,), (0,)), ((), ())), preferred_element_type=jnp.float32
    )


def nt(first, second):
    return lax.dot_general(
        first, second, (((1,), (1,)), ((), ())), preferred_element_type=jnp.float32
    )


def tn(first, second):
    return lax.dot_general(
        first, second, (((0,), (0,)), ((), ())), preferred_element_type=jnp.float32
    )


def ring_sum(block_of, axis):
    count = lax.axis_size(axis)
    rank = lax.axis_index(axis)
    moving = None
    for step in range(1, count):
        term = block_of((rank - step) % count)
        moving = low(term if moving is None else wide(moving) + wide(term))
        moving = ring(moving, axis)
    own = wide(block_of(rank))
    return own if moving is None else own + wide(moving)


def attention_forward(queries, keyvals, live, first_key, head_size):
    rows, columns = queries.shape
    heads = columns // head_size
    reach = W + ROWS
    lead = keyvals.shape[0] - rows - W

    def body(info_ref, q_ref, kv_ref, o_ref):
        head, block = pl.program_id(0), pl.program_id(1)
        start = pl.multiple_of(lead + block * ROWS, ROWS)
        keys = kv_ref[pl.ds(start, reach), :head_size]
        vals = kv_ref[pl.ds(start, reach), head_size:]
        scores = nt(q_ref[...], keys)
        row = lax.broadcasted_iota(jnp.int32, scores.shape, 0)
        column = lax.broadcasted_iota(jnp.int32, scores.shape, 1)
        ahead = column - row
        allowed = (ahead > 0) & (ahead <= W) & (column >= info_ref[0] - start)
        scores = jnp.where(allowed, scores, lowest)
        peak = jnp.max(scores, axis=1, keepdims=True)
        shares = jnp.exp(scores - peak)
        total = jnp.sum(shares, axis=1, keepdims=True)
        probs = low(shares * (1.0 / total))
        mixed = nn(probs, vals)
        o_ref[...] = low(mixed * wide(info_ref[1 + head]))

    return pl.pallas_call(
        body,
        out_shape=jax.ShapeDtypeStruct((rows, columns), jnp.bfloat16),
        grid_spec=pltpu.PrefetchScalarGridSpec(
            num_scalar_prefetch=1,
            grid=(heads, rows // ROWS),
            in_specs=[
                pl.BlockSpec((ROWS, head_size), lambda h, i, info: (i, h)),
                pl.BlockSpec(keyvals.shape, lambda h, i, info: (0, 0)),
            ],
            out_specs=pl.BlockSpec((ROWS, head_size), lambda h, i, info: (i, h)),
        ),
        compiler_params=pltpu.CompilerParams(vmem_limit_bytes=VMEM_BYTES),
        cost_estimate=pl.CostEstimate(
            flops=4 * heads * rows * reach * head_size,
            bytes_accessed=4 * rows * columns + 2 * keyvals.size,
            transcendentals=heads * rows * reach,
        ),
        name="attention_forward",
    )(jnp.concatenate([first_key[None], live]).astype(jnp.int32), queries, keyvals)


def attention_backward(queries, keyvals, d_attended, first_key, head_size):
    rows, columns = queries.shape
    heads = columns // head_size
    reach = W + ROWS
    span = keyvals.shape[0]
    lead = span - rows - W

    def body(info_ref, q_ref, kv_ref, do_ref, dq_ref, dkv_ref, sums):
        head, block = pl.program_id(0), pl.program_id(1)

        @pl.when((head == 0) & (block == 0))
        def _():
            sums[...] = jnp.zeros_like(sums)

        start = pl.multiple_of(lead + block * ROWS, ROWS)
        keys = kv_ref[pl.ds(start, reach), :head_size]
        vals = kv_ref[pl.ds(start, reach), head_size:]
        query = q_ref[...]
        d_out = do_ref[...]
        scores = nt(keys, query)
        column = lax.broadcasted_iota(jnp.int32, scores.shape, 0)
        row = lax.broadcasted_iota(jnp.int32, scores.shape, 1)
        ahead = column - row
        allowed = (ahead > 0) & (ahead <= W) & (column >= info_ref[0] - start)
        scores = jnp.where(allowed, scores, lowest)
        peak = jnp.max(scores, axis=0, keepdims=True)
        shares = jnp.exp(scores - peak)
        total = jnp.sum(shares, axis=0, keepdims=True)
        probs = shares * (1.0 / total)
        d_probs = nt(vals, d_out)
        inner = jnp.sum(probs * d_probs, axis=0, keepdims=True)
        d_scores = low(probs * (d_probs - inner))
        dq_ref[...] = tn(d_scores, keys)
        sums[pl.ds(start, reach), :head_size] += nn(d_scores, query)
        sums[pl.ds(start, reach), head_size:] += nn(low(probs), d_out)

        @pl.when((head == heads - 1) & (block == rows // ROWS - 1))
        def _():
            dkv_ref[...] = low(sums[...])

    return pl.pallas_call(
        body,
        out_shape=(
            jax.ShapeDtypeStruct((rows, columns), jnp.float32),
            jax.ShapeDtypeStruct(keyvals.shape, jnp.bfloat16),
        ),
        grid_spec=pltpu.PrefetchScalarGridSpec(
            num_scalar_prefetch=1,
            grid=(heads, rows // ROWS),
            in_specs=[
                pl.BlockSpec((ROWS, head_size), lambda h, i, info: (i, h)),
                pl.BlockSpec(keyvals.shape, lambda h, i, info: (0, 0)),
                pl.BlockSpec((ROWS, head_size), lambda h, i, info: (i, h)),
            ],
            out_specs=(
                pl.BlockSpec((ROWS, head_size), lambda h, i, info: (i, h)),
                pl.BlockSpec(keyvals.shape, lambda h, i, info: (0, 0)),
            ),
            scratch_shapes=[pltpu.VMEM(keyvals.shape, jnp.float32)],
        ),
        compiler_params=pltpu.CompilerParams(vmem_limit_bytes=VMEM_BYTES),
        cost_estimate=pl.CostEstimate(
            flops=10 * heads * rows * reach * head_size,
            bytes_accessed=8 * rows * columns + 4 * keyvals.size,
            transcendentals=heads * rows * reach,
        ),
        name="attention_backward",
    )(first_key[None].astype(jnp.int32), queries, keyvals, d_attended)


def gelu_tanh(values):
    return jax.nn.gelu(values, approximate=True)


def local(
    hidden,
    lengths,
    teacher,
    attn_gain,
    query_weight,
    kv_weight,
    out_weight,
    mlp_gain,
    gate_weight,
    up_weight,
    down_weight,
):
    tp_count = lax.axis_size("tp")
    ctx_count = lax.axis_size("ctx")
    fsdp_count = lax.axis_size("fsdp")
    tp_rank = lax.axis_index("tp")
    ctx_rank = lax.axis_index("ctx")
    fsdp_rank = lax.axis_index("fsdp")
    y_rank, core_rank = tp_rank // 2, tp_rank % 2
    hi_rank, lo_rank = ctx_rank // 2, ctx_rank % 2
    seq_count, rows, width = hidden.shape
    assert seq_count == 1 and tp_count == 4 and ctx_count == 4
    part_rows = rows // tp_count
    head_size = kv_weight.shape[1] // 2
    head_count = query_weight.shape[1] // head_size
    slot_count = -(-head_count // tp_count)
    slot_width = slot_count * head_size
    fuller = head_count - (slot_count - 1) * tp_count
    kv_width = 2 * head_size // tp_count

    def first_head_of(rank):
        return rank * (slot_count - 1) + jnp.minimum(rank, fuller)

    def slot_base_of(rank):
        return jnp.minimum(first_head_of(rank), head_count - slot_count)

    slot_heads = slot_base_of(tp_rank) + jnp.arange(slot_count)
    first_head = first_head_of(tp_rank)
    held_heads = slot_count - 1 + (tp_rank < fuller).astype(jnp.int32)
    live = ((slot_heads >= first_head) & (slot_heads < first_head + held_heads)).astype(jnp.int32)

    def over_tp(columns_of):
        blocks = [columns_of(tp_rank)]
        for bit in range(1, tp_count):
            blocks.append(flip(columns_of(tp_rank ^ bit), "tp", bit))
        return jnp.concatenate(swapped(blocks, tp_rank), axis=0)

    def over_ctx_and_fsdp(block):
        pieces, slots = [], []
        around = block
        for step in range(ctx_count):
            if step:
                around = ring(around, "ctx")
            across = around
            for turn_at in range(fsdp_count):
                if turn_at:
                    across = ring(across, "fsdp")
                pieces.append(across)
                slots.append(
                    (fsdp_rank - turn_at) % fsdp_count * ctx_count
                    + (ctx_rank - step) % ctx_count
                )
        return place(pieces, slots).reshape(width, block.shape[1])

    def head_columns(weight):
        return lambda rank: lax.dynamic_slice_in_dim(
            weight, slot_base_of(rank) * head_size, slot_width, 1
        )

    gains = jnp.pad(jnp.stack([attn_gain, mlp_gain], axis=1), ((0, 0), (0, 126)))
    kv_and_gains = over_ctx_and_fsdp(
        over_tp(
            lambda rank: jnp.concatenate(
                [lax.dynamic_slice_in_dim(kv_weight, rank * kv_width, kv_width, 1), gains], axis=1
            )
        )
    )
    kv_part = kv_and_gains[:, :kv_width]
    gain_attn = wide(kv_and_gains[:, kv_width])
    gain_mlp = wide(kv_and_gains[:, kv_width + 1])
    query_part = over_ctx_and_fsdp(over_tp(head_columns(query_weight)))
    out_part = over_ctx_and_fsdp(over_tp(head_columns(out_weight)))

    unit_count = gate_weight.shape[1]
    half = -(-unit_count // 256) * 128
    rest = unit_count - half

    def mlp_gather(block):
        near, far = block[:, :half], jnp.pad(block[:, half:], ((0, 0), (0, half - rest)))
        mine = jnp.where(lo_rank == 0, near, far)
        theirs = jnp.where(lo_rank == 0, far, near)
        got = flip(theirs, "ctx", 1)
        pair = jnp.stack(swapped([mine, got], lo_rank))
        pieces, slots = [], []
        for far_bit, around in ((0, pair), (1, flip(pair, "ctx", 2))):
            across = around
            for turn_at in range(fsdp_count):
                if turn_at:
                    across = ring(across, "fsdp")
                pieces.append(across)
                slots.append((fsdp_rank - turn_at) % fsdp_count * 2 + (hi_rank ^ far_bit))
        return place(pieces, slots).reshape(width, half)

    gate_full = mlp_gather(gate_weight)
    up_full = mlp_gather(up_weight)
    down_full = mlp_gather(down_weight.T)

    inputs_low = hidden[0]
    inputs = wide(inputs_low)
    inputs_part_low = lax.dynamic_slice_in_dim(inputs_low, tp_rank * part_rows, part_rows, 0)
    inputs_part = wide(inputs_part_low)
    scale_one = lax.rsqrt(jnp.mean(inputs * inputs, axis=-1, keepdims=True) + epsilon)
    normed = low(inputs * scale_one * gain_attn)
    positions = ctx_rank * rows + jnp.arange(rows)
    quarter = head_size // 4
    frequency = 10000.0 ** (-(jnp.arange(quarter).astype(jnp.float32) * 4.0 / head_size))
    angle = wide(positions)[:, None] * frequency[None, :]
    cosine, sine = jnp.cos(angle), jnp.sin(angle)

    def turn(values, cosine, sine):
        first, second = values[..., :quarter], values[..., quarter : 2 * quarter]
        return jnp.concatenate(
            [
                first * cosine - second * sine,
                second * cosine + first * sine,
                values[..., 2 * quarter :],
            ],
            axis=-1,
        )

    turning = tp_rank == 0
    kv_cosine, kv_sine = jnp.where(turning, cosine, 1.0), jnp.where(turning, sine, 0.0)
    kv_raw = nn(normed, kv_part)
    kv_own = low(turn(kv_raw, kv_cosine, kv_sine))
    reach_back = min((W - 2) // rows + 1, ctx_count - 1)
    chunks = [shifted(kv_own, "ctx", by) for by in range(reach_back, 0, -1)] + [kv_own]
    kv_column = jnp.concatenate(chunks, axis=0)
    kv_pair = jnp.stack([kv_column, flip(kv_column, "tp", 2)])
    kv_other = flip(kv_pair, "tp", 1)
    keyvals = jnp.concatenate(
        swapped([kv_pair[0], kv_other[0], kv_pair[1], kv_other[1]], tp_rank), axis=1
    )
    first_key = (reach_back - jnp.minimum(ctx_rank, reach_back)) * rows

    query_scale = head_size ** (-0.5)
    query_raw = nn(normed, query_part).reshape(rows, slot_count, head_size)
    queries = low(turn(query_raw, cosine[:, None, :], sine[:, None, :]) * query_scale)
    queries = queries.reshape(rows, slot_width)
    attended = attention_forward(queries, keyvals, live, first_key, head_size)

    def tp_sum(partial):
        blocks = partial.reshape(2, 2, part_rows, -1)
        got = flip(take(blocks, 1 - core_rank, 1), "tp", 1)
        summed = wide(take(blocks, core_rank, 1)) + wide(got)
        got = flip(low(take(summed, 1 - y_rank)), "tp", 2)
        return take(summed, y_rank) + wide(got)

    def tp_gather(part):
        pair = jnp.stack([part, flip(part, "tp", 2)])
        other = flip(pair, "tp", 1)
        blocks = swapped([pair[0], other[0], pair[1], other[1]], tp_rank)
        return jnp.concatenate(blocks, axis=0)

    def group_gather(part):
        middle = part_rows // 2
        over_y = flip(part, "tp", 2)
        over_z = flip(part, "ctx", 1)
        corner_top = flip(over_y[:middle], "ctx", 1)
        corner_end = flip(over_z[middle:], "tp", 2)
        near = jnp.concatenate([part, over_y, over_z, corner_top, corner_end], axis=0)
        return jnp.concatenate([near, flip(near, "tp", 1)], axis=0)

    def group_sum(partial):
        blocks = partial.reshape(2, 4, part_rows, -1)
        middle = part_rows // 2
        got = flip(blocks[1], "tp", 1)
        summed = wide(blocks[0]) + wide(got)
        own, over_y, over_z, corner = summed[0], summed[1], summed[2], summed[3]
        top = flip(low(corner[:middle]), "ctx", 1)
        end = flip(low(corner[middle:]), "tp", 2)
        over_y = jnp.concatenate([over_y[:middle] + wide(top), over_y[middle:]], axis=0)
        over_z = jnp.concatenate([over_z[:middle], over_z[middle:] + wide(end)], axis=0)
        return own + wide(flip(low(over_y), "tp", 2)) + wide(flip(low(over_z), "ctx", 1))

    attn_part = tp_sum(low(nt(attended, out_part)))
    residual = inputs_part + attn_part
    scale_two = lax.rsqrt(jnp.mean(residual * residual, axis=-1, keepdims=True) + epsilon)
    normed_two = group_gather(low(residual * scale_two * gain_mlp))
    gate_proj = nn(normed_two, gate_full)
    up_proj = nn(normed_two, up_full)
    activated, gelu_back = jax.vjp(gelu_tanh, gate_proj)
    hidden_act = low(activated * up_proj)
    ffn_part = group_sum(low(nt(hidden_act, down_full)))

    my_length = lengths[fsdp_rank]
    part_positions = ctx_rank * rows + tp_rank * part_rows + jnp.arange(part_rows)
    valid = wide(part_positions < my_length)[:, None]
    output = (residual + ffn_part) * valid
    mismatch = output - wide(teacher[0])
    count = wide(jnp.sum(lengths))
    loss_part = jnp.sum(valid * mismatch * mismatch)
    d_output = valid * mismatch * (lengths.shape[0] * ctx_count * rows / count)

    d_ffn = group_gather(low(d_output))
    d_hidden = nn(d_ffn, down_full)
    d_gate = low(gelu_back(d_hidden * up_proj)[0])
    d_up = low(d_hidden * activated)
    d_normed_two = group_sum(low(nt(d_gate, gate_full) + nt(d_up, up_full)))

    def mlp_scatter(grad):
        blocks = grad.reshape(fsdp_count, 2, 2, -1, half)
        mine = ring_sum(lambda owner: take(blocks, owner), "fsdp")
        got = flip(low(take(mine, 1 - hi_rank)), "ctx", 2)
        mine = take(mine, hi_rank) + wide(got)
        got = flip(low(take(mine, 1 - lo_rank)), "ctx", 1)
        near, far = swapped([take(mine, lo_rank), wide(got)], lo_rank)
        return jnp.concatenate([near, far[:, :rest]], axis=1)

    down_grad = mlp_scatter(tn(d_ffn, hidden_act)).T
    gate_grad = mlp_scatter(tn(normed_two, d_gate))
    up_grad = mlp_scatter(tn(normed_two, d_up))

    def vector_sum(vector):
        for axis, bit in (("tp", 1), ("tp", 2), ("ctx", 1), ("ctx", 2)):
            vector = vector + flip(vector, axis, bit)
        moving = vector
        for _ in range(1, fsdp_count):
            moving = ring(moving, "fsdp")
            vector = vector + moving
        return vector

    own_rows = attn_gain.shape[0]
    own_start = ((fsdp_rank * ctx_count + ctx_rank) * tp_count + tp_rank) * own_rows

    scaled = gain_mlp * d_normed_two
    inner_two = jnp.mean(scaled * residual, axis=-1, keepdims=True)
    d_residual = d_output + scale_two * scaled - residual * scale_two**3 * inner_two
    gain_mlp_sums = jnp.sum(d_normed_two * residual * scale_two, axis=0)
    early = vector_sum(jnp.concatenate([gain_mlp_sums, jnp.full((128,), loss_part)]))
    gain_mlp_grad = lax.dynamic_slice_in_dim(early, own_start, own_rows, 0)
    loss = early[width] / (count * width)

    d_attn = tp_gather(low(d_residual))

    def head_scatter(grad):
        blocks = grad.reshape(fsdp_count, ctx_count, tp_count, own_rows, -1)
        mine = ring_sum(lambda owner: take(blocks, owner), "fsdp")
        mine = ring_sum(lambda owner: take(mine, owner), "ctx")
        parts = [take(mine, tp_rank)]
        for bit in range(1, tp_count):
            parts.append(wide(flip(low(take(mine, tp_rank ^ bit)), "tp", bit)))
        return swapped(parts, tp_rank)

    def whole_heads(parts):
        columns = []
        for rank, part in enumerate(parts):
            first = rank * (slot_count - 1) + min(rank, fuller)
            base = min(first, head_count - slot_count)
            held = slot_count - 1 + (1 if rank < fuller else 0)
            start = (first - base) * head_size
            columns.append(part[:, start : start + held * head_size])
        return jnp.concatenate(columns, axis=1)

    out_grad = whole_heads(head_scatter(tn(d_attn, attended)))
    live_columns = jnp.repeat(live, head_size).astype(jnp.float32)
    d_attended = low(nn(d_attn, out_part) * live_columns)
    d_queries, d_keyvals = attention_backward(queries, keyvals, d_attended, first_key, head_size)
    d_query_raw = turn(
        d_queries.reshape(rows, slot_count, head_size) * query_scale,
        cosine[:, None, :],
        -sine[:, None, :],
    )
    d_query_low = low(d_query_raw.reshape(rows, slot_width))
    query_grad = whole_heads(head_scatter(tn(normed, d_query_low)))

    kv_blocks = jnp.stack(jnp.split(d_keyvals, tp_count, axis=1)).reshape(
        2, 2, -1, kv_width
    )
    got = flip(take(kv_blocks, 1 - core_rank, 1), "tp", 1)
    kv_sum = wide(take(kv_blocks, core_rank, 1)) + wide(got)
    got = flip(low(take(kv_sum, 1 - y_rank)), "tp", 2)
    kv_sum = (take(kv_sum, y_rank) + wide(got)).reshape(reach_back + 1, rows, kv_width)
    d_kv = kv_sum[reach_back]
    for by in range(1, reach_back + 1):
        d_kv = d_kv + wide(shifted(low(kv_sum[reach_back - by]), "ctx", -by))
    d_kv_low = low(turn(d_kv, kv_cosine, -kv_sine))
    kv_parts = head_scatter(tn(normed, d_kv_low))
    kv_grad = jnp.concatenate(kv_parts, axis=1)

    d_normed_partial = nt(d_query_low, query_part) + nt(d_kv_low, kv_part)
    gain_attn_sums = jnp.sum(d_normed_partial * inputs * scale_one, axis=0)
    gain_attn_grad = lax.dynamic_slice_in_dim(vector_sum(gain_attn_sums), own_start, own_rows, 0)
    d_normed = tp_sum(low(d_normed_partial))
    scale_part = lax.dynamic_slice_in_dim(scale_one, tp_rank * part_rows, part_rows, 0)
    scaled = gain_attn * d_normed
    inner_one = jnp.mean(scaled * inputs_part, axis=-1, keepdims=True)
    input_grad = d_residual + scale_part * scaled - inputs_part * scale_part**3 * inner_one
    return (
        low(output)[None],
        loss,
        input_grad[None],
        gain_attn_grad,
        query_grad,
        kv_grad,
        out_grad,
        gain_mlp_grad,
        gate_grad,
        up_grad,
        down_grad,
    )


def solution(mesh):
    in_specs = (
        P("fsdp", "ctx", None),
        P(),
        P("fsdp", ("ctx", "tp"), None),
        P(("fsdp", "ctx", "tp")),
        P(("fsdp", "ctx", "tp"), None),
        P(("fsdp", "ctx", "tp"), None),
        P(("fsdp", "ctx", "tp"), None),
        P(("fsdp", "ctx", "tp")),
        P(("fsdp", "ctx"), "tp"),
        P(("fsdp", "ctx"), "tp"),
        P("tp", ("fsdp", "ctx")),
    )
    out_specs = (
        P("fsdp", ("ctx", "tp"), None),
        P(),
        P("fsdp", ("ctx", "tp"), None),
        P(("fsdp", "ctx", "tp")),
        P(("fsdp", "ctx", "tp"), None),
        P(("fsdp", "ctx", "tp"), None),
        P(("fsdp", "ctx", "tp"), None),
        P(("fsdp", "ctx", "tp")),
        P(("fsdp", "ctx"), "tp"),
        P(("fsdp", "ctx"), "tp"),
        P("tp", ("fsdp", "ctx")),
    )
    return jax.shard_map(local, mesh=mesh, in_specs=in_specs, out_specs=out_specs, check_vma=False)
```

```python
import jax
import jax.numpy as jnp
from jax import lax
from jax.experimental import pallas as pl
from jax.experimental.pallas import tpu as pltpu
from jax.sharding import PartitionSpec as P

W = 2048

epsilon = 1e-06
lowest = -1e30
ROWS = 256
VMEM_BYTES = 40 * 1024 * 1024


def flip(array, axis, bit):
    link = Chain.link(axis, bit)
    array = Chain.before(array, link)
    got = lax.ppermute(array, axis, [(i, i ^ bit) for i in range(lax.axis_size(axis))])
    return Chain.done(got, link)


def ring(array, axis, by=1):
    count = lax.axis_size(axis)
    link = Chain.link(axis, 2)
    array = Chain.before(array, link)
    got = lax.ppermute(array, axis, [(i, (i + by) % count) for i in range(count)])
    return Chain.done(got, link)


def shifted(array, axis, by):
    count = lax.axis_size(axis)
    pairs = [(i, i + by) for i in range(count) if 0 <= i + by < count]
    return lax.ppermute(array, axis, pairs)


class Chain:
    on = ()
    sent = {}

    @staticmethod
    def link(axis, bit=1):
        if axis == "fsdp":
            return "x"
        if axis == "tp":
            return "y" if bit > 1 else None
        return "z" if bit != 1 else "zl"

    @staticmethod
    def before(array, link):
        if link in Chain.on and len(Chain.sent.setdefault(link, [])) >= 1:
            array = after(array, Chain.sent[link][-1])
        return array

    @staticmethod
    def done(got, link):
        Chain.sent.setdefault(link, []).append(got)
        return got


class Steps:
    on = True

    def next(self):
        if not Steps.on:
            return
        self.__dict__.update(lax.optimization_barrier(dict(self.__dict__)))

    def drop(self, *names):
        return [self.__dict__.pop(name) for name in names]


def sync(*trees):
    return lax.optimization_barrier(trees)


def after(array, *others):
    return lax.optimization_barrier((array, others))[0]


def low(values):
    return values.astype(jnp.bfloat16)


def wide(values):
    return values.astype(jnp.float32)


def take(array, index, axis=0):
    return lax.dynamic_index_in_dim(array, index, axis, keepdims=False)


def swapped(blocks, rank):
    if len(blocks) == 2:
        odd = rank == 1
        return [jnp.where(odd, blocks[1], blocks[0]), jnp.where(odd, blocks[0], blocks[1])]
    first = swapped(blocks[:2], rank % 2) + swapped(blocks[2:], rank % 2)
    outer = rank // 2 == 1
    return [jnp.where(outer, first[i ^ 2], first[i]) for i in range(4)]


def place(pieces, slots):
    count = len(pieces)
    shape = pieces[0].shape

    def body(slots_ref, *refs):
        out_ref, held, came, left = refs[count:]
        into = [pltpu.make_async_copy(refs[k], held.at[k], came.at[k]) for k in range(count)]
        out_of = [
            pltpu.make_async_copy(held.at[k], out_ref.at[slots_ref[k]], left.at[k])
            for k in range(count)
        ]
        for copy in into:
            copy.start()
        for first, second in zip(into, out_of):
            first.wait()
            second.start()
        for copy in out_of:
            copy.wait()

    return pl.pallas_call(
        body,
        out_shape=jax.ShapeDtypeStruct((count,) + shape, pieces[0].dtype),
        grid_spec=pltpu.PrefetchScalarGridSpec(
            num_scalar_prefetch=1,
            grid=(1,),
            in_specs=[pl.BlockSpec(memory_space=pl.ANY)] * count,
            out_specs=pl.BlockSpec(memory_space=pl.ANY),
            scratch_shapes=[
                pltpu.VMEM((count,) + shape, pieces[0].dtype),
                pltpu.SemaphoreType.DMA((count,)),
                pltpu.SemaphoreType.DMA((count,)),
            ],
        ),
        compiler_params=pltpu.CompilerParams(vmem_limit_bytes=VMEM_BYTES),
        cost_estimate=pl.CostEstimate(
            flops=0, bytes_accessed=4 * count * pieces[0].size, transcendentals=0
        ),
        name="place",
    )(jnp.stack(slots).astype(jnp.int32), *pieces)


def nn(first, second):
    return lax.dot_general(
        first, second, (((1,), (0,)), ((), ())), preferred_element_type=jnp.float32
    )


def nt(first, second):
    return lax.dot_general(
        first, second, (((1,), (1,)), ((), ())), preferred_element_type=jnp.float32
    )


def tn(first, second):
    return lax.dot_general(
        first, second, (((0,), (0,)), ((), ())), preferred_element_type=jnp.float32
    )


def ring_sum(block_of, axis):
    count = lax.axis_size(axis)
    rank = lax.axis_index(axis)
    moving = None
    for step in range(1, count):
        term = block_of((rank - step) % count)
        moving = low(term if moving is None else wide(moving) + wide(term))
        moving = ring(moving, axis)
    own = wide(block_of(rank))
    return own if moving is None else own + wide(moving)


def attention_forward(queries, keyvals, live, first_key, head_size):
    rows, columns = queries.shape
    heads = columns // head_size
    reach = W + ROWS
    lead = keyvals.shape[0] - rows - W

    def body(info_ref, q_ref, kv_ref, o_ref):
        head, block = pl.program_id(0), pl.program_id(1)
        start = pl.multiple_of(lead + block * ROWS, ROWS)
        keys = kv_ref[pl.ds(start, reach), :head_size]
        vals = kv_ref[pl.ds(start, reach), head_size:]
        scores = nt(q_ref[...], keys)
        row = lax.broadcasted_iota(jnp.int32, scores.shape, 0)
        column = lax.broadcasted_iota(jnp.int32, scores.shape, 1)
        ahead = column - row
        allowed = (ahead > 0) & (ahead <= W) & (column >= info_ref[0] - start)
        scores = jnp.where(allowed, scores, lowest)
        peak = jnp.max(scores, axis=1, keepdims=True)
        shares = jnp.exp(scores - peak)
        total = jnp.sum(shares, axis=1, keepdims=True)
        probs = low(shares * (1.0 / total))
        mixed = nn(probs, vals)
        o_ref[...] = low(mixed * wide(info_ref[1 + head]))

    return pl.pallas_call(
        body,
        out_shape=jax.ShapeDtypeStruct((rows, columns), jnp.bfloat16),
        grid_spec=pltpu.PrefetchScalarGridSpec(
            num_scalar_prefetch=1,
            grid=(heads, rows // ROWS),
            in_specs=[
                pl.BlockSpec((ROWS, head_size), lambda h, i, info: (i, h)),
                pl.BlockSpec(keyvals.shape, lambda h, i, info: (0, 0)),
            ],
            out_specs=pl.BlockSpec((ROWS, head_size), lambda h, i, info: (i, h)),
        ),
        compiler_params=pltpu.CompilerParams(vmem_limit_bytes=VMEM_BYTES),
        cost_estimate=pl.CostEstimate(
            flops=4 * heads * rows * reach * head_size,
            bytes_accessed=4 * rows * columns + 2 * keyvals.size,
            transcendentals=heads * rows * reach,
        ),
        name="attention_forward",
    )(jnp.concatenate([first_key[None], live]).astype(jnp.int32), queries, keyvals)


def attention_backward(queries, keyvals, d_attended, first_key, head_size):
    rows, columns = queries.shape
    heads = columns // head_size
    reach = W + ROWS
    span = keyvals.shape[0]
    lead = span - rows - W

    def body(info_ref, q_ref, kv_ref, do_ref, dq_ref, dkv_ref, sums):
        head, block = pl.program_id(0), pl.program_id(1)

        @pl.when((head == 0) & (block == 0))
        def _():
            sums[...] = jnp.zeros_like(sums)

        start = pl.multiple_of(lead + block * ROWS, ROWS)
        keys = kv_ref[pl.ds(start, reach), :head_size]
        vals = kv_ref[pl.ds(start, reach), head_size:]
        query = q_ref[...]
        d_out = do_ref[...]
        scores = nt(keys, query)
        column = lax.broadcasted_iota(jnp.int32, scores.shape, 0)
        row = lax.broadcasted_iota(jnp.int32, scores.shape, 1)
        ahead = column - row
        allowed = (ahead > 0) & (ahead <= W) & (column >= info_ref[0] - start)
        scores = jnp.where(allowed, scores, lowest)
        peak = jnp.max(scores, axis=0, keepdims=True)
        shares = jnp.exp(scores - peak)
        total = jnp.sum(shares, axis=0, keepdims=True)
        probs = shares * (1.0 / total)
        d_probs = nt(vals, d_out)
        inner = jnp.sum(probs * d_probs, axis=0, keepdims=True)
        d_scores = low(probs * (d_probs - inner))
        dq_ref[...] = tn(d_scores, keys)
        sums[pl.ds(start, reach), :head_size] += nn(d_scores, query)
        sums[pl.ds(start, reach), head_size:] += nn(low(probs), d_out)

        @pl.when((head == heads - 1) & (block == rows // ROWS - 1))
        def _():
            dkv_ref[...] = low(sums[...])

    return pl.pallas_call(
        body,
        out_shape=(
            jax.ShapeDtypeStruct((rows, columns), jnp.float32),
            jax.ShapeDtypeStruct(keyvals.shape, jnp.bfloat16),
        ),
        grid_spec=pltpu.PrefetchScalarGridSpec(
            num_scalar_prefetch=1,
            grid=(heads, rows // ROWS),
            in_specs=[
                pl.BlockSpec((ROWS, head_size), lambda h, i, info: (i, h)),
                pl.BlockSpec(keyvals.shape, lambda h, i, info: (0, 0)),
                pl.BlockSpec((ROWS, head_size), lambda h, i, info: (i, h)),
            ],
            out_specs=(
                pl.BlockSpec((ROWS, head_size), lambda h, i, info: (i, h)),
                pl.BlockSpec(keyvals.shape, lambda h, i, info: (0, 0)),
            ),
            scratch_shapes=[pltpu.VMEM(keyvals.shape, jnp.float32)],
        ),
        compiler_params=pltpu.CompilerParams(vmem_limit_bytes=VMEM_BYTES),
        cost_estimate=pl.CostEstimate(
            flops=10 * heads * rows * reach * head_size,
            bytes_accessed=8 * rows * columns + 4 * keyvals.size,
            transcendentals=heads * rows * reach,
        ),
        name="attention_backward",
    )(first_key[None].astype(jnp.int32), queries, keyvals, d_attended)


def gelu_tanh(values):
    return jax.nn.gelu(values, approximate=True)


def local(
    hidden,
    lengths,
    teacher,
    attn_gain,
    query_weight,
    kv_weight,
    out_weight,
    mlp_gain,
    gate_weight,
    up_weight,
    down_weight,
):
    tp_count = lax.axis_size("tp")
    ctx_count = lax.axis_size("ctx")
    fsdp_count = lax.axis_size("fsdp")
    tp_rank = lax.axis_index("tp")
    ctx_rank = lax.axis_index("ctx")
    fsdp_rank = lax.axis_index("fsdp")
    y_rank, core_rank = tp_rank // 2, tp_rank % 2
    hi_rank, lo_rank = ctx_rank // 2, ctx_rank % 2
    seq_count, rows, width = hidden.shape
    assert seq_count == 1 and tp_count == 4 and ctx_count == 4
    part_rows = rows // tp_count
    head_size = kv_weight.shape[1] // 2
    head_count = query_weight.shape[1] // head_size
    slot_count = -(-head_count // tp_count)
    slot_width = slot_count * head_size
    fuller = head_count - (slot_count - 1) * tp_count
    kv_width = 2 * head_size // tp_count

    def first_head_of(rank):
        return rank * (slot_count - 1) + jnp.minimum(rank, fuller)

    def slot_base_of(rank):
        return jnp.minimum(first_head_of(rank), head_count - slot_count)

    slot_heads = slot_base_of(tp_rank) + jnp.arange(slot_count)
    first_head = first_head_of(tp_rank)
    held_heads = slot_count - 1 + (tp_rank < fuller).astype(jnp.int32)
    live = ((slot_heads >= first_head) & (slot_heads < first_head + held_heads)).astype(jnp.int32)

    def over_tp(columns_of):
        blocks = [columns_of(tp_rank)]
        for bit in range(1, tp_count):
            blocks.append(flip(columns_of(tp_rank ^ bit), "tp", bit))
        return jnp.concatenate(swapped(blocks, tp_rank), axis=0)

    def over_fsdp(block):
        blocks = [block]
        for _ in range(1, fsdp_count):
            blocks.append(ring(blocks[-1], "fsdp"))
        return blocks

    def placed(by_ctx):
        pieces, slots = [], []
        for step, blocks in enumerate(by_ctx):
            for turn_at, block in enumerate(blocks):
                pieces.append(block)
                slots.append(
                    (fsdp_rank - turn_at) % fsdp_count * ctx_count
                    + (ctx_rank - step) % ctx_count
                )
        return place(pieces, slots).reshape(width, pieces[0].shape[1])

    def head_columns(weight):
        return lambda rank: lax.dynamic_slice_in_dim(
            weight, slot_base_of(rank) * head_size, slot_width, 1
        )

    unit_count = gate_weight.shape[1]
    half = -(-unit_count // 256) * 128
    rest = unit_count - half

    def near_halves(block):
        near, far = block[:, :half], jnp.pad(block[:, half:], ((0, 0), (0, half - rest)))
        mine = jnp.where(lo_rank == 0, near, far)
        theirs = jnp.where(lo_rank == 0, far, near)
        return mine, theirs

    def near_pair(halves):
        mine, theirs = halves
        return jnp.stack(swapped([mine, flip(theirs, "ctx", 1)], lo_rank))

    def quarters(pair):
        return jnp.split(pair.reshape(-1, half), 4)

    def far(pieces):
        if len(pieces) == 1:
            return [flip(pieces[0], "ctx", 2)]
        return jnp.split(flip(jnp.concatenate(pieces, axis=0), "ctx", 2), len(pieces))

    def mlp_placed(own, other):
        pieces, slots = [], []
        for far_bit, blocks in enumerate((own, other)):
            for turn_at, block in enumerate(blocks):
                pieces.append(block.reshape(-1, half))
                slots.append((fsdp_rank - turn_at) % fsdp_count * 2 + (hi_rank ^ far_bit))
        return place(pieces, slots).reshape(width, half)

    inputs_low = hidden[0]
    inputs = wide(inputs_low)
    inputs_part_low = lax.dynamic_slice_in_dim(inputs_low, tp_rank * part_rows, part_rows, 0)
    inputs_part = wide(inputs_part_low)
    scale_one = lax.rsqrt(jnp.mean(inputs * inputs, axis=-1, keepdims=True) + epsilon)
    positions = ctx_rank * rows + jnp.arange(rows)
    quarter = head_size // 4
    frequency = 10000.0 ** (-(jnp.arange(quarter).astype(jnp.float32) * 4.0 / head_size))
    angle = wide(positions)[:, None] * frequency[None, :]
    cosine, sine = jnp.cos(angle), jnp.sin(angle)

    def turn(values, cosine, sine):
        first, second = values[..., :quarter], values[..., quarter : 2 * quarter]
        return jnp.concatenate(
            [
                first * cosine - second * sine,
                second * cosine + first * sine,
                values[..., 2 * quarter :],
            ],
            axis=-1,
        )

    turning = tp_rank == 0
    kv_cosine, kv_sine = jnp.where(turning, cosine, 1.0), jnp.where(turning, sine, 0.0)
    query_scale = head_size ** (-0.5)
    reach_back = min((W - 2) // rows + 1, ctx_count - 1)
    first_key = (reach_back - jnp.minimum(ctx_rank, reach_back)) * rows

    at = Steps()
    Steps.on = True
    Chain.on = ()
    Chain.sent = {}
    gains = jnp.pad(jnp.stack([attn_gain, mlp_gain], axis=1), ((0, 0), (0, 126)))

    def qkv_columns(rank):
        kv = lax.dynamic_slice_in_dim(kv_weight, rank * kv_width, kv_width, 1)
        return jnp.concatenate([head_columns(query_weight)(rank), kv, gains], axis=1)

    def to_tp(columns_of):
        return [columns_of(tp_rank ^ bit) for bit in range(tp_count)]

    def flip_tp(blocks):
        return blocks[:1] + [flip(blocks[bit], "tp", bit) for bit in range(1, tp_count)]

    def from_tp(blocks):
        return jnp.concatenate(swapped(blocks, tp_rank), axis=0)

    def paired(mine, got):
        return jnp.stack(swapped([mine, got], lo_rank))

    at.qkv = to_tp(qkv_columns)
    at.gate_mine, at.gate_sent = near_halves(gate_weight)
    at.out = to_tp(head_columns(out_weight))
    at.up_mine, at.up_sent = near_halves(up_weight)
    at.down_mine, at.down_sent = near_halves(down_weight.T)
    at.next()
    at.qkv = flip_tp(at.qkv)
    at.gate_got = flip(at.gate_sent, "ctx", 1)
    at.next()
    at.qkv_0 = from_tp(at.drop("qkv")[0])
    at.gate_pair = paired(*at.drop("gate_mine", "gate_got"))
    at.next()
    at.qkv_x = [over_fsdp(at.qkv_0)]
    at.qkv_1 = ring(at.qkv_0, "ctx")
    at.next()
    at.qkv_x.append(over_fsdp(at.qkv_1))
    at.qkv_2 = ring(at.qkv_1, "ctx")
    at.next()
    at.qkv_x.append(over_fsdp(at.qkv_2))
    at.qkv_3 = ring(at.qkv_2, "ctx")
    at.out = flip_tp(at.out)
    at.next()
    at.out_0 = from_tp(at.drop("out")[0])
    at.drop("qkv_0", "qkv_1", "qkv_2", "gate_sent")
    at.next()
    at.qkv_x.append(over_fsdp(at.qkv_3))
    at.out_1 = ring(at.out_0, "ctx")
    at.next()

    qkv_part = placed(at.drop("qkv_x")[0])
    query_part = qkv_part[:, :slot_width]
    kv_part = qkv_part[:, slot_width : slot_width + kv_width]
    gain_attn = wide(qkv_part[:, slot_width + kv_width])
    gain_mlp = wide(qkv_part[:, slot_width + kv_width + 1])
    at.normed = low(inputs * scale_one * gain_attn)
    at.kv_own = low(turn(nn(at.normed, kv_part), kv_cosine, kv_sine))
    query_raw = nn(at.normed, query_part).reshape(rows, slot_count, head_size)
    queries = low(turn(query_raw, cosine[:, None, :], sine[:, None, :]) * query_scale)
    at.queries = queries.reshape(rows, slot_width)
    at.gate_x = over_fsdp(at.gate_pair)
    at.out_2 = ring(at.out_1, "ctx")
    at.up_got = flip(at.up_sent, "ctx", 1)
    at.far_1 = far(quarters(at.gate_pair)[:1])
    at.next()
    normed = at.normed
    at.up_pair = paired(*at.drop("up_mine", "up_got"))
    at.out_near = jnp.stack([at.out_0, at.out_1, at.out_2])
    at.next()
    out_x = over_fsdp(at.out_near)
    at.chunks = [shifted(at.kv_own, "ctx", by) for by in range(reach_back, 0, -1)]
    at.out_3 = ring(at.out_2, "ctx")
    at.next()
    at.kv_column = jnp.concatenate(at.drop("chunks")[0] + [at.kv_own], axis=0)
    at.gate_far = jnp.concatenate(quarters(at.gate_pair)[1:3], axis=0)
    at.drop("out_0", "out_1", "out_2", "kv_own", "qkv_3")
    at.next()
    at.kv_over_y = flip(at.kv_column, "tp", 2)
    at.down_got = flip(at.down_sent, "ctx", 1)
    at.far_2 = flip(at.gate_far, "ctx", 2)
    at.out_x = out_x
    at.next()
    at.kv_pair = jnp.stack(at.drop("kv_column", "kv_over_y"))
    at.down_pair = paired(*at.drop("down_mine", "down_got"))
    at.next()
    at.kv_other = flip(at.kv_pair, "tp", 1)
    at.out_y = over_fsdp(at.out_3)
    at.next()
    kv_pair, kv_other = at.drop("kv_pair", "kv_other")
    at.keyvals = jnp.concatenate(
        swapped([kv_pair[0], kv_other[0], kv_pair[1], kv_other[1]], tp_rank), axis=1
    )
    at.mixed_far = jnp.concatenate(quarters(at.gate_pair)[3:] + quarters(at.up_pair)[:1], axis=0)
    at.drop("up_sent", "down_sent", "gate_far", "out_near")
    at.next()

    queries, keyvals = at.queries, at.keyvals
    at.attended = attention_forward(queries, keyvals, live, first_key, head_size)
    out_x, out_y = at.drop("out_x", "out_y")
    at.out_part = placed([[block[i] for block in out_x] for i in range(3)] + [out_y])
    blocks = low(nt(at.attended, at.out_part)).reshape(2, 2, part_rows, -1)
    at.kept, at.sent = take(blocks, core_rank, 1), take(blocks, 1 - core_rank, 1)
    at.up_x = over_fsdp(at.up_pair)
    at.far_3 = flip(at.mixed_far, "ctx", 2)
    at.next()

    out_part = at.out_part
    quarter_rows = at.far_1[0].shape[0]
    at.gate_other = jnp.concatenate(
        at.far_1 + [at.far_2, at.far_3[:quarter_rows]], axis=0
    ).reshape(at.gate_pair.shape)
    at.up_far = jnp.concatenate(quarters(at.up_pair)[1:3], axis=0)
    at.next()
    at.got = flip(at.sent, "tp", 1)
    at.next()
    summed = wide(at.kept) + wide(at.got)
    at.kept, at.sent = take(summed, y_rank), low(take(summed, 1 - y_rank))
    at.next()
    at.got = flip(at.sent, "tp", 2)
    at.gate_z = over_fsdp(at.gate_other)
    at.far_4 = flip(at.up_far, "ctx", 2)
    at.next()

    middle = part_rows // 2

    def gather_sides():
        at.over_y, at.over_z = flip(at.part, "tp", 2), flip(at.part, "ctx", 1)
        at.core_own = flip(at.part, "tp", 1)

    def between_sides_and_corners():
        at.to_z, at.to_y = at.over_y[:middle], at.over_z[middle:]
        at.sides = jnp.concatenate([at.over_y, at.over_z], axis=0)

    def gather_corners():
        at.corner_top = flip(at.to_z, "ctx", 1)
        at.corner_end = flip(at.to_y, "tp", 2)
        at.core_sides = flip(at.sides, "tp", 1)

    def between_corners_and_core():
        at.corner = jnp.concatenate(at.drop("corner_top", "corner_end"), axis=0)
        at.drop("to_z", "to_y", "over_y", "over_z")

    def gathered():
        return jnp.concatenate(
            at.drop("part", "sides", "corner", "core_own", "core_sides", "core_corner"), axis=0
        )

    def before_sum(partial):
        mine, theirs = partial.reshape(2, 4, part_rows, -1)
        at.mine, at.mine_corner = mine[:3], mine[3]
        at.theirs, at.theirs_corner = theirs[:3], theirs[3]

    def between_core_and_corners():
        corner = wide(at.drop("mine_corner")[0]) + wide(at.drop("got_corner")[0])
        at.to_z, at.to_y = low(corner[:middle]), low(corner[middle:])

    def sum_corners():
        at.corner_top = flip(at.to_z, "ctx", 1)
        at.corner_end = flip(at.to_y, "tp", 2)

    def between_corners_and_sides():
        mine, got, top, end = at.drop("mine", "got", "corner_top", "corner_end")
        own, over_y, over_z = wide(mine) + wide(got)
        at.over_y = low(jnp.concatenate([over_y[:middle] + wide(top), over_y[middle:]], axis=0))
        at.over_z = low(jnp.concatenate([over_z[:middle], over_z[middle:] + wide(end)], axis=0))
        at.part = own
        at.drop("theirs", "theirs_corner", "to_z", "to_y")

    def sum_sides():
        at.got_y, at.got_z = flip(at.over_y, "tp", 2), flip(at.over_z, "ctx", 1)

    def summed():
        own, got_y, got_z = at.drop("part", "got_y", "got_z")
        at.drop("over_y", "over_z")
        return own + wide(got_y) + wide(got_z)

    residual = inputs_part + (at.kept + wide(at.got))
    at.drop("kept", "got", "sent")
    scale_two = lax.rsqrt(jnp.mean(residual * residual, axis=-1, keepdims=True) + epsilon)
    at.residual = residual
    at.part = low(residual * scale_two * gain_mlp)
    at.mixed_far = jnp.concatenate(quarters(at.up_pair)[3:] + quarters(at.down_pair)[:1], axis=0)
    at.next()
    residual = at.residual
    gather_sides()
    at.down_x = over_fsdp(at.down_pair)
    at.far_5 = flip(at.mixed_far, "ctx", 2)
    at.next()
    between_sides_and_corners()
    at.up_a = jnp.concatenate([at.far_3[quarter_rows:], at.far_4[:quarter_rows]], axis=0)
    at.up_b = jnp.concatenate([at.far_4[quarter_rows:], at.far_5[:quarter_rows]], axis=0)
    at.down_quarters = quarters(at.down_pair)[1:]
    at.next()
    gather_corners()
    at.up_a = over_fsdp(at.up_a)
    at.far_6 = flip(at.down_quarters[0], "ctx", 2)
    at.next()
    between_corners_and_core()
    at.down_a = jnp.concatenate([at.far_5[quarter_rows:], at.far_6], axis=0)
    at.next()
    at.core_corner = flip(at.corner, "tp", 1)
    at.next()
    at.normed_two = gathered()
    gate_full = mlp_placed(*at.drop("gate_x", "gate_z"))
    at.gate_proj = nn(at.normed_two, gate_full)
    at.up_b = over_fsdp(at.up_b)
    at.far_7 = flip(at.down_quarters[1], "ctx", 2)
    at.next()
    up_a, up_b = at.drop("up_a", "up_b")
    up_z = [jnp.stack(pair) for pair in zip(up_a, up_b)]
    up_full = mlp_placed(at.drop("up_x")[0], up_z)
    at.up_proj = nn(at.normed_two, up_full)
    at.down_a = over_fsdp(at.down_a)
    at.far_8 = flip(at.down_quarters[2], "ctx", 2)
    at.next()
    at.down_b = jnp.concatenate([at.far_7, at.far_8], axis=0)
    at.next()
    gate_proj, up_proj = at.gate_proj, at.up_proj
    activated, gelu_back = jax.vjp(gelu_tanh, gate_proj)
    at.hidden_act = low(activated * up_proj)
    at.down_b = over_fsdp(at.down_b)
    at.next()
    at.drop("far_1", "far_2", "far_3", "far_4", "far_5", "far_6", "far_7", "gate_pair", "up_pair")
    at.drop("far_8", "gate_other", "up_far", "down_quarters", "mixed_far")
    at.drop("gate_proj", "up_proj", "down_pair")
    down_x, down_a, down_b = at.drop("down_x", "down_a", "down_b")
    down_z = [jnp.stack(pair) for pair in zip(down_a, down_b)]
    down_full = mlp_placed(down_x, down_z)
    before_sum(low(nt(at.hidden_act, down_full)))
    at.next()
    at.got = flip(at.theirs, "tp", 1)
    at.got_corner = flip(at.theirs_corner, "tp", 1)
    at.next()
    between_core_and_corners()
    at.next()
    sum_corners()
    at.next()
    between_corners_and_sides()
    at.next()
    sum_sides()
    at.next()
    ffn_part = summed()

    my_length = lengths[fsdp_rank]
    part_positions = ctx_rank * rows + tp_rank * part_rows + jnp.arange(part_rows)
    valid = wide(part_positions < my_length)[:, None]
    output = (residual + ffn_part) * valid
    mismatch = output - wide(teacher[0])
    count = wide(jnp.sum(lengths))
    loss_part = jnp.sum(valid * mismatch * mismatch)
    at.d_output = valid * mismatch * (lengths.shape[0] * ctx_count * rows / count)
    at.part = low(at.d_output)
    at.next()
    gather_sides()
    at.next()
    between_sides_and_corners()
    at.next()
    gather_corners()
    at.next()
    between_corners_and_core()
    at.next()
    at.core_corner = flip(at.corner, "tp", 1)
    at.next()

    def terms(blocks_of, axis):
        count, rank = lax.axis_size(axis), lax.axis_index(axis)
        return [blocks_of((rank - step) % count) for step in range(1, count + 1)]

    def around(sent, axis):
        moving = ring(sent[0], axis)
        for term in sent[1:-1]:
            moving = ring(low(wide(moving) + wide(term)), axis)
        return moving

    def with_own(sent, arrived):
        return wide(sent[-1]) + wide(arrived)

    def far_and_own(grad):
        blocks = grad.reshape(fsdp_count, 2, 2, -1, half)
        return [
            terms(lambda owner: take(take(blocks, owner), high), "fsdp")
            for high in (1 - hi_rank, hi_rank)
        ]

    def near_split(mine):
        return wide(take(mine, lo_rank)), low(take(mine, 1 - lo_rank))

    def near_joined(kept, got):
        near, rest_of = swapped([kept, wide(got)], lo_rank)
        return jnp.concatenate([near, rest_of[:, :rest]], axis=1)

    at.d_ffn = gathered()
    at.down_far, at.down_own = far_and_own(low(tn(at.d_ffn, at.hidden_act)))
    at.next()
    Steps.on = False
    Chain.on = ('x',)
    Chain.sent = {}
    at.down_far_got = around(at.down_far, "fsdp")
    d_hidden = nn(at.d_ffn, down_full)
    at.d_gate = low(gelu_back(d_hidden * up_proj)[0])
    at.d_up = low(d_hidden * activated)
    at.next()
    at.drop("d_ffn", "hidden_act")
    at.down_far = low(with_own(*at.drop("down_far", "down_far_got")))
    at.next()
    at.down_own_got = around(at.down_own, "fsdp")
    at.down_got_0 = flip(at.down_far[0], "ctx", 2)
    before_sum(low(nt(at.d_gate, gate_full) + nt(at.d_up, up_full)))
    at.next()
    at.got = flip(at.theirs, "tp", 1)
    at.got_corner = flip(at.theirs_corner, "tp", 1)
    at.next()
    between_core_and_corners()
    at.next()
    sum_corners()
    at.down_got_1 = flip(at.down_far[1], "ctx", 2)
    at.gate_far, at.gate_own = far_and_own(low(tn(at.normed_two, at.d_gate)))
    at.next()
    at.drop("d_gate")
    between_corners_and_sides()
    at.down_own = low(with_own(*at.drop("down_own", "down_own_got")))
    at.next()
    sum_sides()
    at.gate_far_got = around(at.gate_far, "fsdp")
    at.up_far, at.up_own = far_and_own(low(tn(at.normed_two, at.d_up)))
    at.next()
    at.drop("normed_two", "d_up")
    at.gate_far = low(with_own(*at.drop("gate_far", "gate_far_got")))
    d_normed_two = summed()
    scaled = gain_mlp * d_normed_two
    inner_two = jnp.mean(scaled * residual, axis=-1, keepdims=True)
    at.d_residual = at.d_output + scale_two * scaled - residual * scale_two**3 * inner_two
    gain_mlp_sums = jnp.sum(d_normed_two * residual * scale_two, axis=0)
    at.vector = jnp.concatenate([gain_mlp_sums, jnp.full((128,), loss_part)])
    at.part = low(at.d_residual)
    at.next()
    at.over_y = flip(at.part, "tp", 2)
    at.gate_own_got = around(at.gate_own, "fsdp")
    at.gate_got_0 = flip(at.gate_far[0], "ctx", 2)
    at.next()
    at.pair = jnp.stack(at.drop("part", "over_y"))
    at.next()
    at.other = flip(at.pair, "tp", 1)
    at.got_vector = flip(at.vector, "tp", 1)
    at.next()
    pair, other = at.drop("pair", "other")
    d_attn = swapped([pair[0], other[0], pair[1], other[1]], tp_rank)
    at.d_attn = jnp.concatenate(d_attn, axis=0)
    down_got = jnp.stack(at.drop("down_got_0", "down_got_1"))
    at.down_kept, at.down_sent = near_split(wide(at.down_own) + wide(down_got))
    at.vector = at.vector + at.drop("got_vector")[0]
    at.next()
    at.drop("down_own", "down_far")
    at.got_vector = flip(at.vector, "tp", 2)
    at.down_got = flip(at.down_sent, "ctx", 1)
    live_columns = jnp.repeat(live, head_size).astype(jnp.float32)
    at.d_attended = low(nn(at.d_attn, out_part) * live_columns)
    out_grad = low(tn(at.d_attn, at.attended))

    own_rows = attn_gain.shape[0]
    own_start = ((fsdp_rank * ctx_count + ctx_rank) * tp_count + tp_rank) * own_rows

    def by_rows(grad):
        return grad.reshape(fsdp_count, ctx_count, tp_count * own_rows, -1)

    at.out_terms = terms(lambda owner: take(by_rows(out_grad), owner), "fsdp")
    at.gate_own = low(with_own(*at.drop("gate_own", "gate_own_got")))
    at.next()
    at.drop("attended", "d_attn", "down_sent")
    at.vector = at.vector + at.drop("got_vector")[0]
    at.next()
    at.got_vector = flip(at.vector, "ctx", 1)
    at.gate_got_1 = flip(at.gate_far[1], "ctx", 2)
    at.up_far_got = around(at.up_far, "fsdp")
    at.d_queries, at.d_keyvals = attention_backward(
        queries, keyvals, at.d_attended, first_key, head_size
    )
    kv_blocks = jnp.stack(jnp.split(at.d_keyvals, tp_count, axis=1)).reshape(2, 2, -1, kv_width)
    at.kv_kept, at.kv_sent = take(kv_blocks, core_rank, 1), take(kv_blocks, 1 - core_rank, 1)
    at.next()
    at.drop("d_attended", "d_keyvals")
    at.kv_got = flip(at.kv_sent, "tp", 1)
    at.next()
    at.vector = at.vector + at.drop("got_vector")[0]
    kv_sum = wide(at.kv_kept) + wide(at.kv_got)
    at.kv_kept, at.kv_sent = take(kv_sum, y_rank), low(take(kv_sum, 1 - y_rank))
    at.up_far = low(with_own(*at.drop("up_far", "up_far_got")))
    at.next()
    at.kv_got = flip(at.kv_sent, "tp", 2)
    at.got_vector = flip(at.vector, "ctx", 2)
    at.up_got_0 = flip(at.up_far[0], "ctx", 2)
    at.out_got = around(at.out_terms, "fsdp")
    d_query_raw = turn(
        at.d_queries.reshape(rows, slot_count, head_size) * query_scale,
        cosine[:, None, :],
        -sine[:, None, :],
    )
    at.d_query_low = low(d_query_raw.reshape(rows, slot_width))
    query_grad = by_rows(low(tn(normed, at.d_query_low)))
    turned = [take(query_grad, (ctx_rank - by) % ctx_count, 1) for by in range(1, ctx_count + 1)]
    first_half, second_half = jnp.stack(turned[:2], axis=1), jnp.stack(turned[2:], axis=1)
    at.query_1 = terms(lambda owner: take(first_half, owner), "fsdp")
    at.query_2 = terms(lambda owner: take(second_half, owner), "fsdp")
    at.next()
    at.drop("d_queries", "kv_sent", "gate_far")
    at.vector = at.vector + at.drop("got_vector")[0]
    kv_sum = (at.drop("kv_kept")[0] + wide(at.drop("kv_got")[0])).reshape(reach_back + 1, rows, -1)
    at.kv_low = [low(kv_sum[reach_back - by]) for by in range(1, reach_back + 1)]
    at.d_kv = kv_sum[reach_back]
    out_mine = low(with_own(*at.drop("out_terms", "out_got")))
    at.out_terms = terms(lambda owner: take(out_mine, owner), "ctx")
    at.next()
    at.kv_got = [shifted(at.kv_low[by - 1], "ctx", -by) for by in range(1, reach_back + 1)]
    at.up_own_got = around(at.up_own, "fsdp")
    at.out_z = ring(at.out_terms[0], "ctx")
    gate_got = jnp.stack(at.drop("gate_got_0", "gate_got_1"))
    at.gate_kept, at.gate_sent = near_split(wide(at.gate_own) + wide(gate_got))
    at.next()
    at.drop("gate_own")
    d_kv = at.d_kv
    for got in at.drop("kv_got")[0]:
        d_kv = d_kv + wide(got)
    d_kv_low = low(turn(d_kv, kv_cosine, -kv_sine))
    partial = low(nt(at.d_query_low, query_part) + nt(d_kv_low, kv_part))
    gain_attn_sums = jnp.sum(wide(partial) * inputs * scale_one, axis=0)
    gain_column = jnp.pad(gain_attn_sums[:, None], ((0, 0), (0, 127)))
    kv_grad = low(jnp.concatenate([tn(normed, d_kv_low), gain_column], axis=1))
    at.kv_terms = terms(lambda owner: take(by_rows(kv_grad), owner), "fsdp")
    blocks = partial.reshape(2, 2, part_rows, -1)
    at.kept, at.sent = take(blocks, core_rank, 1), take(blocks, 1 - core_rank, 1)
    at.query_1_got = around(at.query_1, "fsdp")
    at.up_got_1 = flip(at.up_far[1], "ctx", 2)
    at.gate_got = flip(at.gate_sent, "ctx", 1)
    at.up_own = low(with_own(*at.drop("up_own", "up_own_got")))
    at.out_z = low(wide(at.out_z) + wide(at.out_terms[1]))
    at.next()
    at.drop("d_query_low", "kv_low", "d_kv", "gate_sent")
    at.query_1 = low(with_own(*at.drop("query_1", "query_1_got")))
    at.got = flip(at.sent, "tp", 1)
    at.next()
    summed_rows = wide(at.kept) + wide(at.got)
    at.kept, at.sent = take(summed_rows, y_rank), low(take(summed_rows, 1 - y_rank))
    at.next()
    at.got = flip(at.sent, "tp", 2)
    at.query_2_got = around(at.query_2, "fsdp")
    at.query_z = ring(at.query_1[0], "ctx")
    at.out_z = ring(at.out_z, "ctx")
    at.next()
    at.query_z = low(wide(at.query_z) + wide(at.query_1[1]))
    at.out_z = low(wide(at.out_z) + wide(at.out_terms[2]))
    at.query_2 = with_own(*at.drop("query_2", "query_2_got"))
    at.d_normed = at.kept + wide(at.got)
    up_got = jnp.stack(at.drop("up_got_0", "up_got_1"))
    at.up_kept, at.up_sent = near_split(wide(at.up_own) + wide(up_got))
    at.next()
    at.drop("query_1", "kept", "sent", "got")
    at.query_z = ring(at.query_z, "ctx")
    at.out_z = ring(at.out_z, "ctx")
    at.kv_got = around(at.kv_terms, "fsdp")
    at.up_got = flip(at.up_sent, "ctx", 1)
    moving = ring(at.vector, "fsdp")
    at.vector = at.vector + moving
    for _ in range(2, fsdp_count):
        moving = ring(moving, "fsdp")
        at.vector = at.vector + moving
    at.next()
    at.query_z = low(wide(at.query_z) + at.query_2[0])
    kv_mine = low(with_own(*at.drop("kv_terms", "kv_got")))
    at.kv_own = take(kv_mine, ctx_rank)
    at.kv_sent = [take(kv_mine, (ctx_rank + by) % ctx_count) for by in range(1, ctx_count)]

    def to_tp_back(mine):
        blocks = low(mine).reshape(tp_count, own_rows, -1)
        return [take(blocks, tp_rank ^ bit) for bit in range(tp_count)]

    at.out_back = to_tp_back(wide(at.out_z) + wide(at.out_terms[3]))
    at.next()
    at.drop("up_far", "up_own", "out_z", "out_terms")
    at.query_z = ring(at.query_z, "ctx")
    at.kv_got = [ring(at.kv_sent[by - 1], "ctx", by) for by in range(1, ctx_count)]
    at.next()
    at.query_back = to_tp_back(wide(at.query_z) + at.query_2[1])
    at.kv_back = to_tp_back(sum([wide(got) for got in at.kv_got], wide(at.kv_own)))
    at.next()
    at.drop("query_z", "query_2", "kv_got", "kv_own", "kv_sent", "up_sent")

    def whole_heads(parts):
        columns = []
        for rank, part in enumerate(parts):
            first = rank * (slot_count - 1) + min(rank, fuller)
            base = min(first, head_count - slot_count)
            held = slot_count - 1 + (1 if rank < fuller else 0)
            start = (first - base) * head_size
            columns.append(wide(part[:, start : start + held * head_size]))
        return jnp.concatenate(columns, axis=1)

    query_grad = whole_heads(swapped(flip_tp(at.query_back), tp_rank))
    out_grad = whole_heads(swapped(flip_tp(at.out_back), tp_rank))
    kv_parts = [wide(part) for part in swapped(flip_tp(at.kv_back), tp_rank)]
    kv_grad = jnp.concatenate([part[:, :kv_width] for part in kv_parts], axis=1)
    gain_attn_grad = sum(part[:, kv_width] for part in kv_parts)
    down_grad = near_joined(at.down_kept, at.down_got).T
    gate_grad = near_joined(at.gate_kept, at.gate_got)
    up_grad = near_joined(at.up_kept, at.up_got)
    gain_mlp_grad = lax.dynamic_slice_in_dim(at.vector, own_start, own_rows, 0)
    loss = at.vector[width] / (count * width)
    d_normed, d_residual = at.d_normed, at.d_residual
    scale_part = lax.dynamic_slice_in_dim(scale_one, tp_rank * part_rows, part_rows, 0)
    scaled = gain_attn * d_normed
    inner_one = jnp.mean(scaled * inputs_part, axis=-1, keepdims=True)
    input_grad = d_residual + scale_part * scaled - inputs_part * scale_part**3 * inner_one
    return (
        low(output)[None],
        loss,
        input_grad[None],
        gain_attn_grad,
        query_grad,
        kv_grad,
        out_grad,
        gain_mlp_grad,
        gate_grad,
        up_grad,
        down_grad,
    )


def solution(mesh):
    in_specs = (
        P("fsdp", "ctx", None),
        P(),
        P("fsdp", ("ctx", "tp"), None),
        P(("fsdp", "ctx", "tp")),
        P(("fsdp", "ctx", "tp"), None),
        P(("fsdp", "ctx", "tp"), None),
        P(("fsdp", "ctx", "tp"), None),
        P(("fsdp", "ctx", "tp")),
        P(("fsdp", "ctx"), "tp"),
        P(("fsdp", "ctx"), "tp"),
        P("tp", ("fsdp", "ctx")),
    )
    out_specs = (
        P("fsdp", ("ctx", "tp"), None),
        P(),
        P("fsdp", ("ctx", "tp"), None),
        P(("fsdp", "ctx", "tp")),
        P(("fsdp", "ctx", "tp"), None),
        P(("fsdp", "ctx", "tp"), None),
        P(("fsdp", "ctx", "tp"), None),
        P(("fsdp", "ctx", "tp")),
        P(("fsdp", "ctx"), "tp"),
        P(("fsdp", "ctx"), "tp"),
        P("tp", ("fsdp", "ctx")),
    )
    return jax.shard_map(local, mesh=mesh, in_specs=in_specs, out_specs=out_specs, check_vma=False)
```

```python
import jax
import jax.numpy as jnp
from jax import lax
from jax.experimental import pallas as pl
from jax.experimental.pallas import tpu as pltpu
from jax.sharding import PartitionSpec as P

W = 2048

epsilon = 1e-06
lowest = -1e30
ROWS = 256
VMEM_BYTES = 40 * 1024 * 1024


def flip(array, axis, bit):
    return lax.ppermute(array, axis, [(i, i ^ bit) for i in range(lax.axis_size(axis))])


def ring(array, axis, by=1):
    count = lax.axis_size(axis)
    return lax.ppermute(array, axis, [(i, (i + by) % count) for i in range(count)])


def shifted(array, axis, by):
    count = lax.axis_size(axis)
    pairs = [(i, i + by) for i in range(count) if 0 <= i + by < count]
    return lax.ppermute(array, axis, pairs)


class Steps:
    def next(self):
        self.__dict__.update(lax.optimization_barrier(dict(self.__dict__)))

    def drop(self, *names):
        return [self.__dict__.pop(name) for name in names]


def sync(*trees):
    return lax.optimization_barrier(trees)


def after(array, *others):
    return lax.optimization_barrier((array, others))[0]


def low(values):
    return values.astype(jnp.bfloat16)


def wide(values):
    return values.astype(jnp.float32)


def take(array, index, axis=0):
    return lax.dynamic_index_in_dim(array, index, axis, keepdims=False)


def swapped(blocks, rank):
    if len(blocks) == 2:
        odd = rank == 1
        return [jnp.where(odd, blocks[1], blocks[0]), jnp.where(odd, blocks[0], blocks[1])]
    first = swapped(blocks[:2], rank % 2) + swapped(blocks[2:], rank % 2)
    outer = rank // 2 == 1
    return [jnp.where(outer, first[i ^ 2], first[i]) for i in range(4)]


def place(pieces, slots):
    count = len(pieces)
    shape = pieces[0].shape

    def body(slots_ref, *refs):
        out_ref, held, came, left = refs[count:]
        into = [pltpu.make_async_copy(refs[k], held.at[k], came.at[k]) for k in range(count)]
        out_of = [
            pltpu.make_async_copy(held.at[k], out_ref.at[slots_ref[k]], left.at[k])
            for k in range(count)
        ]
        for copy in into:
            copy.start()
        for first, second in zip(into, out_of):
            first.wait()
            second.start()
        for copy in out_of:
            copy.wait()

    return pl.pallas_call(
        body,
        out_shape=jax.ShapeDtypeStruct((count,) + shape, pieces[0].dtype),
        grid_spec=pltpu.PrefetchScalarGridSpec(
            num_scalar_prefetch=1,
            grid=(1,),
            in_specs=[pl.BlockSpec(memory_space=pl.ANY)] * count,
            out_specs=pl.BlockSpec(memory_space=pl.ANY),
            scratch_shapes=[
                pltpu.VMEM((count,) + shape, pieces[0].dtype),
                pltpu.SemaphoreType.DMA((count,)),
                pltpu.SemaphoreType.DMA((count,)),
            ],
        ),
        compiler_params=pltpu.CompilerParams(vmem_limit_bytes=VMEM_BYTES),
        cost_estimate=pl.CostEstimate(
            flops=0, bytes_accessed=4 * count * pieces[0].size, transcendentals=0
        ),
        name="place",
    )(jnp.stack(slots).astype(jnp.int32), *pieces)


def nn(first, second):
    return lax.dot_general(
        first, second, (((1,), (0,)), ((), ())), preferred_element_type=jnp.float32
    )


def nt(first, second):
    return lax.dot_general(
        first, second, (((1,), (1,)), ((), ())), preferred_element_type=jnp.float32
    )


def tn(first, second):
    return lax.dot_general(
        first, second, (((0,), (0,)), ((), ())), preferred_element_type=jnp.float32
    )


def ring_sum(block_of, axis):
    count = lax.axis_size(axis)
    rank = lax.axis_index(axis)
    moving = None
    for step in range(1, count):
        term = block_of((rank - step) % count)
        moving = low(term if moving is None else wide(moving) + wide(term))
        moving = ring(moving, axis)
    own = wide(block_of(rank))
    return own if moving is None else own + wide(moving)


def attention_forward(queries, keyvals, live, first_key, head_size):
    rows, columns = queries.shape
    heads = columns // head_size
    reach = W + ROWS
    lead = keyvals.shape[0] - rows - W

    def body(info_ref, q_ref, kv_ref, o_ref):
        head, block = pl.program_id(0), pl.program_id(1)
        start = pl.multiple_of(lead + block * ROWS, ROWS)
        keys = kv_ref[pl.ds(start, reach), :head_size]
        vals = kv_ref[pl.ds(start, reach), head_size:]
        scores = nt(q_ref[...], keys)
        row = lax.broadcasted_iota(jnp.int32, scores.shape, 0)
        column = lax.broadcasted_iota(jnp.int32, scores.shape, 1)
        ahead = column - row
        allowed = (ahead > 0) & (ahead <= W) & (column >= info_ref[0] - start)
        scores = jnp.where(allowed, scores, lowest)
        peak = jnp.max(scores, axis=1, keepdims=True)
        shares = jnp.exp(scores - peak)
        total = jnp.sum(shares, axis=1, keepdims=True)
        probs = low(shares * (1.0 / total))
        mixed = nn(probs, vals)
        o_ref[...] = low(mixed * wide(info_ref[1 + head]))

    return pl.pallas_call(
        body,
        out_shape=jax.ShapeDtypeStruct((rows, columns), jnp.bfloat16),
        grid_spec=pltpu.PrefetchScalarGridSpec(
            num_scalar_prefetch=1,
            grid=(heads, rows // ROWS),
            in_specs=[
                pl.BlockSpec((ROWS, head_size), lambda h, i, info: (i, h)),
                pl.BlockSpec(keyvals.shape, lambda h, i, info: (0, 0)),
            ],
            out_specs=pl.BlockSpec((ROWS, head_size), lambda h, i, info: (i, h)),
        ),
        compiler_params=pltpu.CompilerParams(vmem_limit_bytes=VMEM_BYTES),
        cost_estimate=pl.CostEstimate(
            flops=4 * heads * rows * reach * head_size,
            bytes_accessed=4 * rows * columns + 2 * keyvals.size,
            transcendentals=heads * rows * reach,
        ),
        name="attention_forward",
    )(jnp.concatenate([first_key[None], live]).astype(jnp.int32), queries, keyvals)


def attention_backward(queries, keyvals, d_attended, first_key, head_size):
    rows, columns = queries.shape
    heads = columns // head_size
    reach = W + ROWS
    span = keyvals.shape[0]
    lead = span - rows - W

    def body(info_ref, q_ref, kv_ref, do_ref, dq_ref, dkv_ref, sums):
        head, block = pl.program_id(0), pl.program_id(1)

        @pl.when((head == 0) & (block == 0))
        def _():
            sums[...] = jnp.zeros_like(sums)

        start = pl.multiple_of(lead + block * ROWS, ROWS)
        keys = kv_ref[pl.ds(start, reach), :head_size]
        vals = kv_ref[pl.ds(start, reach), head_size:]
        query = q_ref[...]
        d_out = do_ref[...]
        scores = nt(keys, query)
        column = lax.broadcasted_iota(jnp.int32, scores.shape, 0)
        row = lax.broadcasted_iota(jnp.int32, scores.shape, 1)
        ahead = column - row
        allowed = (ahead > 0) & (ahead <= W) & (column >= info_ref[0] - start)
        scores = jnp.where(allowed, scores, lowest)
        peak = jnp.max(scores, axis=0, keepdims=True)
        shares = jnp.exp(scores - peak)
        total = jnp.sum(shares, axis=0, keepdims=True)
        probs = shares * (1.0 / total)
        d_probs = nt(vals, d_out)
        inner = jnp.sum(probs * d_probs, axis=0, keepdims=True)
        d_scores = low(probs * (d_probs - inner))
        dq_ref[...] = tn(d_scores, keys)
        sums[pl.ds(start, reach), :head_size] += nn(d_scores, query)
        sums[pl.ds(start, reach), head_size:] += nn(low(probs), d_out)

        @pl.when((head == heads - 1) & (block == rows // ROWS - 1))
        def _():
            dkv_ref[...] = low(sums[...])

    return pl.pallas_call(
        body,
        out_shape=(
            jax.ShapeDtypeStruct((rows, columns), jnp.float32),
            jax.ShapeDtypeStruct(keyvals.shape, jnp.bfloat16),
        ),
        grid_spec=pltpu.PrefetchScalarGridSpec(
            num_scalar_prefetch=1,
            grid=(heads, rows // ROWS),
            in_specs=[
                pl.BlockSpec((ROWS, head_size), lambda h, i, info: (i, h)),
                pl.BlockSpec(keyvals.shape, lambda h, i, info: (0, 0)),
                pl.BlockSpec((ROWS, head_size), lambda h, i, info: (i, h)),
            ],
            out_specs=(
                pl.BlockSpec((ROWS, head_size), lambda h, i, info: (i, h)),
                pl.BlockSpec(keyvals.shape, lambda h, i, info: (0, 0)),
            ),
            scratch_shapes=[pltpu.VMEM(keyvals.shape, jnp.float32)],
        ),
        compiler_params=pltpu.CompilerParams(vmem_limit_bytes=VMEM_BYTES),
        cost_estimate=pl.CostEstimate(
            flops=10 * heads * rows * reach * head_size,
            bytes_accessed=8 * rows * columns + 4 * keyvals.size,
            transcendentals=heads * rows * reach,
        ),
        name="attention_backward",
    )(first_key[None].astype(jnp.int32), queries, keyvals, d_attended)


def gelu_tanh(values):
    return jax.nn.gelu(values, approximate=True)


def local(
    hidden,
    lengths,
    teacher,
    attn_gain,
    query_weight,
    kv_weight,
    out_weight,
    mlp_gain,
    gate_weight,
    up_weight,
    down_weight,
):
    tp_count = lax.axis_size("tp")
    ctx_count = lax.axis_size("ctx")
    fsdp_count = lax.axis_size("fsdp")
    tp_rank = lax.axis_index("tp")
    ctx_rank = lax.axis_index("ctx")
    fsdp_rank = lax.axis_index("fsdp")
    y_rank, core_rank = tp_rank // 2, tp_rank % 2
    hi_rank, lo_rank = ctx_rank // 2, ctx_rank % 2
    seq_count, rows, width = hidden.shape
    assert seq_count == 1 and tp_count == 4 and ctx_count == 4
    part_rows = rows // tp_count
    head_size = kv_weight.shape[1] // 2
    head_count = query_weight.shape[1] // head_size
    slot_count = -(-head_count // tp_count)
    slot_width = slot_count * head_size
    fuller = head_count - (slot_count - 1) * tp_count
    kv_width = 2 * head_size // tp_count

    def first_head_of(rank):
        return rank * (slot_count - 1) + jnp.minimum(rank, fuller)

    def slot_base_of(rank):
        return jnp.minimum(first_head_of(rank), head_count - slot_count)

    slot_heads = slot_base_of(tp_rank) + jnp.arange(slot_count)
    first_head = first_head_of(tp_rank)
    held_heads = slot_count - 1 + (tp_rank < fuller).astype(jnp.int32)
    live = ((slot_heads >= first_head) & (slot_heads < first_head + held_heads)).astype(jnp.int32)

    def over_tp(columns_of):
        blocks = [columns_of(tp_rank)]
        for bit in range(1, tp_count):
            blocks.append(flip(columns_of(tp_rank ^ bit), "tp", bit))
        return jnp.concatenate(swapped(blocks, tp_rank), axis=0)

    def over_fsdp(block):
        blocks = [block]
        for _ in range(1, fsdp_count):
            blocks.append(ring(blocks[-1], "fsdp"))
        return blocks

    def placed(by_ctx):
        pieces, slots = [], []
        for step, blocks in enumerate(by_ctx):
            for turn_at, block in enumerate(blocks):
                pieces.append(block)
                slots.append(
                    (fsdp_rank - turn_at) % fsdp_count * ctx_count
                    + (ctx_rank - step) % ctx_count
                )
        return place(pieces, slots).reshape(width, pieces[0].shape[1])

    def head_columns(weight):
        return lambda rank: lax.dynamic_slice_in_dim(
            weight, slot_base_of(rank) * head_size, slot_width, 1
        )

    unit_count = gate_weight.shape[1]
    half = -(-unit_count // 256) * 128
    rest = unit_count - half

    def near_halves(block):
        near, far = block[:, :half], jnp.pad(block[:, half:], ((0, 0), (0, half - rest)))
        mine = jnp.where(lo_rank == 0, near, far)
        theirs = jnp.where(lo_rank == 0, far, near)
        return mine, theirs

    def near_pair(halves):
        mine, theirs = halves
        return jnp.stack(swapped([mine, flip(theirs, "ctx", 1)], lo_rank))

    def quarters(pair):
        return jnp.split(pair.reshape(-1, half), 4)

    def far(pieces):
        if len(pieces) == 1:
            return [flip(pieces[0], "ctx", 2)]
        return jnp.split(flip(jnp.concatenate(pieces, axis=0), "ctx", 2), len(pieces))

    def mlp_placed(own, other):
        pieces, slots = [], []
        for far_bit, blocks in enumerate((own, other)):
            for turn_at, block in enumerate(blocks):
                pieces.append(block.reshape(-1, half))
                slots.append((fsdp_rank - turn_at) % fsdp_count * 2 + (hi_rank ^ far_bit))
        return place(pieces, slots).reshape(width, half)

    inputs_low = hidden[0]
    inputs = wide(inputs_low)
    inputs_part_low = lax.dynamic_slice_in_dim(inputs_low, tp_rank * part_rows, part_rows, 0)
    inputs_part = wide(inputs_part_low)
    scale_one = lax.rsqrt(jnp.mean(inputs * inputs, axis=-1, keepdims=True) + epsilon)
    positions = ctx_rank * rows + jnp.arange(rows)
    quarter = head_size // 4
    frequency = 10000.0 ** (-(jnp.arange(quarter).astype(jnp.float32) * 4.0 / head_size))
    angle = wide(positions)[:, None] * frequency[None, :]
    cosine, sine = jnp.cos(angle), jnp.sin(angle)

    def turn(values, cosine, sine):
        first, second = values[..., :quarter], values[..., quarter : 2 * quarter]
        return jnp.concatenate(
            [
                first * cosine - second * sine,
                second * cosine + first * sine,
                values[..., 2 * quarter :],
            ],
            axis=-1,
        )

    turning = tp_rank == 0
    kv_cosine, kv_sine = jnp.where(turning, cosine, 1.0), jnp.where(turning, sine, 0.0)
    query_scale = head_size ** (-0.5)
    reach_back = min((W - 2) // rows + 1, ctx_count - 1)
    first_key = (reach_back - jnp.minimum(ctx_rank, reach_back)) * rows

    at = Steps()
    gains = jnp.pad(jnp.stack([attn_gain, mlp_gain], axis=1), ((0, 0), (0, 126)))

    def qkv_columns(rank):
        kv = lax.dynamic_slice_in_dim(kv_weight, rank * kv_width, kv_width, 1)
        return jnp.concatenate([head_columns(query_weight)(rank), kv, gains], axis=1)

    def to_tp(columns_of):
        return [columns_of(tp_rank ^ bit) for bit in range(tp_count)]

    def flip_tp(blocks):
        return blocks[:1] + [flip(blocks[bit], "tp", bit) for bit in range(1, tp_count)]

    def from_tp(blocks):
        return jnp.concatenate(swapped(blocks, tp_rank), axis=0)

    def paired(mine, got):
        return jnp.stack(swapped([mine, got], lo_rank))

    at.qkv = to_tp(qkv_columns)
    at.gate_mine, at.gate_sent = near_halves(gate_weight)
    at.out = to_tp(head_columns(out_weight))
    at.up_mine, at.up_sent = near_halves(up_weight)
    at.down_mine, at.down_sent = near_halves(down_weight.T)
    at.next()
    at.qkv = flip_tp(at.qkv)
    at.gate_got = flip(at.gate_sent, "ctx", 1)
    at.next()
    at.qkv_0 = from_tp(at.drop("qkv")[0])
    at.gate_pair = paired(*at.drop("gate_mine", "gate_got"))
    at.next()
    at.qkv_x = [over_fsdp(at.qkv_0)]
    at.qkv_1 = ring(at.qkv_0, "ctx")
    at.next()
    at.qkv_x.append(over_fsdp(at.qkv_1))
    at.qkv_2 = ring(at.qkv_1, "ctx")
    at.next()
    at.qkv_x.append(over_fsdp(at.qkv_2))
    at.qkv_3 = ring(at.qkv_2, "ctx")
    at.out = flip_tp(at.out)
    at.next()
    at.out_0 = from_tp(at.drop("out")[0])
    at.drop("qkv_0", "qkv_1", "qkv_2", "gate_sent")
    at.next()
    at.qkv_x.append(over_fsdp(at.qkv_3))
    at.out_1 = ring(at.out_0, "ctx")
    at.next()

    qkv_part = placed(at.drop("qkv_x")[0])
    gain_attn = wide(qkv_part[:, slot_width + kv_width])
    gain_mlp = wide(qkv_part[:, slot_width + kv_width + 1])
    at.normed = low(inputs * scale_one * gain_attn)
    at.qkv_raw = nn(at.normed, qkv_part)
    at.gate_a = over_fsdp(at.gate_pair[0])
    at.out_2 = ring(at.out_1, "ctx")
    at.up_got = flip(at.up_sent, "ctx", 1)
    at.next()
    (qkv_raw,) = at.drop("qkv_raw")
    kv_raw = qkv_raw[:, slot_width : slot_width + kv_width]
    at.kv_own = low(turn(kv_raw, kv_cosine, kv_sine))
    query_raw = qkv_raw[:, :slot_width].reshape(rows, slot_count, head_size)
    queries = low(turn(query_raw, cosine[:, None, :], sine[:, None, :]) * query_scale)
    at.queries = queries.reshape(rows, slot_width)
    at.gate_b = over_fsdp(at.gate_pair[1])
    at.out_3 = ring(at.out_2, "ctx")
    at.next()
    normed = at.normed
    at.up_pair = paired(*at.drop("up_mine", "up_got"))
    at.out_near = jnp.stack([at.out_0, at.out_1, at.out_2, at.out_3])
    at.next()
    out_x = over_fsdp(at.out_near)
    at.chunks = [shifted(at.kv_own, "ctx", by) for by in range(reach_back, 0, -1)]
    at.next()
    at.kv_column = jnp.concatenate(at.drop("chunks")[0] + [at.kv_own], axis=0)
    at.gate_far = jnp.concatenate(quarters(at.gate_pair)[:2], axis=0)
    at.drop("out_0", "out_1", "out_2", "kv_own", "qkv_3")
    at.next()
    at.kv_over_y = flip(at.kv_column, "tp", 2)
    at.down_got = flip(at.down_sent, "ctx", 1)
    at.far_2 = flip(at.gate_far, "ctx", 2)
    at.out_x = out_x
    at.next()
    at.kv_pair = jnp.stack(at.drop("kv_column", "kv_over_y"))
    at.down_pair = paired(*at.drop("down_mine", "down_got"))
    at.next()
    at.kv_other = flip(at.kv_pair, "tp", 1)
    at.far_1 = far(quarters(at.gate_pair)[2:3])
    (out_x,) = at.drop("out_x")
    at.out_part = placed([[block[i] for block in out_x] for i in range(ctx_count)])
    at.next()
    kv_pair, kv_other = at.drop("kv_pair", "kv_other")
    at.keyvals = jnp.concatenate(
        swapped([kv_pair[0], kv_other[0], kv_pair[1], kv_other[1]], tp_rank), axis=1
    )
    at.mixed_far = jnp.concatenate(quarters(at.gate_pair)[3:] + quarters(at.up_pair)[:2], axis=0)
    at.drop("up_sent", "down_sent", "gate_far", "out_near")
    at.next()

    queries, keyvals = at.queries, at.keyvals
    at.attended = attention_forward(queries, keyvals, live, first_key, head_size)
    blocks = low(nt(at.attended, at.out_part)).reshape(2, 2, part_rows, -1)
    at.kept, at.sent = take(blocks, core_rank, 1), take(blocks, 1 - core_rank, 1)
    at.up_x = over_fsdp(at.up_pair)
    at.far_3 = flip(at.mixed_far, "ctx", 2)
    at.next()

    out_part = at.out_part
    quarter_rows = at.far_1[0].shape[0]
    at.got = flip(at.sent, "tp", 1)
    at.gate_other = jnp.concatenate(
        [at.far_2] + at.far_1 + [at.far_3[:quarter_rows]], axis=0
    ).reshape(at.gate_pair.shape)
    at.up_far = jnp.concatenate(quarters(at.up_pair)[2:], axis=0)
    at.next()
    summed = wide(at.kept) + wide(at.got)
    at.kept, at.sent = take(summed, y_rank), low(take(summed, 1 - y_rank))
    at.next()
    at.got = flip(at.sent, "tp", 2)
    at.gate_z = over_fsdp(at.gate_other)
    at.far_4 = flip(at.up_far, "ctx", 2)
    at.next()

    middle = part_rows // 2

    def gather_sides():
        at.over_y, at.over_z = flip(at.part, "tp", 2), flip(at.part, "ctx", 1)
        at.core_own = flip(at.part, "tp", 1)

    def between_sides_and_corners():
        at.to_z, at.to_y = at.over_y[:middle], at.over_z[middle:]
        at.sides = jnp.concatenate([at.over_y, at.over_z], axis=0)

    def gather_corners():
        at.corner_top = flip(at.to_z, "ctx", 1)
        at.corner_end = flip(at.to_y, "tp", 2)
        at.core_sides = flip(at.sides, "tp", 1)

    def between_corners_and_core():
        at.corner = jnp.concatenate(at.drop("corner_top", "corner_end"), axis=0)
        at.drop("to_z", "to_y", "over_y", "over_z")

    def gathered():
        return jnp.concatenate(
            at.drop("part", "sides", "corner", "core_own", "core_sides", "core_corner"), axis=0
        )

    def before_sum(partial):
        mine, theirs = partial.reshape(2, 4, part_rows, -1)
        at.mine, at.mine_corner = mine[:3], mine[3]
        at.theirs, at.theirs_corner = theirs[:3], theirs[3]

    def between_core_and_corners():
        corner = wide(at.drop("mine_corner")[0]) + wide(at.drop("got_corner")[0])
        at.to_z, at.to_y = low(corner[:middle]), low(corner[middle:])

    def sum_corners():
        at.corner_top = flip(at.to_z, "ctx", 1)
        at.corner_end = flip(at.to_y, "tp", 2)

    def between_corners_and_sides():
        mine, got, top, end = at.drop("mine", "got", "corner_top", "corner_end")
        own, over_y, over_z = wide(mine) + wide(got)
        at.over_y = low(jnp.concatenate([over_y[:middle] + wide(top), over_y[middle:]], axis=0))
        at.over_z = low(jnp.concatenate([over_z[:middle], over_z[middle:] + wide(end)], axis=0))
        at.part = own
        at.drop("theirs", "theirs_corner", "to_z", "to_y")

    def sum_sides():
        at.got_y, at.got_z = flip(at.over_y, "tp", 2), flip(at.over_z, "ctx", 1)

    def summed():
        own, got_y, got_z = at.drop("part", "got_y", "got_z")
        at.drop("over_y", "over_z")
        return own + wide(got_y) + wide(got_z)

    residual = inputs_part + (at.kept + wide(at.got))
    at.drop("kept", "got", "sent")
    scale_two = lax.rsqrt(jnp.mean(residual * residual, axis=-1, keepdims=True) + epsilon)
    at.residual = residual
    at.part = low(residual * scale_two * gain_mlp)
    at.down_quarters = quarters(at.down_pair)
    at.next()
    residual = at.residual
    gather_sides()
    at.down_x = over_fsdp(at.down_pair)
    at.far_5 = flip(at.down_quarters[0], "ctx", 2)
    at.up_a, at.up_b = at.far_3[quarter_rows:], at.far_4
    gate_a, gate_b, gate_z = at.drop("gate_a", "gate_b", "gate_z")
    at.gate_full = mlp_placed([jnp.stack(pair) for pair in zip(gate_a, gate_b)], gate_z)
    at.next()
    between_sides_and_corners()
    at.next()
    gather_corners()
    at.up_a = over_fsdp(at.up_a)
    at.far_6 = flip(at.down_quarters[1], "ctx", 2)
    at.next()
    between_corners_and_core()
    at.next()
    at.core_corner = flip(at.corner, "tp", 1)
    at.next()
    at.normed_two = gathered()
    at.gate_proj = nn(at.normed_two, at.gate_full)
    at.up_b = over_fsdp(at.up_b)
    at.far_7 = flip(at.down_quarters[2], "ctx", 2)
    at.down_a = jnp.concatenate([at.far_5, at.far_6], axis=0)
    at.next()
    gate_full = at.gate_full
    up_a, up_b = at.drop("up_a", "up_b")
    up_z = [jnp.stack(pair) for pair in zip(up_a, up_b)]
    up_full = mlp_placed(at.drop("up_x")[0], up_z)
    at.up_proj = nn(at.normed_two, up_full)
    at.down_a = over_fsdp(at.down_a)
    at.far_8 = flip(at.down_quarters[3], "ctx", 2)
    at.next()
    at.down_b = jnp.concatenate([at.far_7, at.far_8], axis=0)
    at.next()
    gate_proj, up_proj = at.gate_proj, at.up_proj
    activated, gelu_back = jax.vjp(gelu_tanh, gate_proj)
    at.hidden_act = low(activated * up_proj)
    at.down_b = over_fsdp(at.down_b)
    at.next()
    at.drop("far_1", "far_2", "far_3", "far_4", "far_5", "far_6", "far_7", "gate_pair", "up_pair")
    at.drop("far_8", "gate_other", "up_far", "down_quarters", "mixed_far")
    at.drop("gate_proj", "up_proj", "down_pair")
    down_x, down_a, down_b = at.drop("down_x", "down_a", "down_b")
    down_z = [jnp.stack(pair) for pair in zip(down_a, down_b)]
    down_full = mlp_placed(down_x, down_z)
    before_sum(low(nt(at.hidden_act, down_full)))
    at.next()
    at.got_corner = flip(at.theirs_corner, "tp", 1)
    at.next()
    between_core_and_corners()
    at.next()
    sum_corners()
    at.got = flip(at.theirs, "tp", 1)
    at.next()
    between_corners_and_sides()
    at.next()
    sum_sides()
    at.next()
    ffn_part = summed()

    my_length = lengths[fsdp_rank]
    part_positions = ctx_rank * rows + tp_rank * part_rows + jnp.arange(part_rows)
    valid = wide(part_positions < my_length)[:, None]
    output = (residual + ffn_part) * valid
    mismatch = output - wide(teacher[0])
    count = wide(jnp.sum(lengths))
    loss_part = jnp.sum(valid * mismatch * mismatch)
    at.d_output = valid * mismatch * (lengths.shape[0] * ctx_count * rows / count)
    at.part = low(at.d_output)
    at.next()
    gather_sides()
    at.next()
    between_sides_and_corners()
    at.next()
    gather_corners()
    at.next()
    between_corners_and_core()
    at.next()
    at.core_corner = flip(at.corner, "tp", 1)
    at.next()

    def terms(blocks_of, axis):
        count, rank = lax.axis_size(axis), lax.axis_index(axis)
        return [blocks_of((rank - step) % count) for step in range(1, count + 1)]

    def around(sent, axis):
        moving = ring(sent[0], axis)
        for term in sent[1:-1]:
            moving = ring(low(wide(moving) + wide(term)), axis)
        return moving

    def with_own(sent, arrived):
        return wide(sent[-1]) + wide(arrived)

    def far_and_own(grad):
        blocks = grad.reshape(fsdp_count, 2, 2, -1, half)
        return [
            terms(lambda owner: take(take(blocks, owner), high), "fsdp")
            for high in (1 - hi_rank, hi_rank)
        ]

    def blocks_of(grad):
        blocks = grad.reshape(fsdp_count, 2, 2, -1, half)
        return [
            terms(lambda owner: take(take(blocks, owner), high)[lo], "fsdp")
            for high in (1 - hi_rank, hi_rank)
            for lo in range(2)
        ]

    def near_split(mine):
        return wide(take(mine, lo_rank)), low(take(mine, 1 - lo_rank))

    def near_joined(kept, got):
        near, rest_of = swapped([kept, wide(got)], lo_rank)
        return jnp.concatenate([near, rest_of[:, :rest]], axis=1)

    at.d_ffn = gathered()
    at.down_terms = blocks_of(low(tn(at.d_ffn, at.hidden_act)))
    at.next()
    at.down_x = [around(at.down_terms[0], "fsdp")]
    d_hidden = nn(at.d_ffn, down_full)
    at.d_gate = low(gelu_back(d_hidden * up_proj)[0])
    at.d_up = low(d_hidden * activated)
    at.next()
    at.drop("d_ffn", "hidden_act")
    at.down_x += [around(at.down_terms[1], "fsdp")]
    at.gate_terms = blocks_of(low(tn(at.normed_two, at.d_gate)))
    at.next()
    at.down_far = [low(with_own(at.down_terms[i], at.down_x[i])) for i in range(2)]
    at.next()
    at.down_x += [around(at.down_terms[2], "fsdp"), around(at.down_terms[3], "fsdp")]
    at.down_got_0 = flip(at.down_far[0], "ctx", 2)
    before_sum(low(nt(at.d_gate, gate_full) + nt(at.d_up, up_full)))
    at.next()
    at.got_corner = flip(at.theirs_corner, "tp", 1)
    at.next()
    between_core_and_corners()
    at.drop("d_gate")
    at.down_rest = jnp.split(at.down_far[1], 2)
    at.next()
    sum_corners()
    at.got = flip(at.theirs, "tp", 1)
    at.gate_got = [around(at.gate_terms[0], "fsdp")]
    at.down_got_1 = flip(at.down_rest[0], "ctx", 2)
    at.next()
    between_corners_and_sides()
    at.next()
    sum_sides()
    down_terms, down_x = at.drop("down_terms", "down_x")
    at.down_own = jnp.stack([low(with_own(down_terms[i], down_x[i])) for i in (2, 3)])
    at.gate_got += [around(at.gate_terms[1], "fsdp"), around(at.gate_terms[2], "fsdp")]
    at.down_got_2 = flip(at.down_rest[1], "ctx", 2)
    at.up_terms = blocks_of(low(tn(at.normed_two, at.d_up)))
    at.next()
    at.drop("normed_two", "d_up", "down_far", "down_rest")
    at.gate_far = [low(with_own(at.gate_terms[i], at.gate_got[i])) for i in range(2)]
    d_normed_two = summed()
    scaled = gain_mlp * d_normed_two
    inner_two = jnp.mean(scaled * residual, axis=-1, keepdims=True)
    at.d_residual = at.d_output + scale_two * scaled - residual * scale_two**3 * inner_two
    at.gain_mlp_sums = jnp.sum(d_normed_two * residual * scale_two, axis=0)
    at.part = low(at.d_residual)
    at.next()
    at.over_y = flip(at.part, "tp", 2)
    got_0, got_1, got_2 = at.drop("down_got_0", "down_got_1", "down_got_2")
    down_got = jnp.stack([got_0, jnp.concatenate([got_1, got_2], axis=0)])
    at.down_kept, at.down_sent = near_split(wide(at.drop("down_own")[0]) + wide(down_got))
    at.gate_got += [around(at.gate_terms[3], "fsdp")]
    at.up_got = [around(at.up_terms[0], "fsdp")]
    at.gate_far_0 = flip(at.gate_far[0], "ctx", 2)
    at.next()
    at.pair = jnp.stack(at.drop("part", "over_y"))
    at.next()
    at.other = flip(at.pair, "tp", 1)
    at.next()
    pair, other = at.drop("pair", "other")
    d_attn = swapped([pair[0], other[0], pair[1], other[1]], tp_rank)
    at.d_attn = jnp.concatenate(d_attn, axis=0)
    at.next()
    at.down_got = flip(at.down_sent, "ctx", 1)
    at.up_got += [around(at.up_terms[1], "fsdp")]
    live_columns = jnp.repeat(live, head_size).astype(jnp.float32)
    at.d_attended = low(nn(at.d_attn, out_part) * live_columns)
    out_grad = low(tn(at.d_attn, at.attended))

    own_rows = attn_gain.shape[0]

    def split_sums(columns):
        rounded = low(columns)
        return jnp.concatenate([rounded, low(columns - wide(rounded))], axis=-1)

    def joined_sums(columns):
        return columns[..., :64] + columns[..., 64:]

    def by_rows(grad):
        return grad.reshape(fsdp_count, ctx_count, tp_count * own_rows, -1)

    def halves_of(grad):
        grad = by_rows(grad)
        turned = [take(grad, (ctx_rank - by) % ctx_count, 1) for by in range(1, ctx_count + 1)]
        pairs = [jnp.stack(turned[:2], axis=1), jnp.stack(turned[2:], axis=1)]
        return [terms(lambda owner: take(pair, owner), "fsdp") for pair in pairs]

    at.out_terms = halves_of(out_grad)
    at.next()
    at.drop("attended", "d_attn", "down_sent")
    at.d_queries, at.d_keyvals = attention_backward(
        queries, keyvals, at.d_attended, first_key, head_size
    )
    at.up_got += [around(at.up_terms[2], "fsdp"), around(at.up_terms[3], "fsdp")]
    at.gate_far_1 = flip(at.gate_far[1], "ctx", 2)
    at.next()
    kv_blocks = jnp.stack(jnp.split(at.d_keyvals, tp_count, axis=1)).reshape(2, 2, -1, kv_width)
    at.kv_kept, at.kv_sent = take(kv_blocks, core_rank, 1), take(kv_blocks, 1 - core_rank, 1)
    at.drop("d_attended", "d_keyvals")
    at.next()
    at.kv_got = flip(at.kv_sent, "tp", 1)
    at.next()
    kv_sum = wide(at.kv_kept) + wide(at.kv_got)
    at.kv_kept, at.kv_sent = take(kv_sum, y_rank), low(take(kv_sum, 1 - y_rank))
    at.up_far = [low(with_own(at.up_terms[i], at.up_got[i])) for i in range(2)]
    at.next()
    at.kv_got = flip(at.kv_sent, "tp", 2)
    at.up_far_0 = flip(at.up_far[0], "ctx", 2)
    at.out_got = [around(at.out_terms[0], "fsdp")]
    d_query_raw = turn(
        at.d_queries.reshape(rows, slot_count, head_size) * query_scale,
        cosine[:, None, :],
        -sine[:, None, :],
    )
    at.d_query_low = low(d_query_raw.reshape(rows, slot_width))
    at.query_terms = halves_of(low(tn(normed, at.d_query_low)))
    at.next()
    at.drop("d_queries", "kv_sent")
    kv_sum = (at.drop("kv_kept")[0] + wide(at.drop("kv_got")[0])).reshape(reach_back + 1, rows, -1)
    at.kv_low = [low(kv_sum[reach_back - by]) for by in range(1, reach_back + 1)]
    at.d_kv = kv_sum[reach_back]
    at.out_1 = low(with_own(at.out_terms[0], at.out_got[0]))
    at.next()
    gate_terms, gate_got = at.drop("gate_terms", "gate_got")
    gate_far_got = jnp.stack(at.drop("gate_far_0", "gate_far_1"))
    gate_own = jnp.stack([with_own(gate_terms[i], gate_got[i]) for i in (2, 3)])
    at.gate_kept, at.gate_sent = near_split(gate_own + wide(gate_far_got))
    at.drop("gate_far")
    at.kv_got = [shifted(at.kv_low[by - 1], "ctx", -by) for by in range(1, reach_back + 1)]
    at.out_got += [around(at.out_terms[1], "fsdp")]
    at.out_z = ring(at.out_1[0], "ctx")
    at.next()
    d_kv = at.d_kv
    for got in at.drop("kv_got")[0]:
        d_kv = d_kv + wide(got)
    d_kv_low = low(turn(d_kv, kv_cosine, -kv_sine))
    at.d_qkv = jnp.concatenate(
        [at.d_query_low, jnp.pad(d_kv_low, ((0, 0), (0, kv_width)))], axis=1
    )
    at.out_z = low(wide(at.out_z) + wide(at.out_1[1]))
    at.next()
    at.query_got = [around(at.query_terms[0], "fsdp")]
    at.up_far_1 = flip(at.up_far[1], "ctx", 2)
    at.gate_near = flip(at.gate_sent, "ctx", 1)
    at.partial = low(nt(at.d_qkv, qkv_part))
    at.next()
    (partial,) = at.drop("partial")
    d_kv_low = at.d_qkv[:, slot_width : slot_width + kv_width]
    gain_attn_sums = jnp.sum(wide(partial) * inputs * scale_one, axis=0)
    sums = [gain_attn_sums, at.gain_mlp_sums, jnp.full(gain_attn_sums.shape, loss_part)]
    columns = jnp.pad(jnp.stack(sums, axis=1), ((0, 0), (0, 61)))
    kv_grad = jnp.concatenate([low(tn(normed, d_kv_low)), split_sums(columns)], axis=1)
    at.kv_terms = terms(lambda owner: take(by_rows(kv_grad), owner), "fsdp")
    blocks = partial.reshape(2, 2, part_rows, -1)
    at.kept, at.sent = take(blocks, core_rank, 1), take(blocks, 1 - core_rank, 1)
    at.next()
    at.drop("d_query_low", "kv_low", "d_kv", "gate_sent", "d_qkv")
    at.query_1 = low(with_own(at.query_terms[0], at.query_got[0]))
    at.got = flip(at.sent, "tp", 1)
    at.next()
    summed_rows = wide(at.kept) + wide(at.got)
    at.kept, at.sent = take(summed_rows, y_rank), low(take(summed_rows, 1 - y_rank))
    at.out_2 = with_own(at.out_terms[1], at.out_got[1])
    at.next()
    at.got = flip(at.sent, "tp", 2)
    at.query_got += [around(at.query_terms[1], "fsdp")]
    at.query_z = ring(at.query_1[0], "ctx")
    at.out_z = ring(at.out_z, "ctx")
    at.next()
    at.query_z = low(wide(at.query_z) + wide(at.query_1[1]))
    at.out_z = low(wide(at.out_z) + at.out_2[0])
    at.query_2 = with_own(at.query_terms[1], at.query_got[1])
    at.d_normed = at.kept + wide(at.got)
    at.next()
    up_terms, up_got = at.drop("up_terms", "up_got")
    up_far_got = jnp.stack(at.drop("up_far_0", "up_far_1"))
    up_own = jnp.stack([with_own(up_terms[i], up_got[i]) for i in (2, 3)])
    at.up_kept, at.up_sent = near_split(up_own + wide(up_far_got))
    at.drop("query_1", "kept", "sent", "got", "up_far", "query_terms", "query_got")
    at.drop("out_terms", "out_got")
    at.query_z = ring(at.query_z, "ctx")
    at.out_z = ring(at.out_z, "ctx")
    at.kv_got = around(at.kv_terms, "fsdp")
    at.next()
    at.query_z = low(wide(at.query_z) + at.query_2[0])
    kv_mine = with_own(*at.drop("kv_terms", "kv_got"))
    kv_mine = jnp.concatenate(
        [low(kv_mine[..., :kv_width]), split_sums(joined_sums(kv_mine[..., kv_width:]))], axis=-1
    )
    at.kv_own = take(kv_mine, ctx_rank)
    at.kv_sent = [take(kv_mine, (ctx_rank + by) % ctx_count) for by in range(1, ctx_count)]

    def to_tp_back(mine):
        blocks = low(mine).reshape(tp_count, own_rows, -1)
        return [take(blocks, tp_rank ^ bit) for bit in range(tp_count)]

    at.out_back = to_tp_back(wide(at.out_z) + at.out_2[1])
    at.next()
    at.drop("out_z", "out_2")
    at.out_back = flip_tp(at.out_back)
    at.query_z = ring(at.query_z, "ctx")
    at.kv_got = [ring(at.kv_sent[by - 1], "ctx", by) for by in range(1, ctx_count)]
    at.next()
    query_mine = low(wide(at.query_z) + at.query_2[1])
    kv_mine = sum([wide(got) for got in at.kv_got], wide(at.kv_own))
    kv_mine = jnp.concatenate(
        [low(kv_mine[:, :kv_width]), split_sums(joined_sums(kv_mine[:, kv_width:]))], axis=1
    )
    at.back = to_tp_back(jnp.concatenate([query_mine, kv_mine], axis=1))
    at.next()
    up_near = flip(at.up_sent, "ctx", 1)
    at.drop("query_z", "query_2", "kv_got", "kv_own", "kv_sent", "up_sent")

    def whole_heads(parts):
        columns = []
        for rank, part in enumerate(parts):
            first = rank * (slot_count - 1) + min(rank, fuller)
            base = min(first, head_count - slot_count)
            held = slot_count - 1 + (1 if rank < fuller else 0)
            start = (first - base) * head_size
            columns.append(wide(part[:, start : start + held * head_size]))
        return jnp.concatenate(columns, axis=1)

    parts = swapped(flip_tp(at.back), tp_rank)
    query_grad = whole_heads([part[:, :slot_width] for part in parts])
    out_grad = whole_heads(swapped(at.out_back, tp_rank))
    kv_parts = [wide(part[:, slot_width:]) for part in parts]
    kv_grad = jnp.concatenate([part[:, :kv_width] for part in kv_parts], axis=1)
    sums = joined_sums(sum(part[:, kv_width:] for part in kv_parts))
    gain_attn_grad, gain_mlp_grad, loss_sum = sums[:, 0], sums[:, 1], sums[0, 2]
    down_grad = near_joined(at.down_kept, at.down_got).T
    gate_grad = near_joined(at.gate_kept, at.gate_near)
    up_grad = near_joined(at.up_kept, up_near)
    loss = loss_sum / (count * width)
    d_normed, d_residual = at.d_normed, at.d_residual
    scale_part = lax.dynamic_slice_in_dim(scale_one, tp_rank * part_rows, part_rows, 0)
    scaled = gain_attn * d_normed
    inner_one = jnp.mean(scaled * inputs_part, axis=-1, keepdims=True)
    input_grad = d_residual + scale_part * scaled - inputs_part * scale_part**3 * inner_one
    return (
        low(output)[None],
        loss,
        input_grad[None],
        gain_attn_grad,
        query_grad,
        kv_grad,
        out_grad,
        gain_mlp_grad,
        gate_grad,
        up_grad,
        down_grad,
    )


def solution(mesh):
    in_specs = (
        P("fsdp", "ctx", None),
        P(),
        P("fsdp", ("ctx", "tp"), None),
        P(("fsdp", "ctx", "tp")),
        P(("fsdp", "ctx", "tp"), None),
        P(("fsdp", "ctx", "tp"), None),
        P(("fsdp", "ctx", "tp"), None),
        P(("fsdp", "ctx", "tp")),
        P(("fsdp", "ctx"), "tp"),
        P(("fsdp", "ctx"), "tp"),
        P("tp", ("fsdp", "ctx")),
    )
    out_specs = (
        P("fsdp", ("ctx", "tp"), None),
        P(),
        P("fsdp", ("ctx", "tp"), None),
        P(("fsdp", "ctx", "tp")),
        P(("fsdp", "ctx", "tp"), None),
        P(("fsdp", "ctx", "tp"), None),
        P(("fsdp", "ctx", "tp"), None),
        P(("fsdp", "ctx", "tp")),
        P(("fsdp", "ctx"), "tp"),
        P(("fsdp", "ctx"), "tp"),
        P("tp", ("fsdp", "ctx")),
    )
    return jax.shard_map(local, mesh=mesh, in_specs=in_specs, out_specs=out_specs, check_vma=False)
```

```python
import jax
import jax.numpy as jnp
from jax import lax
from jax.experimental import pallas as pl
from jax.experimental.pallas import tpu as pltpu
from jax.sharding import PartitionSpec as P

W = 2048

epsilon = 1e-06
lowest = -1e30
ROWS = 256
VMEM_BYTES = 40 * 1024 * 1024


def flip(array, axis, bit):
    return lax.ppermute(array, axis, [(i, i ^ bit) for i in range(lax.axis_size(axis))])


def ring(array, axis, by=1):
    count = lax.axis_size(axis)
    return lax.ppermute(array, axis, [(i, (i + by) % count) for i in range(count)])


def shifted(array, axis, by):
    count = lax.axis_size(axis)
    pairs = [(i, i + by) for i in range(count) if 0 <= i + by < count]
    return lax.ppermute(array, axis, pairs)


class Steps:
    def next(self):
        self.__dict__.update(lax.optimization_barrier(dict(self.__dict__)))

    def drop(self, *names):
        return [self.__dict__.pop(name) for name in names]


def sync(*trees):
    return lax.optimization_barrier(trees)


def after(array, *others):
    return lax.optimization_barrier((array, others))[0]


def low(values):
    return values.astype(jnp.bfloat16)


def wide(values):
    return values.astype(jnp.float32)


def take(array, index, axis=0):
    return lax.dynamic_index_in_dim(array, index, axis, keepdims=False)


def swapped(blocks, rank):
    if len(blocks) == 2:
        odd = rank == 1
        return [jnp.where(odd, blocks[1], blocks[0]), jnp.where(odd, blocks[0], blocks[1])]
    first = swapped(blocks[:2], rank % 2) + swapped(blocks[2:], rank % 2)
    outer = rank // 2 == 1
    return [jnp.where(outer, first[i ^ 2], first[i]) for i in range(4)]


def place(pieces, slots):
    count = len(pieces)
    shape = pieces[0].shape

    def body(slots_ref, *refs):
        out_ref, held, came, left = refs[count:]
        into = [pltpu.make_async_copy(refs[k], held.at[k], came.at[k]) for k in range(count)]
        out_of = [
            pltpu.make_async_copy(held.at[k], out_ref.at[slots_ref[k]], left.at[k])
            for k in range(count)
        ]
        for copy in into:
            copy.start()
        for first, second in zip(into, out_of):
            first.wait()
            second.start()
        for copy in out_of:
            copy.wait()

    return pl.pallas_call(
        body,
        out_shape=jax.ShapeDtypeStruct((count,) + shape, pieces[0].dtype),
        grid_spec=pltpu.PrefetchScalarGridSpec(
            num_scalar_prefetch=1,
            grid=(1,),
            in_specs=[pl.BlockSpec(memory_space=pl.ANY)] * count,
            out_specs=pl.BlockSpec(memory_space=pl.ANY),
            scratch_shapes=[
                pltpu.VMEM((count,) + shape, pieces[0].dtype),
                pltpu.SemaphoreType.DMA((count,)),
                pltpu.SemaphoreType.DMA((count,)),
            ],
        ),
        compiler_params=pltpu.CompilerParams(vmem_limit_bytes=VMEM_BYTES),
        cost_estimate=pl.CostEstimate(
            flops=0, bytes_accessed=4 * count * pieces[0].size, transcendentals=0
        ),
        name="place",
    )(jnp.stack(slots).astype(jnp.int32), *pieces)


def nn(first, second):
    return lax.dot_general(
        first, second, (((1,), (0,)), ((), ())), preferred_element_type=jnp.float32
    )


def nt(first, second):
    return lax.dot_general(
        first, second, (((1,), (1,)), ((), ())), preferred_element_type=jnp.float32
    )


def tn(first, second):
    return lax.dot_general(
        first, second, (((0,), (0,)), ((), ())), preferred_element_type=jnp.float32
    )


def ring_sum(block_of, axis):
    count = lax.axis_size(axis)
    rank = lax.axis_index(axis)
    moving = None
    for step in range(1, count):
        term = block_of((rank - step) % count)
        moving = low(term if moving is None else wide(moving) + wide(term))
        moving = ring(moving, axis)
    own = wide(block_of(rank))
    return own if moving is None else own + wide(moving)


def attention_forward(queries, keyvals, live, first_key, head_size):
    rows, columns = queries.shape
    heads = columns // head_size
    reach = W + ROWS
    lead = keyvals.shape[0] - rows - W

    def body(info_ref, q_ref, kv_ref, o_ref):
        head, block = pl.program_id(0), pl.program_id(1)
        start = pl.multiple_of(lead + block * ROWS, ROWS)
        keys = kv_ref[pl.ds(start, reach), :head_size]
        vals = kv_ref[pl.ds(start, reach), head_size:]
        scores = nt(q_ref[...], keys)
        row = lax.broadcasted_iota(jnp.int32, scores.shape, 0)
        column = lax.broadcasted_iota(jnp.int32, scores.shape, 1)
        ahead = column - row
        allowed = (ahead > 0) & (ahead <= W) & (column >= info_ref[0] - start)
        scores = jnp.where(allowed, scores, lowest)
        peak = jnp.max(scores, axis=1, keepdims=True)
        shares = jnp.exp(scores - peak)
        total = jnp.sum(shares, axis=1, keepdims=True)
        probs = low(shares * (1.0 / total))
        mixed = nn(probs, vals)
        o_ref[...] = low(mixed * wide(info_ref[1 + head]))

    return pl.pallas_call(
        body,
        out_shape=jax.ShapeDtypeStruct((rows, columns), jnp.bfloat16),
        grid_spec=pltpu.PrefetchScalarGridSpec(
            num_scalar_prefetch=1,
            grid=(heads, rows // ROWS),
            in_specs=[
                pl.BlockSpec((ROWS, head_size), lambda h, i, info: (i, h)),
                pl.BlockSpec(keyvals.shape, lambda h, i, info: (0, 0)),
            ],
            out_specs=pl.BlockSpec((ROWS, head_size), lambda h, i, info: (i, h)),
        ),
        compiler_params=pltpu.CompilerParams(vmem_limit_bytes=VMEM_BYTES),
        cost_estimate=pl.CostEstimate(
            flops=4 * heads * rows * reach * head_size,
            bytes_accessed=4 * rows * columns + 2 * keyvals.size,
            transcendentals=heads * rows * reach,
        ),
        name="attention_forward",
    )(jnp.concatenate([first_key[None], live]).astype(jnp.int32), queries, keyvals)


def attention_backward(queries, keyvals, d_attended, first_key, head_size):
    rows, columns = queries.shape
    heads = columns // head_size
    reach = W + ROWS
    span = keyvals.shape[0]
    lead = span - rows - W

    def body(info_ref, q_ref, kv_ref, do_ref, dq_ref, dkv_ref, sums):
        head, block = pl.program_id(0), pl.program_id(1)

        @pl.when((head == 0) & (block == 0))
        def _():
            sums[...] = jnp.zeros_like(sums)

        start = pl.multiple_of(lead + block * ROWS, ROWS)
        keys = kv_ref[pl.ds(start, reach), :head_size]
        vals = kv_ref[pl.ds(start, reach), head_size:]
        query = q_ref[...]
        d_out = do_ref[...]
        scores = nt(keys, query)
        column = lax.broadcasted_iota(jnp.int32, scores.shape, 0)
        row = lax.broadcasted_iota(jnp.int32, scores.shape, 1)
        ahead = column - row
        allowed = (ahead > 0) & (ahead <= W) & (column >= info_ref[0] - start)
        scores = jnp.where(allowed, scores, lowest)
        peak = jnp.max(scores, axis=0, keepdims=True)
        shares = jnp.exp(scores - peak)
        total = jnp.sum(shares, axis=0, keepdims=True)
        probs = shares * (1.0 / total)
        d_probs = nt(vals, d_out)
        inner = jnp.sum(probs * d_probs, axis=0, keepdims=True)
        d_scores = low(probs * (d_probs - inner))
        dq_ref[...] = tn(d_scores, keys)
        sums[pl.ds(start, reach), :head_size] += nn(d_scores, query)
        sums[pl.ds(start, reach), head_size:] += nn(low(probs), d_out)

        @pl.when((head == heads - 1) & (block == rows // ROWS - 1))
        def _():
            dkv_ref[...] = low(sums[...])

    return pl.pallas_call(
        body,
        out_shape=(
            jax.ShapeDtypeStruct((rows, columns), jnp.float32),
            jax.ShapeDtypeStruct(keyvals.shape, jnp.bfloat16),
        ),
        grid_spec=pltpu.PrefetchScalarGridSpec(
            num_scalar_prefetch=1,
            grid=(heads, rows // ROWS),
            in_specs=[
                pl.BlockSpec((ROWS, head_size), lambda h, i, info: (i, h)),
                pl.BlockSpec(keyvals.shape, lambda h, i, info: (0, 0)),
                pl.BlockSpec((ROWS, head_size), lambda h, i, info: (i, h)),
            ],
            out_specs=(
                pl.BlockSpec((ROWS, head_size), lambda h, i, info: (i, h)),
                pl.BlockSpec(keyvals.shape, lambda h, i, info: (0, 0)),
            ),
            scratch_shapes=[pltpu.VMEM(keyvals.shape, jnp.float32)],
        ),
        compiler_params=pltpu.CompilerParams(vmem_limit_bytes=VMEM_BYTES),
        cost_estimate=pl.CostEstimate(
            flops=10 * heads * rows * reach * head_size,
            bytes_accessed=8 * rows * columns + 4 * keyvals.size,
            transcendentals=heads * rows * reach,
        ),
        name="attention_backward",
    )(first_key[None].astype(jnp.int32), queries, keyvals, d_attended)


def gelu_tanh(values):
    return jax.nn.gelu(values, approximate=True)


def local(
    hidden,
    lengths,
    teacher,
    attn_gain,
    query_weight,
    kv_weight,
    out_weight,
    mlp_gain,
    gate_weight,
    up_weight,
    down_weight,
):
    tp_count = lax.axis_size("tp")
    ctx_count = lax.axis_size("ctx")
    fsdp_count = lax.axis_size("fsdp")
    tp_rank = lax.axis_index("tp")
    ctx_rank = lax.axis_index("ctx")
    fsdp_rank = lax.axis_index("fsdp")
    y_rank, core_rank = tp_rank // 2, tp_rank % 2
    hi_rank, lo_rank = ctx_rank // 2, ctx_rank % 2
    seq_count, rows, width = hidden.shape
    assert seq_count == 1 and tp_count == 4 and ctx_count == 4
    part_rows = rows // tp_count
    head_size = kv_weight.shape[1] // 2
    head_count = query_weight.shape[1] // head_size
    slot_count = -(-head_count // tp_count)
    slot_width = slot_count * head_size
    fuller = head_count - (slot_count - 1) * tp_count
    kv_width = 2 * head_size // tp_count

    def first_head_of(rank):
        return rank * (slot_count - 1) + jnp.minimum(rank, fuller)

    def slot_base_of(rank):
        return jnp.minimum(first_head_of(rank), head_count - slot_count)

    slot_heads = slot_base_of(tp_rank) + jnp.arange(slot_count)
    first_head = first_head_of(tp_rank)
    held_heads = slot_count - 1 + (tp_rank < fuller).astype(jnp.int32)
    live = ((slot_heads >= first_head) & (slot_heads < first_head + held_heads)).astype(jnp.int32)

    def over_tp(columns_of):
        blocks = [columns_of(tp_rank)]
        for bit in range(1, tp_count):
            blocks.append(flip(columns_of(tp_rank ^ bit), "tp", bit))
        return jnp.concatenate(swapped(blocks, tp_rank), axis=0)

    def over_fsdp(block):
        blocks = [block]
        for _ in range(1, fsdp_count):
            blocks.append(ring(blocks[-1], "fsdp"))
        return blocks

    def placed(by_ctx):
        pieces, slots = [], []
        for step, blocks in enumerate(by_ctx):
            for turn_at, block in enumerate(blocks):
                pieces.append(block)
                slots.append(
                    (fsdp_rank - turn_at) % fsdp_count * ctx_count
                    + (ctx_rank - step) % ctx_count
                )
        return place(pieces, slots).reshape(width, pieces[0].shape[1])

    def head_columns(weight):
        return lambda rank: lax.dynamic_slice_in_dim(
            weight, slot_base_of(rank) * head_size, slot_width, 1
        )

    unit_count = gate_weight.shape[1]
    half = -(-unit_count // 256) * 128
    rest = unit_count - half

    def near_halves(block):
        near, far = block[:, :half], jnp.pad(block[:, half:], ((0, 0), (0, half - rest)))
        mine = jnp.where(lo_rank == 0, near, far)
        theirs = jnp.where(lo_rank == 0, far, near)
        return mine, theirs

    def near_pair(halves):
        mine, theirs = halves
        return jnp.stack(swapped([mine, flip(theirs, "ctx", 1)], lo_rank))

    def quarters(pair):
        return jnp.split(pair.reshape(-1, half), 4)

    def far(pieces):
        if len(pieces) == 1:
            return [flip(pieces[0], "ctx", 2)]
        return jnp.split(flip(jnp.concatenate(pieces, axis=0), "ctx", 2), len(pieces))

    def mlp_placed(own, other):
        pieces, slots = [], []
        for far_bit, blocks in enumerate((own, other)):
            for turn_at, block in enumerate(blocks):
                pieces.append(block.reshape(-1, half))
                slots.append((fsdp_rank - turn_at) % fsdp_count * 2 + (hi_rank ^ far_bit))
        return place(pieces, slots).reshape(width, half)

    inputs_low = hidden[0]
    inputs = wide(inputs_low)
    inputs_part_low = lax.dynamic_slice_in_dim(inputs_low, tp_rank * part_rows, part_rows, 0)
    inputs_part = wide(inputs_part_low)
    scale_one = lax.rsqrt(jnp.mean(inputs * inputs, axis=-1, keepdims=True) + epsilon)
    positions = ctx_rank * rows + jnp.arange(rows)
    quarter = head_size // 4
    frequency = 10000.0 ** (-(jnp.arange(quarter).astype(jnp.float32) * 4.0 / head_size))
    angle = wide(positions)[:, None] * frequency[None, :]
    cosine, sine = jnp.cos(angle), jnp.sin(angle)

    def turn(values, cosine, sine):
        first, second = values[..., :quarter], values[..., quarter : 2 * quarter]
        return jnp.concatenate(
            [
                first * cosine - second * sine,
                second * cosine + first * sine,
                values[..., 2 * quarter :],
            ],
            axis=-1,
        )

    turning = tp_rank == 0
    kv_cosine, kv_sine = jnp.where(turning, cosine, 1.0), jnp.where(turning, sine, 0.0)
    query_scale = head_size ** (-0.5)
    reach_back = min((W - 2) // rows + 1, ctx_count - 1)
    first_key = (reach_back - jnp.minimum(ctx_rank, reach_back)) * rows

    at = Steps()
    gains = jnp.pad(jnp.stack([attn_gain, mlp_gain], axis=1), ((0, 0), (0, 126)))

    def qkv_columns(rank):
        kv = lax.dynamic_slice_in_dim(kv_weight, rank * kv_width, kv_width, 1)
        return jnp.concatenate([head_columns(query_weight)(rank), kv, gains], axis=1)

    def to_tp(columns_of):
        return [columns_of(tp_rank ^ bit) for bit in range(tp_count)]

    def flip_tp(blocks):
        return blocks[:1] + [flip(blocks[bit], "tp", bit) for bit in range(1, tp_count)]

    def from_tp(blocks):
        return jnp.concatenate(swapped(blocks, tp_rank), axis=0)

    def paired(mine, got):
        return jnp.stack(swapped([mine, got], lo_rank))

    at.qkv = to_tp(qkv_columns)
    at.gate_mine, at.gate_sent = near_halves(gate_weight)
    at.out = to_tp(head_columns(out_weight))
    at.up_mine, at.up_sent = near_halves(up_weight)
    at.down_mine, at.down_sent = near_halves(down_weight.T)
    at.next()
    at.qkv = flip_tp(at.qkv)
    at.gate_got = flip(at.gate_sent, "ctx", 1)
    at.next()
    at.qkv_0 = from_tp(at.drop("qkv")[0])
    at.gate_pair = paired(*at.drop("gate_mine", "gate_got"))
    at.next()
    at.qkv_x = [over_fsdp(at.qkv_0)]
    at.qkv_1 = ring(at.qkv_0, "ctx")
    at.next()
    at.qkv_x.append(over_fsdp(at.qkv_1))
    at.qkv_2 = ring(at.qkv_1, "ctx")
    at.next()
    at.qkv_x.append(over_fsdp(at.qkv_2))
    at.qkv_3 = ring(at.qkv_2, "ctx")
    at.out = flip_tp(at.out)
    at.next()
    at.out_0 = from_tp(at.drop("out")[0])
    at.drop("qkv_0", "qkv_1", "qkv_2", "gate_sent")
    at.next()
    at.qkv_x.append(over_fsdp(at.qkv_3))
    at.out_1 = ring(at.out_0, "ctx")
    at.next()

    qkv_part = placed(at.drop("qkv_x")[0])
    gain_attn = wide(qkv_part[:, slot_width + kv_width])
    gain_mlp = wide(qkv_part[:, slot_width + kv_width + 1])
    at.normed = low(inputs * scale_one * gain_attn)
    at.qkv_raw = nn(at.normed, qkv_part)
    at.gate_a = over_fsdp(at.gate_pair[0])
    at.out_2 = ring(at.out_1, "ctx")
    at.up_got = flip(at.up_sent, "ctx", 1)
    at.next()
    (qkv_raw,) = at.drop("qkv_raw")
    kv_raw = qkv_raw[:, slot_width : slot_width + kv_width]
    at.kv_own = low(turn(kv_raw, kv_cosine, kv_sine))
    query_raw = qkv_raw[:, :slot_width].reshape(rows, slot_count, head_size)
    queries = low(turn(query_raw, cosine[:, None, :], sine[:, None, :]) * query_scale)
    at.queries = queries.reshape(rows, slot_width)
    at.gate_b = over_fsdp(at.gate_pair[1])
    at.out_3 = ring(at.out_2, "ctx")
    at.next()
    normed = at.normed
    at.up_pair = paired(*at.drop("up_mine", "up_got"))
    at.out_near = jnp.stack([at.out_0, at.out_1, at.out_2, at.out_3])
    at.next()
    out_x = over_fsdp(at.out_near)
    at.chunks = [shifted(at.kv_own, "ctx", by) for by in range(reach_back, 0, -1)]
    at.next()
    at.kv_column = jnp.concatenate(at.drop("chunks")[0] + [at.kv_own], axis=0)
    at.gate_far = jnp.concatenate(quarters(at.gate_pair)[:2], axis=0)
    at.drop("out_0", "out_1", "out_2", "kv_own", "qkv_3")
    at.next()
    at.kv_over_y = flip(at.kv_column, "tp", 2)
    at.down_got = flip(at.down_sent, "ctx", 1)
    at.far_2 = flip(at.gate_far, "ctx", 2)
    at.out_x = out_x
    at.next()
    at.kv_pair = jnp.stack(at.drop("kv_column", "kv_over_y"))
    at.down_pair = paired(*at.drop("down_mine", "down_got"))
    at.next()
    at.kv_other = flip(at.kv_pair, "tp", 1)
    at.far_1 = far(quarters(at.gate_pair)[2:3])
    (out_x,) = at.drop("out_x")
    at.out_part = placed([[block[i] for block in out_x] for i in range(ctx_count)])
    at.next()
    kv_pair, kv_other = at.drop("kv_pair", "kv_other")
    at.keyvals = jnp.concatenate(
        swapped([kv_pair[0], kv_other[0], kv_pair[1], kv_other[1]], tp_rank), axis=1
    )
    at.mixed_far = jnp.concatenate(quarters(at.gate_pair)[3:] + quarters(at.up_pair)[:2], axis=0)
    at.drop("up_sent", "down_sent", "gate_far", "out_near")
    at.next()

    queries, keyvals = at.queries, at.keyvals
    at.attended = attention_forward(queries, keyvals, live, first_key, head_size)
    blocks = low(nt(at.attended, at.out_part)).reshape(2, 2, part_rows, -1)
    at.kept, at.sent = take(blocks, core_rank, 1), take(blocks, 1 - core_rank, 1)
    at.up_x = over_fsdp(at.up_pair)
    at.far_3 = flip(at.mixed_far, "ctx", 2)
    at.next()

    out_part = at.out_part
    quarter_rows = at.far_1[0].shape[0]
    at.got = flip(at.sent, "tp", 1)
    at.gate_other = jnp.concatenate(
        [at.far_2] + at.far_1 + [at.far_3[:quarter_rows]], axis=0
    ).reshape(at.gate_pair.shape)
    at.up_far = jnp.concatenate(quarters(at.up_pair)[2:], axis=0)
    at.next()
    summed = wide(at.kept) + wide(at.got)
    at.kept, at.sent = take(summed, y_rank), low(take(summed, 1 - y_rank))
    at.next()
    at.got = flip(at.sent, "tp", 2)
    at.gate_z = over_fsdp(at.gate_other)
    at.far_4 = flip(at.up_far, "ctx", 2)
    at.next()

    middle = part_rows // 2

    def gather_sides():
        at.over_y, at.over_z = flip(at.part, "tp", 2), flip(at.part, "ctx", 1)
        at.core_own = flip(at.part, "tp", 1)

    def between_sides_and_corners():
        at.to_z, at.to_y = at.over_y[:middle], at.over_z[middle:]
        at.sides = jnp.concatenate([at.over_y, at.over_z], axis=0)

    def gather_corners():
        at.corner_top = flip(at.to_z, "ctx", 1)
        at.corner_end = flip(at.to_y, "tp", 2)
        at.core_sides = flip(at.sides, "tp", 1)

    def between_corners_and_core():
        at.corner = jnp.concatenate(at.drop("corner_top", "corner_end"), axis=0)
        at.drop("to_z", "to_y", "over_y", "over_z")

    def gathered():
        return jnp.concatenate(
            at.drop("part", "sides", "corner", "core_own", "core_sides", "core_corner"), axis=0
        )

    def before_sum(partial):
        mine, theirs = partial.reshape(2, 4, part_rows, -1)
        at.mine, at.mine_corner = mine[:3], mine[3]
        at.theirs, at.theirs_corner = theirs[:3], theirs[3]

    def between_core_and_corners():
        corner = wide(at.drop("mine_corner")[0]) + wide(at.drop("got_corner")[0])
        at.to_z, at.to_y = low(corner[:middle]), low(corner[middle:])

    def sum_corners():
        at.corner_top = flip(at.to_z, "ctx", 1)
        at.corner_end = flip(at.to_y, "tp", 2)

    def between_corners_and_sides():
        mine, got, top, end = at.drop("mine", "got", "corner_top", "corner_end")
        own, over_y, over_z = wide(mine) + wide(got)
        at.over_y = low(jnp.concatenate([over_y[:middle] + wide(top), over_y[middle:]], axis=0))
        at.over_z = low(jnp.concatenate([over_z[:middle], over_z[middle:] + wide(end)], axis=0))
        at.part = own
        at.drop("theirs", "theirs_corner", "to_z", "to_y")

    def sum_sides():
        at.got_y, at.got_z = flip(at.over_y, "tp", 2), flip(at.over_z, "ctx", 1)

    def summed():
        own, got_y, got_z = at.drop("part", "got_y", "got_z")
        at.drop("over_y", "over_z")
        return own + wide(got_y) + wide(got_z)

    residual = inputs_part + (at.kept + wide(at.got))
    at.drop("kept", "got", "sent")
    scale_two = lax.rsqrt(jnp.mean(residual * residual, axis=-1, keepdims=True) + epsilon)
    at.residual = residual
    at.part = low(residual * scale_two * gain_mlp)
    at.down_quarters = quarters(at.down_pair)
    at.next()
    residual = at.residual
    gather_sides()
    at.down_x = over_fsdp(at.down_pair)
    at.far_5 = flip(at.down_quarters[0], "ctx", 2)
    at.up_a, at.up_b = at.far_3[quarter_rows:], at.far_4
    gate_a, gate_b, gate_z = at.drop("gate_a", "gate_b", "gate_z")
    at.gate_full = mlp_placed([jnp.stack(pair) for pair in zip(gate_a, gate_b)], gate_z)
    at.next()
    between_sides_and_corners()
    at.next()
    gather_corners()
    at.up_a = over_fsdp(at.up_a)
    at.far_6 = flip(at.down_quarters[1], "ctx", 2)
    at.next()
    between_corners_and_core()
    at.next()
    at.core_corner = flip(at.corner, "tp", 1)
    at.next()
    at.normed_two = gathered()
    at.gate_proj = nn(at.normed_two, at.gate_full)
    at.up_b = over_fsdp(at.up_b)
    at.far_7 = flip(at.down_quarters[2], "ctx", 2)
    at.down_a = jnp.concatenate([at.far_5, at.far_6], axis=0)
    at.next()
    gate_full = at.gate_full
    up_a, up_b = at.drop("up_a", "up_b")
    up_z = [jnp.stack(pair) for pair in zip(up_a, up_b)]
    up_full = mlp_placed(at.drop("up_x")[0], up_z)
    at.up_proj = nn(at.normed_two, up_full)
    at.down_a = over_fsdp(at.down_a)
    at.far_8 = flip(at.down_quarters[3], "ctx", 2)
    at.next()
    at.down_b = jnp.concatenate([at.far_7, at.far_8], axis=0)
    at.next()
    gate_proj, up_proj = at.gate_proj, at.up_proj
    at.hidden_act = low(gelu_tanh(gate_proj) * up_proj)
    at.down_b = over_fsdp(at.down_b)
    at.next()
    at.drop("far_1", "far_2", "far_3", "far_4", "far_5", "far_6", "far_7", "gate_pair", "up_pair")
    at.drop("far_8", "gate_other", "up_far", "down_quarters", "mixed_far")
    at.drop("down_pair")
    down_x, down_a, down_b = at.drop("down_x", "down_a", "down_b")
    down_z = [jnp.stack(pair) for pair in zip(down_a, down_b)]
    down_full = mlp_placed(down_x, down_z)
    before_sum(low(nt(at.hidden_act, down_full)))
    at.next()
    at.got_corner = flip(at.theirs_corner, "tp", 1)
    at.next()
    between_core_and_corners()
    at.next()
    sum_corners()
    at.got = flip(at.theirs, "tp", 1)
    at.next()
    between_corners_and_sides()
    at.next()
    sum_sides()
    gate_proj, up_proj = at.drop("gate_proj", "up_proj")
    at.activated, gelu_back = jax.vjp(gelu_tanh, gate_proj)
    at.slope = gelu_back(up_proj)[0]
    at.next()
    at.ffn_parts = at.drop("part", "got_y", "got_z")
    at.drop("over_y", "over_z")
    my_length = lengths[fsdp_rank]
    part_positions = ctx_rank * rows + tp_rank * part_rows + jnp.arange(part_rows)
    valid = wide(part_positions < my_length)[:, None]
    count = wide(jnp.sum(lengths))
    d_scale = lengths.shape[0] * ctx_count * rows / count

    def outputs_of(residual, ffn_parts):
        own, got_y, got_z = ffn_parts
        output = (residual + (own + wide(got_y) + wide(got_z))) * valid
        return output, output - wide(teacher[0])

    at.part = low(valid * outputs_of(residual, at.ffn_parts)[1] * d_scale)
    at.next()
    output, mismatch = outputs_of(at.residual, at.drop("ffn_parts")[0])
    loss_part = jnp.sum(valid * mismatch * mismatch)
    at.d_output = valid * mismatch * d_scale
    at.output_low = low(output)
    gather_sides()
    at.next()
    between_sides_and_corners()
    at.next()
    gather_corners()
    at.next()
    between_corners_and_core()
    at.next()
    at.core_corner = flip(at.corner, "tp", 1)
    at.next()

    def terms(blocks_of, axis):
        count, rank = lax.axis_size(axis), lax.axis_index(axis)
        return [blocks_of((rank - step) % count) for step in range(1, count + 1)]

    def around(sent, axis):
        moving = ring(sent[0], axis)
        for term in sent[1:-1]:
            moving = ring(low(wide(moving) + wide(term)), axis)
        return moving

    def with_own(sent, arrived):
        return wide(sent[-1]) + wide(arrived)

    def far_and_own(grad):
        blocks = grad.reshape(fsdp_count, 2, 2, -1, half)
        return [
            terms(lambda owner: take(take(blocks, owner), high), "fsdp")
            for high in (1 - hi_rank, hi_rank)
        ]

    def blocks_of(grad):
        blocks = grad.reshape(fsdp_count, 2, 2, -1, half)
        return [
            terms(lambda owner: take(take(blocks, owner), high)[lo], "fsdp")
            for high in (1 - hi_rank, hi_rank)
            for lo in range(2)
        ]

    def near_split(mine):
        return wide(take(mine, lo_rank)), low(take(mine, 1 - lo_rank))

    def near_joined(kept, got):
        near, rest_of = swapped([kept, wide(got)], lo_rank)
        return jnp.concatenate([near, rest_of[:, :rest]], axis=1)

    at.d_ffn = gathered()
    at.down_terms = blocks_of(low(tn(at.d_ffn, at.hidden_act)))
    at.next()
    at.down_x = [around(at.down_terms[0], "fsdp")]
    d_hidden = nn(at.d_ffn, down_full)
    at.d_gate = low(d_hidden * at.slope)
    at.d_up = low(d_hidden * at.activated)
    at.next()
    at.drop("d_ffn", "hidden_act", "slope", "activated")
    at.down_x += [around(at.down_terms[1], "fsdp")]
    at.gate_terms = blocks_of(low(tn(at.normed_two, at.d_gate)))
    at.next()
    at.down_far = [low(with_own(at.down_terms[i], at.down_x[i])) for i in range(2)]
    at.next()
    at.down_x += [around(at.down_terms[2], "fsdp"), around(at.down_terms[3], "fsdp")]
    at.down_got_0 = flip(at.down_far[0], "ctx", 2)
    before_sum(low(nt(at.d_gate, gate_full) + nt(at.d_up, up_full)))
    at.next()
    at.got_corner = flip(at.theirs_corner, "tp", 1)
    at.next()
    between_core_and_corners()
    at.drop("d_gate")
    at.down_rest = jnp.split(at.down_far[1], 2)
    at.next()
    sum_corners()
    at.got = flip(at.theirs, "tp", 1)
    at.gate_got = [around(at.gate_terms[0], "fsdp")]
    at.down_got_1 = flip(at.down_rest[0], "ctx", 2)
    at.next()
    between_corners_and_sides()
    at.next()
    sum_sides()
    down_terms, down_x = at.drop("down_terms", "down_x")
    at.down_own = jnp.stack([low(with_own(down_terms[i], down_x[i])) for i in (2, 3)])
    at.gate_got += [around(at.gate_terms[1], "fsdp"), around(at.gate_terms[2], "fsdp")]
    at.down_got_2 = flip(at.down_rest[1], "ctx", 2)
    up_blocks = low(tn(at.normed_two, at.d_up)).reshape(fsdp_count, 2, 2, -1, half)
    at.up_first = terms(lambda owner: take(take(up_blocks, owner), 1 - hi_rank)[0], "fsdp")
    at.up_others = terms(
        lambda owner: jnp.concatenate(
            [take(take(up_blocks, owner), 1 - hi_rank)[1:], take(take(up_blocks, owner), hi_rank)]
        ),
        "fsdp",
    )
    at.next()
    at.drop("normed_two", "d_up", "down_far", "down_rest")
    at.gate_far = [low(with_own(at.gate_terms[i], at.gate_got[i])) for i in range(2)]
    d_normed_two = summed()
    scaled = gain_mlp * d_normed_two
    inner_two = jnp.mean(scaled * residual, axis=-1, keepdims=True)
    at.d_residual = at.d_output + scale_two * scaled - residual * scale_two**3 * inner_two
    at.gain_mlp_sums = jnp.sum(d_normed_two * residual * scale_two, axis=0)
    at.part = low(at.d_residual)
    at.next()
    at.over_y = flip(at.part, "tp", 2)
    got_0, got_1, got_2 = at.drop("down_got_0", "down_got_1", "down_got_2")
    down_got = jnp.stack([got_0, jnp.concatenate([got_1, got_2], axis=0)])
    at.down_kept, at.down_sent = near_split(wide(at.drop("down_own")[0]) + wide(down_got))
    at.gate_got += [around(at.gate_terms[3], "fsdp")]
    at.up_first_got = around(at.up_first, "fsdp")
    at.gate_far_0 = flip(at.gate_far[0], "ctx", 2)
    at.next()
    at.pair = jnp.stack(at.drop("part", "over_y"))
    at.next()
    at.other = flip(at.pair, "tp", 1)
    at.up_far = jnp.split(low(with_own(*at.drop("up_first", "up_first_got"))), 2)
    gate_terms, gate_got = at.drop("gate_terms", "gate_got")
    at.gate_own = jnp.stack([low(with_own(gate_terms[i], gate_got[i])) for i in (2, 3)])
    at.next()
    pair, other = at.drop("pair", "other")
    d_attn = swapped([pair[0], other[0], pair[1], other[1]], tp_rank)
    at.d_attn = jnp.concatenate(d_attn, axis=0)
    at.next()
    at.down_got = flip(at.down_sent, "ctx", 1)
    live_columns = jnp.repeat(live, head_size).astype(jnp.float32)
    d_attended = low(nn(at.d_attn, out_part) * live_columns)
    out_grad = low(tn(at.d_attn, at.attended))

    own_rows = attn_gain.shape[0]

    def split_sums(columns):
        rounded = low(columns)
        return jnp.concatenate([rounded, low(columns - wide(rounded))], axis=-1)

    def joined_sums(columns):
        return columns[..., :64] + columns[..., 64:]

    def to_tp_back(mine):
        blocks = low(mine).reshape(tp_count, own_rows, -1)
        return [take(blocks, tp_rank ^ bit) for bit in range(tp_count)]

    def by_rows(grad):
        return grad.reshape(fsdp_count, ctx_count, tp_count * own_rows, -1)

    def halves_of(grad):
        grad = by_rows(grad)
        turned = [take(grad, (ctx_rank - by) % ctx_count, 1) for by in range(1, ctx_count + 1)]
        pairs = [jnp.stack(turned[:2], axis=1), jnp.stack(turned[2:], axis=1)]
        return [terms(lambda owner: take(pair, owner), "fsdp") for pair in pairs]

    at.out_terms = halves_of(out_grad)
    at.d_queries, at.d_keyvals = attention_backward(
        queries, keyvals, d_attended, first_key, head_size
    )
    at.up_others_got = around(at.up_others, "fsdp")
    at.gate_far_1 = flip(at.gate_far[1], "ctx", 2)
    at.up_far_0 = flip(at.up_far[0], "ctx", 2)
    at.next()
    at.drop("attended", "d_attn", "down_sent")
    kv_blocks = jnp.stack(jnp.split(at.d_keyvals, tp_count, axis=1)).reshape(2, 2, -1, kv_width)
    at.kv_kept, at.kv_sent = take(kv_blocks, core_rank, 1), take(kv_blocks, 1 - core_rank, 1)
    at.drop("d_keyvals")
    at.next()
    at.kv_got = flip(at.kv_sent, "tp", 1)
    up_others, up_others_got = at.drop("up_others", "up_others_got")
    up_rest = jnp.split(low(wide(up_others[-1][0]) + wide(up_others_got[0])), 2)
    at.up_mixed = jnp.concatenate([at.up_far[1], up_rest[0]], axis=0)
    at.up_last = up_rest[1]
    at.up_own, at.up_own_got = up_others[-1][1:], up_others_got[1:]
    gate_far_got = jnp.stack(at.drop("gate_far_0", "gate_far_1"))
    at.gate_kept, at.gate_sent = near_split(wide(at.drop("gate_own")[0]) + wide(gate_far_got))
    at.drop("gate_far")
    at.next()
    kv_sum = wide(at.kv_kept) + wide(at.kv_got)
    at.kv_kept, at.kv_sent = take(kv_sum, y_rank), low(take(kv_sum, 1 - y_rank))
    at.next()
    at.kv_got = flip(at.kv_sent, "tp", 2)
    at.up_far_1 = flip(at.up_mixed, "ctx", 2)
    at.gate_near = flip(at.gate_sent, "ctx", 1)
    at.up_own = low(wide(at.up_own) + wide(at.drop("up_own_got")[0]))
    at.out_got = [around(at.out_terms[0], "fsdp")]
    d_query_raw = turn(
        at.d_queries.reshape(rows, slot_count, head_size) * query_scale,
        cosine[:, None, :],
        -sine[:, None, :],
    )
    at.d_query_low = low(d_query_raw.reshape(rows, slot_width))
    at.query_terms = halves_of(low(tn(normed, at.d_query_low)))
    at.next()
    at.drop("d_queries", "kv_sent")
    kv_sum = (at.drop("kv_kept")[0] + wide(at.drop("kv_got")[0])).reshape(reach_back + 1, rows, -1)
    at.kv_low = [low(kv_sum[reach_back - by]) for by in range(1, reach_back + 1)]
    at.d_kv = kv_sum[reach_back]
    at.out_1 = low(with_own(at.out_terms[0], at.out_got[0]))
    at.next()
    at.kv_got = [shifted(at.kv_low[by - 1], "ctx", -by) for by in range(1, reach_back + 1)]
    at.out_got += [around(at.out_terms[1], "fsdp")]
    at.out_z = ring(at.out_1[0], "ctx")
    at.next()
    d_kv = at.d_kv
    for got in at.drop("kv_got")[0]:
        d_kv = d_kv + wide(got)
    d_kv_low = low(turn(d_kv, kv_cosine, -kv_sine))
    at.d_qkv = jnp.concatenate(
        [at.d_query_low, jnp.pad(d_kv_low, ((0, 0), (0, kv_width)))], axis=1
    )
    at.out_z = low(wide(at.out_z) + wide(at.out_1[1]))
    at.next()
    at.query_got = [around(at.query_terms[0], "fsdp")]
    at.up_far_2 = flip(at.up_last, "ctx", 2)
    at.out_z = ring(at.out_z, "ctx")
    at.partial = low(nt(at.d_qkv, qkv_part))
    at.next()
    partial = at.partial
    blocks = partial.reshape(2, 2, part_rows, -1)
    at.kept, at.sent = take(blocks, core_rank, 1), take(blocks, 1 - core_rank, 1)
    at.next()
    at.drop("d_query_low", "kv_low", "d_kv", "gate_sent")
    at.query_1 = low(with_own(at.query_terms[0], at.query_got[0]))
    at.out_2 = with_own(at.out_terms[1], at.out_got[1])
    at.out_z = low(wide(at.out_z) + at.out_2[0])
    at.got = flip(at.sent, "tp", 1)
    at.next()
    summed_rows = wide(at.kept) + wide(at.got)
    at.kept, at.sent = take(summed_rows, y_rank), low(take(summed_rows, 1 - y_rank))
    at.next()
    at.got = flip(at.sent, "tp", 2)
    gain_attn_sums = jnp.sum(wide(at.partial) * inputs * scale_one, axis=0)
    sums = [gain_attn_sums, at.gain_mlp_sums, jnp.full(gain_attn_sums.shape, loss_part)]
    columns = jnp.pad(jnp.stack(sums, axis=1), ((0, 0), (0, 61)))
    kv_grad = jnp.concatenate([low(tn(normed, at.d_qkv[:, slot_width : slot_width + kv_width])), split_sums(columns)], axis=1)
    at.kv_terms = terms(lambda owner: take(by_rows(kv_grad), owner), "fsdp")
    at.query_got += [around(at.query_terms[1], "fsdp")]
    at.query_z = ring(at.query_1[0], "ctx")
    at.out_z = ring(at.out_z, "ctx")
    at.next()
    at.query_z = low(wide(at.query_z) + wide(at.query_1[1]))
    at.next()
    at.query_2 = with_own(at.query_terms[1], at.query_got[1])
    at.d_normed = at.kept + wide(at.got)
    got = at.drop("up_far_0", "up_far_1", "up_far_2")
    up_far_got = jnp.concatenate(got, axis=0).reshape(2, -1, half)
    at.up_kept, at.up_sent = near_split(wide(at.up_own) + wide(up_far_got))
    at.drop("partial", "d_qkv")
    at.drop("query_1", "kept", "sent", "got", "up_far", "up_mixed", "up_last", "up_own")
    at.drop("query_terms", "query_got")
    at.drop("out_terms", "out_got")
    at.query_z = ring(at.query_z, "ctx")
    at.kv_got = around(at.kv_terms, "fsdp")
    at.out_back = to_tp_back(wide(at.out_z) + at.out_2[1])
    at.next()
    at.query_z = low(wide(at.query_z) + at.query_2[0])
    kv_mine = with_own(*at.drop("kv_terms", "kv_got"))
    kv_mine = jnp.concatenate(
        [low(kv_mine[..., :kv_width]), split_sums(joined_sums(kv_mine[..., kv_width:]))], axis=-1
    )
    at.kv_own = take(kv_mine, ctx_rank)
    at.kv_sent = [take(kv_mine, (ctx_rank + by) % ctx_count) for by in range(1, ctx_count)]

    at.next()
    at.drop("out_z", "out_2")
    at.out_back = flip_tp(at.out_back)
    at.query_z = ring(at.query_z, "ctx")
    at.kv_got = [ring(at.kv_sent[by - 1], "ctx", by) for by in range(1, ctx_count)]
    at.next()
    query_mine = low(wide(at.query_z) + at.query_2[1])
    kv_mine = sum([wide(got) for got in at.kv_got], wide(at.kv_own))
    kv_mine = jnp.concatenate(
        [low(kv_mine[:, :kv_width]), split_sums(joined_sums(kv_mine[:, kv_width:]))], axis=1
    )
    at.back = to_tp_back(jnp.concatenate([query_mine, kv_mine], axis=1))
    at.next()
    up_near = flip(at.up_sent, "ctx", 1)
    at.drop("query_z", "query_2", "kv_got", "kv_own", "kv_sent", "up_sent")

    def whole_heads(parts):
        columns = []
        for rank, part in enumerate(parts):
            first = rank * (slot_count - 1) + min(rank, fuller)
            base = min(first, head_count - slot_count)
            held = slot_count - 1 + (1 if rank < fuller else 0)
            start = (first - base) * head_size
            columns.append(wide(part[:, start : start + held * head_size]))
        return jnp.concatenate(columns, axis=1)

    parts = swapped(flip_tp(at.back), tp_rank)
    query_grad = whole_heads([part[:, :slot_width] for part in parts])
    out_grad = whole_heads(swapped(at.out_back, tp_rank))
    kv_parts = [wide(part[:, slot_width:]) for part in parts]
    kv_grad = jnp.concatenate([part[:, :kv_width] for part in kv_parts], axis=1)
    sums = joined_sums(sum(part[:, kv_width:] for part in kv_parts))
    gain_attn_grad, gain_mlp_grad, loss_sum = sums[:, 0], sums[:, 1], sums[0, 2]
    down_grad = near_joined(at.down_kept, at.down_got).T
    gate_grad = near_joined(at.gate_kept, at.gate_near)
    up_grad = near_joined(at.up_kept, up_near)
    loss = loss_sum / (count * width)
    d_normed, d_residual = at.d_normed, at.d_residual
    scale_part = lax.dynamic_slice_in_dim(scale_one, tp_rank * part_rows, part_rows, 0)
    scaled = gain_attn * d_normed
    inner_one = jnp.mean(scaled * inputs_part, axis=-1, keepdims=True)
    input_grad = d_residual + scale_part * scaled - inputs_part * scale_part**3 * inner_one
    return (
        at.output_low[None],
        loss,
        input_grad[None],
        gain_attn_grad,
        query_grad,
        kv_grad,
        out_grad,
        gain_mlp_grad,
        gate_grad,
        up_grad,
        down_grad,
    )


def solution(mesh):
    in_specs = (
        P("fsdp", "ctx", None),
        P(),
        P("fsdp", ("ctx", "tp"), None),
        P(("fsdp", "ctx", "tp")),
        P(("fsdp", "ctx", "tp"), None),
        P(("fsdp", "ctx", "tp"), None),
        P(("fsdp", "ctx", "tp"), None),
        P(("fsdp", "ctx", "tp")),
        P(("fsdp", "ctx"), "tp"),
        P(("fsdp", "ctx"), "tp"),
        P("tp", ("fsdp", "ctx")),
    )
    out_specs = (
        P("fsdp", ("ctx", "tp"), None),
        P(),
        P("fsdp", ("ctx", "tp"), None),
        P(("fsdp", "ctx", "tp")),
        P(("fsdp", "ctx", "tp"), None),
        P(("fsdp", "ctx", "tp"), None),
        P(("fsdp", "ctx", "tp"), None),
        P(("fsdp", "ctx", "tp")),
        P(("fsdp", "ctx"), "tp"),
        P(("fsdp", "ctx"), "tp"),
        P("tp", ("fsdp", "ctx")),
    )
    return jax.shard_map(local, mesh=mesh, in_specs=in_specs, out_specs=out_specs, check_vma=False)
```

```python
import jax
import jax.numpy as jnp
from jax import lax
from jax.experimental import pallas as pl
from jax.experimental.pallas import tpu as pltpu
from jax.sharding import PartitionSpec as P

W = 2048

epsilon = 1e-06
lowest = -1e30
ROWS = 256
VMEM_BYTES = 40 * 1024 * 1024


def flip(array, axis, bit):
    return lax.ppermute(array, axis, [(i, i ^ bit) for i in range(lax.axis_size(axis))])


def ring(array, axis, by=1):
    count = lax.axis_size(axis)
    return lax.ppermute(array, axis, [(i, (i + by) % count) for i in range(count)])


def shifted(array, axis, by):
    count = lax.axis_size(axis)
    pairs = [(i, i + by) for i in range(count) if 0 <= i + by < count]
    return lax.ppermute(array, axis, pairs)


class Steps:
    def next(self):
        self.__dict__.update(lax.optimization_barrier(dict(self.__dict__)))

    def drop(self, *names):
        return [self.__dict__.pop(name) for name in names]


def sync(*trees):
    return lax.optimization_barrier(trees)


def after(array, *others):
    return lax.optimization_barrier((array, others))[0]


def low(values):
    return values.astype(jnp.bfloat16)


def wide(values):
    return values.astype(jnp.float32)


def take(array, index, axis=0):
    return lax.dynamic_index_in_dim(array, index, axis, keepdims=False)


def swapped(blocks, rank):
    if len(blocks) == 2:
        odd = rank == 1
        return [jnp.where(odd, blocks[1], blocks[0]), jnp.where(odd, blocks[0], blocks[1])]
    first = swapped(blocks[:2], rank % 2) + swapped(blocks[2:], rank % 2)
    outer = rank // 2 == 1
    return [jnp.where(outer, first[i ^ 2], first[i]) for i in range(4)]


def place(pieces, slots):
    count = len(pieces)
    shape = pieces[0].shape

    def body(slots_ref, *refs):
        out_ref, held, came, left = refs[count:]
        into = [pltpu.make_async_copy(refs[k], held.at[k], came.at[k]) for k in range(count)]
        out_of = [
            pltpu.make_async_copy(held.at[k], out_ref.at[slots_ref[k]], left.at[k])
            for k in range(count)
        ]
        for copy in into:
            copy.start()
        for first, second in zip(into, out_of):
            first.wait()
            second.start()
        for copy in out_of:
            copy.wait()

    return pl.pallas_call(
        body,
        out_shape=jax.ShapeDtypeStruct((count,) + shape, pieces[0].dtype),
        grid_spec=pltpu.PrefetchScalarGridSpec(
            num_scalar_prefetch=1,
            grid=(1,),
            in_specs=[pl.BlockSpec(memory_space=pl.ANY)] * count,
            out_specs=pl.BlockSpec(memory_space=pl.ANY),
            scratch_shapes=[
                pltpu.VMEM((count,) + shape, pieces[0].dtype),
                pltpu.SemaphoreType.DMA((count,)),
                pltpu.SemaphoreType.DMA((count,)),
            ],
        ),
        compiler_params=pltpu.CompilerParams(vmem_limit_bytes=VMEM_BYTES),
        cost_estimate=pl.CostEstimate(
            flops=0, bytes_accessed=4 * count * pieces[0].size, transcendentals=0
        ),
        name="place",
    )(jnp.stack(slots).astype(jnp.int32), *pieces)


def nn(first, second):
    return lax.dot_general(
        first, second, (((1,), (0,)), ((), ())), preferred_element_type=jnp.float32
    )


def nt(first, second):
    return lax.dot_general(
        first, second, (((1,), (1,)), ((), ())), preferred_element_type=jnp.float32
    )


def tn(first, second):
    return lax.dot_general(
        first, second, (((0,), (0,)), ((), ())), preferred_element_type=jnp.float32
    )


def ring_sum(block_of, axis):
    count = lax.axis_size(axis)
    rank = lax.axis_index(axis)
    moving = None
    for step in range(1, count):
        term = block_of((rank - step) % count)
        moving = low(term if moving is None else wide(moving) + wide(term))
        moving = ring(moving, axis)
    own = wide(block_of(rank))
    return own if moving is None else own + wide(moving)


def attention_forward(queries, keyvals, live, first_key, head_size):
    rows, columns = queries.shape
    heads = columns // head_size
    reach = W + ROWS
    lead = keyvals.shape[0] - rows - W

    def body(info_ref, q_ref, kv_ref, o_ref):
        head, block = pl.program_id(0), pl.program_id(1)
        start = pl.multiple_of(lead + block * ROWS, ROWS)
        keys = kv_ref[pl.ds(start, reach), :head_size]
        vals = kv_ref[pl.ds(start, reach), head_size:]
        scores = nt(q_ref[...], keys)
        row = lax.broadcasted_iota(jnp.int32, scores.shape, 0)
        column = lax.broadcasted_iota(jnp.int32, scores.shape, 1)
        ahead = column - row
        allowed = (ahead > 0) & (ahead <= W) & (column >= info_ref[0] - start)
        scores = jnp.where(allowed, scores, lowest)
        peak = jnp.max(scores, axis=1, keepdims=True)
        shares = jnp.exp(scores - peak)
        total = jnp.sum(shares, axis=1, keepdims=True)
        probs = low(shares * (1.0 / total))
        mixed = nn(probs, vals)
        o_ref[...] = low(mixed * wide(info_ref[1 + head]))

    return pl.pallas_call(
        body,
        out_shape=jax.ShapeDtypeStruct((rows, columns), jnp.bfloat16),
        grid_spec=pltpu.PrefetchScalarGridSpec(
            num_scalar_prefetch=1,
            grid=(heads, rows // ROWS),
            in_specs=[
                pl.BlockSpec((ROWS, head_size), lambda h, i, info: (i, h)),
                pl.BlockSpec(keyvals.shape, lambda h, i, info: (0, 0)),
            ],
            out_specs=pl.BlockSpec((ROWS, head_size), lambda h, i, info: (i, h)),
        ),
        compiler_params=pltpu.CompilerParams(vmem_limit_bytes=VMEM_BYTES),
        cost_estimate=pl.CostEstimate(
            flops=4 * heads * rows * reach * head_size,
            bytes_accessed=4 * rows * columns + 2 * keyvals.size,
            transcendentals=heads * rows * reach,
        ),
        name="attention_forward",
    )(jnp.concatenate([first_key[None], live]).astype(jnp.int32), queries, keyvals)


def attention_backward(queries, keyvals, d_attended, first_key, head_size):
    rows, columns = queries.shape
    heads = columns // head_size
    reach = W + ROWS
    span = keyvals.shape[0]
    lead = span - rows - W

    def body(info_ref, q_ref, kv_ref, do_ref, dq_ref, dkv_ref, sums):
        head, block = pl.program_id(0), pl.program_id(1)

        @pl.when((head == 0) & (block == 0))
        def _():
            sums[...] = jnp.zeros_like(sums)

        start = pl.multiple_of(lead + block * ROWS, ROWS)
        keys = kv_ref[pl.ds(start, reach), :head_size]
        vals = kv_ref[pl.ds(start, reach), head_size:]
        query = q_ref[...]
        d_out = do_ref[...]
        scores = nt(keys, query)
        column = lax.broadcasted_iota(jnp.int32, scores.shape, 0)
        row = lax.broadcasted_iota(jnp.int32, scores.shape, 1)
        ahead = column - row
        allowed = (ahead > 0) & (ahead <= W) & (column >= info_ref[0] - start)
        scores = jnp.where(allowed, scores, lowest)
        peak = jnp.max(scores, axis=0, keepdims=True)
        shares = jnp.exp(scores - peak)
        total = jnp.sum(shares, axis=0, keepdims=True)
        probs = shares * (1.0 / total)
        d_probs = nt(vals, d_out)
        inner = jnp.sum(probs * d_probs, axis=0, keepdims=True)
        d_scores = low(probs * (d_probs - inner))
        dq_ref[...] = tn(d_scores, keys)
        sums[pl.ds(start, reach), :head_size] += nn(d_scores, query)
        sums[pl.ds(start, reach), head_size:] += nn(low(probs), d_out)

        @pl.when((head == heads - 1) & (block == rows // ROWS - 1))
        def _():
            dkv_ref[...] = low(sums[...])

    return pl.pallas_call(
        body,
        out_shape=(
            jax.ShapeDtypeStruct((rows, columns), jnp.float32),
            jax.ShapeDtypeStruct(keyvals.shape, jnp.bfloat16),
        ),
        grid_spec=pltpu.PrefetchScalarGridSpec(
            num_scalar_prefetch=1,
            grid=(heads, rows // ROWS),
            in_specs=[
                pl.BlockSpec((ROWS, head_size), lambda h, i, info: (i, h)),
                pl.BlockSpec(keyvals.shape, lambda h, i, info: (0, 0)),
                pl.BlockSpec((ROWS, head_size), lambda h, i, info: (i, h)),
            ],
            out_specs=(
                pl.BlockSpec((ROWS, head_size), lambda h, i, info: (i, h)),
                pl.BlockSpec(keyvals.shape, lambda h, i, info: (0, 0)),
            ),
            scratch_shapes=[pltpu.VMEM(keyvals.shape, jnp.float32)],
        ),
        compiler_params=pltpu.CompilerParams(vmem_limit_bytes=VMEM_BYTES),
        cost_estimate=pl.CostEstimate(
            flops=10 * heads * rows * reach * head_size,
            bytes_accessed=8 * rows * columns + 4 * keyvals.size,
            transcendentals=heads * rows * reach,
        ),
        name="attention_backward",
    )(first_key[None].astype(jnp.int32), queries, keyvals, d_attended)


def gelu_tanh(values):
    return jax.nn.gelu(values, approximate=True)


def local(
    hidden,
    lengths,
    teacher,
    attn_gain,
    query_weight,
    kv_weight,
    out_weight,
    mlp_gain,
    gate_weight,
    up_weight,
    down_weight,
):
    tp_count = lax.axis_size("tp")
    ctx_count = lax.axis_size("ctx")
    fsdp_count = lax.axis_size("fsdp")
    tp_rank = lax.axis_index("tp")
    ctx_rank = lax.axis_index("ctx")
    fsdp_rank = lax.axis_index("fsdp")
    y_rank, core_rank = tp_rank // 2, tp_rank % 2
    hi_rank, lo_rank = ctx_rank // 2, ctx_rank % 2
    seq_count, rows, width = hidden.shape
    assert seq_count == 1 and tp_count == 4 and ctx_count == 4
    part_rows = rows // tp_count
    head_size = kv_weight.shape[1] // 2
    head_count = query_weight.shape[1] // head_size
    slot_count = -(-head_count // tp_count)
    slot_width = slot_count * head_size
    fuller = head_count - (slot_count - 1) * tp_count
    kv_width = 2 * head_size // tp_count

    def first_head_of(rank):
        return rank * (slot_count - 1) + jnp.minimum(rank, fuller)

    def slot_base_of(rank):
        return jnp.minimum(first_head_of(rank), head_count - slot_count)

    slot_heads = slot_base_of(tp_rank) + jnp.arange(slot_count)
    first_head = first_head_of(tp_rank)
    held_heads = slot_count - 1 + (tp_rank < fuller).astype(jnp.int32)
    live = ((slot_heads >= first_head) & (slot_heads < first_head + held_heads)).astype(jnp.int32)

    def over_tp(columns_of):
        blocks = [columns_of(tp_rank)]
        for bit in range(1, tp_count):
            blocks.append(flip(columns_of(tp_rank ^ bit), "tp", bit))
        return jnp.concatenate(swapped(blocks, tp_rank), axis=0)

    def over_fsdp(block):
        blocks = [block]
        for _ in range(1, fsdp_count):
            blocks.append(ring(blocks[-1], "fsdp"))
        return blocks

    def placed(by_ctx):
        pieces, slots = [], []
        for step, blocks in enumerate(by_ctx):
            for turn_at, block in enumerate(blocks):
                pieces.append(block)
                slots.append(
                    (fsdp_rank - turn_at) % fsdp_count * ctx_count
                    + (ctx_rank - step) % ctx_count
                )
        return place(pieces, slots).reshape(width, pieces[0].shape[1])

    def head_columns(weight):
        return lambda rank: lax.dynamic_slice_in_dim(
            weight, slot_base_of(rank) * head_size, slot_width, 1
        )

    unit_count = gate_weight.shape[1]
    half = -(-unit_count // 256) * 128
    rest = unit_count - half

    def near_halves(block):
        near, far = block[:, :half], jnp.pad(block[:, half:], ((0, 0), (0, half - rest)))
        mine = jnp.where(lo_rank == 0, near, far)
        theirs = jnp.where(lo_rank == 0, far, near)
        return mine, theirs

    def near_pair(halves):
        mine, theirs = halves
        return jnp.stack(swapped([mine, flip(theirs, "ctx", 1)], lo_rank))

    def quarters(pair):
        return jnp.split(pair.reshape(-1, half), 4)

    def far(pieces):
        if len(pieces) == 1:
            return [flip(pieces[0], "ctx", 2)]
        return jnp.split(flip(jnp.concatenate(pieces, axis=0), "ctx", 2), len(pieces))

    def mlp_placed(own, other):
        pieces, slots = [], []
        for far_bit, blocks in enumerate((own, other)):
            for turn_at, block in enumerate(blocks):
                pieces.append(block.reshape(-1, half))
                slots.append((fsdp_rank - turn_at) % fsdp_count * 2 + (hi_rank ^ far_bit))
        return place(pieces, slots).reshape(width, half)

    inputs_low = hidden[0]
    inputs = wide(inputs_low)
    inputs_part_low = lax.dynamic_slice_in_dim(inputs_low, tp_rank * part_rows, part_rows, 0)
    inputs_part = wide(inputs_part_low)
    scale_one = lax.rsqrt(jnp.mean(inputs * inputs, axis=-1, keepdims=True) + epsilon)
    positions = ctx_rank * rows + jnp.arange(rows)
    quarter = head_size // 4
    frequency = 10000.0 ** (-(jnp.arange(quarter).astype(jnp.float32) * 4.0 / head_size))
    angle = wide(positions)[:, None] * frequency[None, :]
    cosine, sine = jnp.cos(angle), jnp.sin(angle)

    def turn(values, cosine, sine):
        first, second = values[..., :quarter], values[..., quarter : 2 * quarter]
        return jnp.concatenate(
            [
                first * cosine - second * sine,
                second * cosine + first * sine,
                values[..., 2 * quarter :],
            ],
            axis=-1,
        )

    turning = tp_rank == 0
    kv_cosine, kv_sine = jnp.where(turning, cosine, 1.0), jnp.where(turning, sine, 0.0)
    query_scale = head_size ** (-0.5)
    reach_back = min((W - 2) // rows + 1, ctx_count - 1)
    first_key = (reach_back - jnp.minimum(ctx_rank, reach_back)) * rows

    at = Steps()
    gains = jnp.pad(jnp.stack([attn_gain, mlp_gain], axis=1), ((0, 0), (0, 126)))

    def qkv_columns(rank):
        kv = lax.dynamic_slice_in_dim(kv_weight, rank * kv_width, kv_width, 1)
        return jnp.concatenate([head_columns(query_weight)(rank), kv, gains], axis=1)

    def to_tp(columns_of):
        return [columns_of(tp_rank ^ bit) for bit in range(tp_count)]

    def flip_tp(blocks):
        return blocks[:1] + [flip(blocks[bit], "tp", bit) for bit in range(1, tp_count)]

    def from_tp(blocks):
        return jnp.concatenate(swapped(blocks, tp_rank), axis=0)

    def paired(mine, got):
        return jnp.stack(swapped([mine, got], lo_rank))

    at.qkv = to_tp(qkv_columns)
    at.gate_mine, at.gate_sent = near_halves(gate_weight)
    at.out = to_tp(head_columns(out_weight))
    at.up_mine, at.up_sent = near_halves(up_weight)
    at.down_mine, at.down_sent = near_halves(down_weight.T)
    at.next()
    at.qkv = flip_tp(at.qkv)
    at.gate_got = flip(at.gate_sent, "ctx", 1)
    at.next()
    at.qkv_0 = from_tp(at.drop("qkv")[0])
    at.gate_pair = paired(*at.drop("gate_mine", "gate_got"))
    at.next()
    at.qkv_x = [over_fsdp(at.qkv_0)]
    at.qkv_1 = ring(at.qkv_0, "ctx")
    at.next()
    at.qkv_x.append(over_fsdp(at.qkv_1))
    at.qkv_2 = ring(at.qkv_1, "ctx")
    at.next()
    at.qkv_x.append(over_fsdp(at.qkv_2))
    at.qkv_3 = ring(at.qkv_2, "ctx")
    at.out = flip_tp(at.out)
    at.next()
    at.out_0 = from_tp(at.drop("out")[0])
    at.drop("qkv_0", "qkv_1", "qkv_2", "gate_sent")
    at.next()
    at.qkv_x.append(over_fsdp(at.qkv_3))
    at.out_1 = ring(at.out_0, "ctx")
    at.next()

    qkv_part = placed(at.drop("qkv_x")[0])
    gain_attn = wide(qkv_part[:, slot_width + kv_width])
    gain_mlp = wide(qkv_part[:, slot_width + kv_width + 1])
    at.normed = low(inputs * scale_one * gain_attn)
    at.qkv_raw = nn(at.normed, qkv_part)
    at.gate_a = over_fsdp(at.gate_pair[0])
    at.out_2 = ring(at.out_1, "ctx")
    at.up_got = flip(at.up_sent, "ctx", 1)
    at.next()
    (qkv_raw,) = at.drop("qkv_raw")
    kv_raw = qkv_raw[:, slot_width : slot_width + kv_width]
    at.kv_own = low(turn(kv_raw, kv_cosine, kv_sine))
    query_raw = qkv_raw[:, :slot_width].reshape(rows, slot_count, head_size)
    queries = low(turn(query_raw, cosine[:, None, :], sine[:, None, :]) * query_scale)
    at.queries = queries.reshape(rows, slot_width)
    at.gate_b = over_fsdp(at.gate_pair[1])
    at.out_3 = ring(at.out_2, "ctx")
    at.next()
    normed = at.normed
    at.out_near = jnp.stack([at.out_0, at.out_1, at.out_2, at.out_3])
    at.next()
    out_x = over_fsdp(at.out_near)
    at.chunks = [shifted(at.kv_own, "ctx", by) for by in range(reach_back, 0, -1)]
    at.up_pair = paired(*at.drop("up_mine", "up_got"))
    at.next()
    at.kv_column = jnp.concatenate(at.drop("chunks")[0] + [at.kv_own], axis=0)
    at.gate_far = jnp.concatenate(quarters(at.gate_pair)[:2], axis=0)
    at.drop("out_0", "out_1", "out_2", "kv_own", "qkv_3")
    at.next()
    at.kv_over_y = flip(at.kv_column, "tp", 2)
    at.down_got = flip(at.down_sent, "ctx", 1)
    at.far_2 = flip(at.gate_far, "ctx", 2)
    at.out_x = out_x
    at.next()
    at.kv_pair = jnp.stack(at.drop("kv_column", "kv_over_y"))
    at.next()
    at.kv_other = flip(at.kv_pair, "tp", 1)
    at.down_pair = paired(*at.drop("down_mine", "down_got"))
    at.mixed_far = jnp.concatenate(quarters(at.gate_pair)[3:] + quarters(at.up_pair)[:2], axis=0)
    at.far_1 = far(quarters(at.gate_pair)[2:3])
    (out_x,) = at.drop("out_x")
    at.out_part = placed([[block[i] for block in out_x] for i in range(ctx_count)])
    at.next()
    kv_pair, kv_other = at.drop("kv_pair", "kv_other")
    at.keyvals = jnp.concatenate(
        swapped([kv_pair[0], kv_other[0], kv_pair[1], kv_other[1]], tp_rank), axis=1
    )
    at.drop("up_sent", "down_sent", "gate_far", "out_near")
    at.next()

    queries, keyvals = at.queries, at.keyvals
    at.attended = attention_forward(queries, keyvals, live, first_key, head_size)
    blocks = low(nt(at.attended, at.out_part)).reshape(2, 2, part_rows, -1)
    at.kept, at.sent = take(blocks, core_rank, 1), take(blocks, 1 - core_rank, 1)
    at.up_x = over_fsdp(at.up_pair)
    at.far_3 = flip(at.mixed_far, "ctx", 2)
    at.next()

    out_part = at.out_part
    quarter_rows = at.far_1[0].shape[0]
    at.got = flip(at.sent, "tp", 1)
    at.gate_other = jnp.concatenate(
        [at.far_2] + at.far_1 + [at.far_3[:quarter_rows]], axis=0
    ).reshape(at.gate_pair.shape)
    at.up_far = jnp.concatenate(quarters(at.up_pair)[2:], axis=0)
    at.next()
    summed = wide(at.kept) + wide(at.got)
    at.kept, at.sent = take(summed, y_rank), low(take(summed, 1 - y_rank))
    at.next()
    at.got = flip(at.sent, "tp", 2)
    at.gate_z = over_fsdp(at.gate_other)
    at.far_4 = flip(at.up_far, "ctx", 2)
    at.next()

    middle = part_rows // 2

    def gather_sides():
        at.over_y, at.over_z = flip(at.part, "tp", 2), flip(at.part, "ctx", 1)
        at.core_own = flip(at.part, "tp", 1)

    def between_sides_and_corners():
        at.to_z, at.to_y = at.over_y[:middle], at.over_z[middle:]
        at.sides = jnp.concatenate([at.over_y, at.over_z], axis=0)

    def gather_corners():
        at.corner_top = flip(at.to_z, "ctx", 1)
        at.corner_end = flip(at.to_y, "tp", 2)
        at.core_sides = flip(at.sides, "tp", 1)

    def between_corners_and_core():
        at.corner = jnp.concatenate(at.drop("corner_top", "corner_end"), axis=0)
        at.drop("to_z", "to_y", "over_y", "over_z")

    def gathered():
        return jnp.concatenate(
            at.drop("part", "sides", "corner", "core_own", "core_sides", "core_corner"), axis=0
        )

    def before_sum(partial):
        mine, theirs = partial.reshape(2, 4, part_rows, -1)
        at.mine, at.mine_corner = mine[:3], mine[3]
        at.theirs, at.theirs_corner = theirs[:3], theirs[3]

    def between_core_and_corners():
        corner = wide(at.drop("mine_corner")[0]) + wide(at.drop("got_corner")[0])
        at.to_z, at.to_y = low(corner[:middle]), low(corner[middle:])

    def sum_corners():
        at.corner_top = flip(at.to_z, "ctx", 1)
        at.corner_end = flip(at.to_y, "tp", 2)

    def between_corners_and_sides():
        mine, got, top, end = at.drop("mine", "got", "corner_top", "corner_end")
        own, over_y, over_z = wide(mine) + wide(got)
        at.over_y = low(jnp.concatenate([over_y[:middle] + wide(top), over_y[middle:]], axis=0))
        at.over_z = low(jnp.concatenate([over_z[:middle], over_z[middle:] + wide(end)], axis=0))
        at.part = own
        at.drop("theirs", "theirs_corner", "to_z", "to_y")

    def sum_sides():
        at.got_y, at.got_z = flip(at.over_y, "tp", 2), flip(at.over_z, "ctx", 1)

    def summed():
        own, got_y, got_z = at.drop("part", "got_y", "got_z")
        at.drop("over_y", "over_z")
        return own + wide(got_y) + wide(got_z)

    residual = inputs_part + (at.kept + wide(at.got))
    at.drop("kept", "got", "sent")
    scale_two = lax.rsqrt(jnp.mean(residual * residual, axis=-1, keepdims=True) + epsilon)
    at.residual = residual
    at.part = low(residual * scale_two * gain_mlp)
    at.down_quarters = quarters(at.down_pair)
    at.next()
    residual = at.residual
    gather_sides()
    at.down_x = over_fsdp(at.down_pair)
    at.far_5 = flip(at.down_quarters[0], "ctx", 2)
    at.up_a, at.up_b = at.far_3[quarter_rows:], at.far_4
    gate_a, gate_b, gate_z = at.drop("gate_a", "gate_b", "gate_z")
    at.gate_full = mlp_placed([jnp.stack(pair) for pair in zip(gate_a, gate_b)], gate_z)
    at.next()
    between_sides_and_corners()
    at.next()
    gather_corners()
    at.up_a = over_fsdp(at.up_a)
    at.far_6 = flip(at.down_quarters[1], "ctx", 2)
    at.next()
    between_corners_and_core()
    at.next()
    at.core_corner = flip(at.corner, "tp", 1)
    at.next()
    at.normed_two = gathered()
    at.gate_proj = nn(at.normed_two, at.gate_full)
    at.up_b = over_fsdp(at.up_b)
    at.far_7 = flip(at.down_quarters[2], "ctx", 2)
    at.down_a = jnp.concatenate([at.far_5, at.far_6], axis=0)
    at.next()
    gate_full = at.gate_full
    up_a, up_b = at.drop("up_a", "up_b")
    up_z = [jnp.stack(pair) for pair in zip(up_a, up_b)]
    up_full = mlp_placed(at.drop("up_x")[0], up_z)
    at.up_proj = nn(at.normed_two, up_full)
    at.down_a = over_fsdp(at.down_a)
    at.far_8 = flip(at.down_quarters[3], "ctx", 2)
    at.next()
    at.down_b = jnp.concatenate([at.far_7, at.far_8], axis=0)
    at.next()
    gate_proj, up_proj = at.gate_proj, at.up_proj
    at.hidden_act = low(gelu_tanh(gate_proj) * up_proj)
    at.down_b = over_fsdp(at.down_b)
    at.next()
    at.drop("far_1", "far_2", "far_3", "far_4", "far_5", "far_6", "far_7", "gate_pair", "up_pair")
    at.drop("far_8", "gate_other", "up_far", "down_quarters", "mixed_far")
    at.drop("down_pair")
    down_x, down_a, down_b = at.drop("down_x", "down_a", "down_b")
    down_z = [jnp.stack(pair) for pair in zip(down_a, down_b)]
    down_full = mlp_placed(down_x, down_z)
    before_sum(low(nt(at.hidden_act, down_full)))
    at.next()
    at.got_corner = flip(at.theirs_corner, "tp", 1)
    at.next()
    between_core_and_corners()
    at.next()
    sum_corners()
    at.got = flip(at.theirs, "tp", 1)
    at.next()
    between_corners_and_sides()
    at.next()
    sum_sides()
    gate_proj, up_proj = at.drop("gate_proj", "up_proj")
    activated, gelu_back = jax.vjp(gelu_tanh, gate_proj)
    at.activated, at.slope = low(activated), low(gelu_back(up_proj)[0])
    at.next()
    at.ffn_parts = at.drop("part", "got_y", "got_z")
    at.drop("over_y", "over_z")
    my_length = lengths[fsdp_rank]
    part_positions = ctx_rank * rows + tp_rank * part_rows + jnp.arange(part_rows)
    valid = wide(part_positions < my_length)[:, None]
    count = wide(jnp.sum(lengths))
    d_scale = lengths.shape[0] * ctx_count * rows / count

    def outputs_of(residual, ffn_parts):
        own, got_y, got_z = ffn_parts
        output = (residual + (own + wide(got_y) + wide(got_z))) * valid
        return output, output - wide(teacher[0])

    at.part = low(valid * outputs_of(residual, at.ffn_parts)[1] * d_scale)
    at.next()
    output, mismatch = outputs_of(at.residual, at.drop("ffn_parts")[0])
    loss_part = jnp.sum(valid * mismatch * mismatch)
    at.d_output = valid * mismatch * d_scale
    at.output_low = low(output)
    gather_sides()
    at.next()
    between_sides_and_corners()
    at.next()
    gather_corners()
    at.next()
    between_corners_and_core()
    at.next()
    at.core_corner = flip(at.corner, "tp", 1)
    at.next()

    def terms(blocks_of, axis):
        count, rank = lax.axis_size(axis), lax.axis_index(axis)
        return [blocks_of((rank - step) % count) for step in range(1, count + 1)]

    def around(sent, axis):
        moving = ring(sent[0], axis)
        for term in sent[1:-1]:
            moving = ring(low(wide(moving) + wide(term)), axis)
        return moving

    def with_own(sent, arrived):
        return wide(sent[-1]) + wide(arrived)

    def far_and_own(grad):
        blocks = grad.reshape(fsdp_count, 2, 2, -1, half)
        return [
            terms(lambda owner: take(take(blocks, owner), high), "fsdp")
            for high in (1 - hi_rank, hi_rank)
        ]

    def blocks_of(grad):
        blocks = grad.reshape(fsdp_count, 2, 2, -1, half)
        return [
            terms(lambda owner: take(take(blocks, owner), high)[lo], "fsdp")
            for high in (1 - hi_rank, hi_rank)
            for lo in range(2)
        ]

    def near_split(mine):
        return wide(take(mine, lo_rank)), low(take(mine, 1 - lo_rank))

    def near_joined(kept, got):
        near, rest_of = swapped([kept, wide(got)], lo_rank)
        return jnp.concatenate([near, rest_of[:, :rest]], axis=1)

    at.d_ffn = gathered()
    at.down_terms = blocks_of(low(tn(at.d_ffn, at.hidden_act)))
    at.next()
    at.down_x = [around(at.down_terms[0], "fsdp")]
    d_hidden = nn(at.d_ffn, down_full)
    at.d_gate = low(d_hidden * wide(at.slope))
    at.d_up = low(d_hidden * wide(at.activated))
    at.next()
    at.drop("d_ffn", "hidden_act", "slope", "activated")
    at.down_x += [around(at.down_terms[1], "fsdp")]
    at.gate_terms = blocks_of(low(tn(at.normed_two, at.d_gate)))
    at.next()
    at.down_far = [low(with_own(at.down_terms[i], at.down_x[i])) for i in range(2)]
    at.next()
    at.down_x += [around(at.down_terms[2], "fsdp"), around(at.down_terms[3], "fsdp")]
    at.down_got_0 = flip(at.down_far[0], "ctx", 2)
    before_sum(low(nt(at.d_gate, gate_full) + nt(at.d_up, up_full)))
    at.next()
    at.got_corner = flip(at.theirs_corner, "tp", 1)
    at.next()
    between_core_and_corners()
    at.drop("d_gate")
    at.down_rest = jnp.split(at.down_far[1], 2)
    at.next()
    sum_corners()
    at.got = flip(at.theirs, "tp", 1)
    at.gate_got = [around(at.gate_terms[0], "fsdp")]
    at.down_got_1 = flip(at.down_rest[0], "ctx", 2)
    at.next()
    between_corners_and_sides()
    at.next()
    sum_sides()
    down_terms, down_x = at.drop("down_terms", "down_x")
    at.down_own = jnp.stack([low(with_own(down_terms[i], down_x[i])) for i in (2, 3)])
    at.gate_got += [around(at.gate_terms[1], "fsdp"), around(at.gate_terms[2], "fsdp")]
    at.down_got_2 = flip(at.down_rest[1], "ctx", 2)
    up_blocks = low(tn(at.normed_two, at.d_up)).reshape(fsdp_count, 2, 2, -1, half)
    at.up_first = terms(lambda owner: take(take(up_blocks, owner), 1 - hi_rank)[0], "fsdp")
    at.up_others = terms(
        lambda owner: jnp.concatenate(
            [take(take(up_blocks, owner), 1 - hi_rank)[1:], take(take(up_blocks, owner), hi_rank)]
        ),
        "fsdp",
    )
    at.next()
    at.drop("normed_two", "d_up", "down_far", "down_rest")
    at.gate_far = [low(with_own(at.gate_terms[i], at.gate_got[i])) for i in range(2)]
    d_normed_two = summed()
    scaled = gain_mlp * d_normed_two
    inner_two = jnp.mean(scaled * residual, axis=-1, keepdims=True)
    at.d_residual = at.d_output + scale_two * scaled - residual * scale_two**3 * inner_two
    at.gain_mlp_sums = jnp.sum(d_normed_two * residual * scale_two, axis=0)
    at.part = low(at.d_residual)
    at.next()
    at.over_y = flip(at.part, "tp", 2)
    got_0, got_1, got_2 = at.drop("down_got_0", "down_got_1", "down_got_2")
    down_got = jnp.stack([got_0, jnp.concatenate([got_1, got_2], axis=0)])
    at.down_kept, at.down_sent = near_split(wide(at.drop("down_own")[0]) + wide(down_got))
    at.gate_got += [around(at.gate_terms[3], "fsdp")]
    at.up_first_got = around(at.up_first, "fsdp")
    at.gate_far_0 = flip(at.gate_far[0], "ctx", 2)
    at.next()
    at.pair = jnp.stack(at.drop("part", "over_y"))
    at.next()
    at.other = flip(at.pair, "tp", 1)
    at.up_far = jnp.split(low(with_own(*at.drop("up_first", "up_first_got"))), 2)
    gate_terms, gate_got = at.drop("gate_terms", "gate_got")
    at.gate_own = jnp.stack([low(with_own(gate_terms[i], gate_got[i])) for i in (2, 3)])
    at.next()
    pair, other = at.drop("pair", "other")
    d_attn = swapped([pair[0], other[0], pair[1], other[1]], tp_rank)
    at.d_attn = jnp.concatenate(d_attn, axis=0)
    at.next()
    at.down_got = flip(at.down_sent, "ctx", 1)
    live_columns = jnp.repeat(live, head_size).astype(jnp.float32)
    d_attended = low(nn(at.d_attn, out_part) * live_columns)
    out_grad = low(tn(at.d_attn, at.attended))

    own_rows = attn_gain.shape[0]

    def split_sums(columns):
        rounded = low(columns)
        return jnp.concatenate([rounded, low(columns - wide(rounded))], axis=-1)

    def joined_sums(columns):
        return columns[..., :64] + columns[..., 64:]

    def to_tp_back(mine):
        blocks = low(mine).reshape(tp_count, own_rows, -1)
        return [take(blocks, tp_rank ^ bit) for bit in range(tp_count)]

    def by_rows(grad):
        return grad.reshape(fsdp_count, ctx_count, tp_count * own_rows, -1)

    def halves_of(grad):
        grad = by_rows(grad)
        turned = [take(grad, (ctx_rank - by) % ctx_count, 1) for by in range(1, ctx_count + 1)]
        pairs = [jnp.stack(turned[:2], axis=1), jnp.stack(turned[2:], axis=1)]
        return [terms(lambda owner: take(pair, owner), "fsdp") for pair in pairs]

    at.out_terms = halves_of(out_grad)
    at.d_queries, at.d_keyvals = attention_backward(
        queries, keyvals, d_attended, first_key, head_size
    )
    at.up_others_got = around(at.up_others, "fsdp")
    at.gate_far_1 = flip(at.gate_far[1], "ctx", 2)
    at.up_far_0 = flip(at.up_far[0], "ctx", 2)
    at.next()
    at.drop("attended", "d_attn", "down_sent")
    kv_blocks = jnp.stack(jnp.split(at.d_keyvals, tp_count, axis=1)).reshape(2, 2, -1, kv_width)
    at.kv_kept, at.kv_sent = take(kv_blocks, core_rank, 1), take(kv_blocks, 1 - core_rank, 1)
    at.drop("d_keyvals")
    at.next()
    at.kv_got = flip(at.kv_sent, "tp", 1)
    up_others, up_others_got = at.drop("up_others", "up_others_got")
    up_rest = jnp.split(low(wide(up_others[-1][0]) + wide(up_others_got[0])), 2)
    at.up_mixed = jnp.concatenate([at.up_far[1], up_rest[0]], axis=0)
    at.up_last = up_rest[1]
    at.up_own, at.up_own_got = up_others[-1][1:], up_others_got[1:]
    gate_far_got = jnp.stack(at.drop("gate_far_0", "gate_far_1"))
    at.gate_kept, at.gate_sent = near_split(wide(at.drop("gate_own")[0]) + wide(gate_far_got))
    at.drop("gate_far")
    at.next()
    kv_sum = wide(at.kv_kept) + wide(at.kv_got)
    at.kv_kept, at.kv_sent = take(kv_sum, y_rank), low(take(kv_sum, 1 - y_rank))
    at.next()
    at.kv_got = flip(at.kv_sent, "tp", 2)
    at.up_far_1 = flip(at.up_mixed, "ctx", 2)
    at.gate_near = flip(at.gate_sent, "ctx", 1)
    at.down_out = near_joined(*at.drop("down_kept", "down_got")).T
    at.up_own = low(wide(at.up_own) + wide(at.drop("up_own_got")[0]))
    at.out_got = [around(at.out_terms[0], "fsdp")]
    d_query_raw = turn(
        at.d_queries.reshape(rows, slot_count, head_size) * query_scale,
        cosine[:, None, :],
        -sine[:, None, :],
    )
    at.d_query_low = low(d_query_raw.reshape(rows, slot_width))
    at.query_terms = halves_of(low(tn(normed, at.d_query_low)))
    at.next()
    at.drop("d_queries", "kv_sent")
    kv_sum = (at.drop("kv_kept")[0] + wide(at.drop("kv_got")[0])).reshape(reach_back + 1, rows, -1)
    at.kv_low = [low(kv_sum[reach_back - by]) for by in range(1, reach_back + 1)]
    at.d_kv = kv_sum[reach_back]
    at.out_1 = low(with_own(at.out_terms[0], at.out_got[0]))
    at.next()
    at.kv_got = [shifted(at.kv_low[by - 1], "ctx", -by) for by in range(1, reach_back + 1)]
    at.out_got += [around(at.out_terms[1], "fsdp")]
    at.next()
    d_kv = at.d_kv
    for got in at.drop("kv_got")[0]:
        d_kv = d_kv + wide(got)
    d_kv_low = low(turn(d_kv, kv_cosine, -kv_sine))
    at.d_qkv = jnp.concatenate(
        [at.d_query_low, jnp.pad(d_kv_low, ((0, 0), (0, kv_width)))], axis=1
    )
    at.next()
    at.query_got = [around(at.query_terms[0], "fsdp")]
    at.up_far_2 = flip(at.up_last, "ctx", 2)
    at.out_z = ring(at.out_1[0], "ctx")
    at.partial = low(nt(at.d_qkv, qkv_part))
    at.next()
    partial = at.partial
    blocks = partial.reshape(2, 2, part_rows, -1)
    at.kept, at.sent = take(blocks, core_rank, 1), take(blocks, 1 - core_rank, 1)
    at.next()
    at.drop("d_query_low", "kv_low", "d_kv", "gate_sent")
    at.query_1 = low(with_own(at.query_terms[0], at.query_got[0]))
    at.out_2 = with_own(at.out_terms[1], at.out_got[1])
    at.out_z = low(wide(at.out_z) + wide(at.out_1[1]))
    at.got = flip(at.sent, "tp", 1)
    at.out_z = ring(at.out_z, "ctx")
    gain_attn_sums = jnp.sum(wide(at.partial) * inputs * scale_one, axis=0)
    sums = [gain_attn_sums, at.gain_mlp_sums, jnp.full(gain_attn_sums.shape, loss_part)]
    columns = jnp.pad(jnp.stack(sums, axis=1), ((0, 0), (0, 61)))
    kv_grad = jnp.concatenate([low(tn(normed, at.d_qkv[:, slot_width : slot_width + kv_width])), split_sums(columns)], axis=1)
    at.kv_terms = terms(lambda owner: take(by_rows(kv_grad), owner), "fsdp")
    at.next()
    summed_rows = wide(at.kept) + wide(at.got)
    at.kept, at.sent = take(summed_rows, y_rank), low(take(summed_rows, 1 - y_rank))
    at.out_z = low(wide(at.out_z) + at.out_2[0])
    at.next()
    at.got = flip(at.sent, "tp", 2)
    at.query_got += [around(at.query_terms[1], "fsdp")]
    got = at.drop("up_far_0", "up_far_1", "up_far_2")
    up_far_got = jnp.concatenate(got, axis=0).reshape(2, -1, half)
    at.up_kept, up_sent = near_split(wide(at.up_own) + wide(up_far_got))
    at.up_sent = jnp.split(up_sent, 2)
    at.gate_out = near_joined(*at.drop("gate_kept", "gate_near"))
    at.query_z = ring(at.query_1[0], "ctx")
    at.out_z = ring(at.out_z, "ctx")
    at.next()
    at.query_z = low(wide(at.query_z) + wide(at.query_1[1]))
    at.next()
    at.query_2 = with_own(at.query_terms[1], at.query_got[1])
    at.d_normed = at.kept + wide(at.got)
    at.drop("partial", "d_qkv")
    at.drop("query_1", "kept", "sent", "got", "up_far", "up_mixed", "up_last", "up_own")
    at.drop("query_terms", "query_got")
    at.drop("out_terms", "out_got")
    at.query_z = ring(at.query_z, "ctx")
    at.kv_got = around(at.kv_terms, "fsdp")
    at.up_near = flip(at.up_sent[0], "ctx", 1)
    at.out_back = to_tp_back(wide(at.out_z) + at.out_2[1])
    at.next()
    at.query_z = low(wide(at.query_z) + at.query_2[0])
    kv_mine = with_own(*at.drop("kv_terms", "kv_got"))
    kv_mine = jnp.concatenate(
        [low(kv_mine[..., :kv_width]), split_sums(joined_sums(kv_mine[..., kv_width:]))], axis=-1
    )
    at.kv_own = take(kv_mine, ctx_rank)
    at.kv_sent = [take(kv_mine, (ctx_rank + by) % ctx_count) for by in range(1, ctx_count)]

    at.next()
    at.drop("out_z", "out_2")
    at.out_back = flip_tp(at.out_back)
    at.query_z = ring(at.query_z, "ctx")
    at.kv_got = [ring(at.kv_sent[by - 1], "ctx", by) for by in range(1, ctx_count)]
    at.next()
    query_mine = low(wide(at.query_z) + at.query_2[1])
    kv_mine = sum([wide(got) for got in at.kv_got], wide(at.kv_own))
    kv_mine = jnp.concatenate(
        [low(kv_mine[:, :kv_width]), split_sums(joined_sums(kv_mine[:, kv_width:]))], axis=1
    )
    at.back = to_tp_back(jnp.concatenate([query_mine, kv_mine], axis=1))
    at.next()
    up_near = jnp.concatenate([at.up_near, flip(at.up_sent[1], "ctx", 1)], axis=0)
    at.drop("query_z", "query_2", "kv_got", "kv_own", "kv_sent", "up_sent")

    def whole_heads(parts):
        columns = []
        for rank, part in enumerate(parts):
            first = rank * (slot_count - 1) + min(rank, fuller)
            base = min(first, head_count - slot_count)
            held = slot_count - 1 + (1 if rank < fuller else 0)
            start = (first - base) * head_size
            columns.append(wide(part[:, start : start + held * head_size]))
        return jnp.concatenate(columns, axis=1)

    parts = swapped(flip_tp(at.back), tp_rank)
    query_grad = whole_heads([part[:, :slot_width] for part in parts])
    out_grad = whole_heads(swapped(at.out_back, tp_rank))
    kv_parts = [wide(part[:, slot_width:]) for part in parts]
    kv_grad = jnp.concatenate([part[:, :kv_width] for part in kv_parts], axis=1)
    sums = joined_sums(sum(part[:, kv_width:] for part in kv_parts))
    gain_attn_grad, gain_mlp_grad, loss_sum = sums[:, 0], sums[:, 1], sums[0, 2]
    down_grad, gate_grad = at.down_out, at.gate_out
    up_grad = near_joined(at.up_kept, up_near)
    loss = loss_sum / (count * width)
    d_normed, d_residual = at.d_normed, at.d_residual
    scale_part = lax.dynamic_slice_in_dim(scale_one, tp_rank * part_rows, part_rows, 0)
    scaled = gain_attn * d_normed
    inner_one = jnp.mean(scaled * inputs_part, axis=-1, keepdims=True)
    input_grad = d_residual + scale_part * scaled - inputs_part * scale_part**3 * inner_one
    return (
        at.output_low[None],
        loss,
        input_grad[None],
        gain_attn_grad,
        query_grad,
        kv_grad,
        out_grad,
        gain_mlp_grad,
        gate_grad,
        up_grad,
        down_grad,
    )


def solution(mesh):
    in_specs = (
        P("fsdp", "ctx", None),
        P(),
        P("fsdp", ("ctx", "tp"), None),
        P(("fsdp", "ctx", "tp")),
        P(("fsdp", "ctx", "tp"), None),
        P(("fsdp", "ctx", "tp"), None),
        P(("fsdp", "ctx", "tp"), None),
        P(("fsdp", "ctx", "tp")),
        P(("fsdp", "ctx"), "tp"),
        P(("fsdp", "ctx"), "tp"),
        P("tp", ("fsdp", "ctx")),
    )
    out_specs = (
        P("fsdp", ("ctx", "tp"), None),
        P(),
        P("fsdp", ("ctx", "tp"), None),
        P(("fsdp", "ctx", "tp")),
        P(("fsdp", "ctx", "tp"), None),
        P(("fsdp", "ctx", "tp"), None),
        P(("fsdp", "ctx", "tp"), None),
        P(("fsdp", "ctx", "tp")),
        P(("fsdp", "ctx"), "tp"),
        P(("fsdp", "ctx"), "tp"),
        P("tp", ("fsdp", "ctx")),
    )
    return jax.shard_map(local, mesh=mesh, in_specs=in_specs, out_specs=out_specs, check_vma=False)
```

```python
import jax
import jax.numpy as jnp
from jax import lax
from jax.experimental import pallas as pl
from jax.experimental.pallas import tpu as pltpu
from jax.sharding import PartitionSpec as P

W = 2048

epsilon = 1e-06
lowest = -1e30
ROWS = 256
VMEM_BYTES = 40 * 1024 * 1024


def flip(array, axis, bit):
    return lax.ppermute(array, axis, [(i, i ^ bit) for i in range(lax.axis_size(axis))])


def ring(array, axis, by=1):
    count = lax.axis_size(axis)
    return lax.ppermute(array, axis, [(i, (i + by) % count) for i in range(count)])


def shifted(array, axis, by):
    count = lax.axis_size(axis)
    pairs = [(i, i + by) for i in range(count) if 0 <= i + by < count]
    return lax.ppermute(array, axis, pairs)


class Steps:
    def next(self):
        self.__dict__.update(lax.optimization_barrier(dict(self.__dict__)))

    def drop(self, *names):
        return [self.__dict__.pop(name) for name in names]


def sync(*trees):
    return lax.optimization_barrier(trees)


def after(array, *others):
    return lax.optimization_barrier((array, others))[0]


def low(values):
    return values.astype(jnp.bfloat16)


def wide(values):
    return values.astype(jnp.float32)


def take(array, index, axis=0):
    return lax.dynamic_index_in_dim(array, index, axis, keepdims=False)


def swapped(blocks, rank):
    if len(blocks) == 2:
        odd = rank == 1
        return [jnp.where(odd, blocks[1], blocks[0]), jnp.where(odd, blocks[0], blocks[1])]
    first = swapped(blocks[:2], rank % 2) + swapped(blocks[2:], rank % 2)
    outer = rank // 2 == 1
    return [jnp.where(outer, first[i ^ 2], first[i]) for i in range(4)]


def place(pieces, slots):
    count = len(pieces)
    shape = pieces[0].shape

    def body(slots_ref, *refs):
        out_ref, held, came, left = refs[count:]
        into = [pltpu.make_async_copy(refs[k], held.at[k], came.at[k]) for k in range(count)]
        out_of = [
            pltpu.make_async_copy(held.at[k], out_ref.at[slots_ref[k]], left.at[k])
            for k in range(count)
        ]
        for copy in into:
            copy.start()
        for first, second in zip(into, out_of):
            first.wait()
            second.start()
        for copy in out_of:
            copy.wait()

    return pl.pallas_call(
        body,
        out_shape=jax.ShapeDtypeStruct((count,) + shape, pieces[0].dtype),
        grid_spec=pltpu.PrefetchScalarGridSpec(
            num_scalar_prefetch=1,
            grid=(1,),
            in_specs=[pl.BlockSpec(memory_space=pl.ANY)] * count,
            out_specs=pl.BlockSpec(memory_space=pl.ANY),
            scratch_shapes=[
                pltpu.VMEM((count,) + shape, pieces[0].dtype),
                pltpu.SemaphoreType.DMA((count,)),
                pltpu.SemaphoreType.DMA((count,)),
            ],
        ),
        compiler_params=pltpu.CompilerParams(vmem_limit_bytes=VMEM_BYTES),
        cost_estimate=pl.CostEstimate(
            flops=0, bytes_accessed=4 * count * pieces[0].size, transcendentals=0
        ),
        name="place",
    )(jnp.stack(slots).astype(jnp.int32), *pieces)


def nn(first, second):
    return lax.dot_general(
        first, second, (((1,), (0,)), ((), ())), preferred_element_type=jnp.float32
    )


def nt(first, second):
    return lax.dot_general(
        first, second, (((1,), (1,)), ((), ())), preferred_element_type=jnp.float32
    )


def tn(first, second):
    return lax.dot_general(
        first, second, (((0,), (0,)), ((), ())), preferred_element_type=jnp.float32
    )


def ring_sum(block_of, axis):
    count = lax.axis_size(axis)
    rank = lax.axis_index(axis)
    moving = None
    for step in range(1, count):
        term = block_of((rank - step) % count)
        moving = low(term if moving is None else wide(moving) + wide(term))
        moving = ring(moving, axis)
    own = wide(block_of(rank))
    return own if moving is None else own + wide(moving)


def attention_forward(queries, keyvals, live, first_key, head_size):
    rows, columns = queries.shape
    heads = columns // head_size
    reach = W + ROWS
    lead = keyvals.shape[0] - rows - W

    def body(info_ref, q_ref, kv_ref, o_ref):
        head, block = pl.program_id(0), pl.program_id(1)
        start = pl.multiple_of(lead + block * ROWS, ROWS)
        keys = kv_ref[pl.ds(start, reach), :head_size]
        vals = kv_ref[pl.ds(start, reach), head_size:]
        scores = nt(q_ref[...], keys)
        row = lax.broadcasted_iota(jnp.int32, scores.shape, 0)
        column = lax.broadcasted_iota(jnp.int32, scores.shape, 1)
        ahead = column - row
        allowed = (ahead > 0) & (ahead <= W) & (column >= info_ref[0] - start)
        scores = jnp.where(allowed, scores, lowest)
        peak = jnp.max(scores, axis=1, keepdims=True)
        shares = jnp.exp(scores - peak)
        total = jnp.sum(shares, axis=1, keepdims=True)
        probs = low(shares * (1.0 / total))
        mixed = nn(probs, vals)
        o_ref[...] = low(mixed * wide(info_ref[1 + head]))

    return pl.pallas_call(
        body,
        out_shape=jax.ShapeDtypeStruct((rows, columns), jnp.bfloat16),
        grid_spec=pltpu.PrefetchScalarGridSpec(
            num_scalar_prefetch=1,
            grid=(heads, rows // ROWS),
            in_specs=[
                pl.BlockSpec((ROWS, head_size), lambda h, i, info: (i, h)),
                pl.BlockSpec(keyvals.shape, lambda h, i, info: (0, 0)),
            ],
            out_specs=pl.BlockSpec((ROWS, head_size), lambda h, i, info: (i, h)),
        ),
        compiler_params=pltpu.CompilerParams(vmem_limit_bytes=VMEM_BYTES),
        cost_estimate=pl.CostEstimate(
            flops=4 * heads * rows * reach * head_size,
            bytes_accessed=4 * rows * columns + 2 * keyvals.size,
            transcendentals=heads * rows * reach,
        ),
        name="attention_forward",
    )(jnp.concatenate([first_key[None], live]).astype(jnp.int32), queries, keyvals)


def attention_backward(queries, keyvals, d_attended, first_key, head_size):
    rows, columns = queries.shape
    heads = columns // head_size
    reach = W + ROWS
    span = keyvals.shape[0]
    lead = span - rows - W

    def body(info_ref, q_ref, kv_ref, do_ref, dq_ref, dkv_ref, sums):
        head, block = pl.program_id(0), pl.program_id(1)

        @pl.when((head == 0) & (block == 0))
        def _():
            sums[...] = jnp.zeros_like(sums)

        start = pl.multiple_of(lead + block * ROWS, ROWS)
        keys = kv_ref[pl.ds(start, reach), :head_size]
        vals = kv_ref[pl.ds(start, reach), head_size:]
        query = q_ref[...]
        d_out = do_ref[...]
        scores = nt(keys, query)
        column = lax.broadcasted_iota(jnp.int32, scores.shape, 0)
        row = lax.broadcasted_iota(jnp.int32, scores.shape, 1)
        ahead = column - row
        allowed = (ahead > 0) & (ahead <= W) & (column >= info_ref[0] - start)
        scores = jnp.where(allowed, scores, lowest)
        peak = jnp.max(scores, axis=0, keepdims=True)
        shares = jnp.exp(scores - peak)
        total = jnp.sum(shares, axis=0, keepdims=True)
        probs = shares * (1.0 / total)
        d_probs = nt(vals, d_out)
        inner = jnp.sum(probs * d_probs, axis=0, keepdims=True)
        d_scores = low(probs * (d_probs - inner))
        dq_ref[...] = tn(d_scores, keys)
        sums[pl.ds(start, reach), :head_size] += nn(d_scores, query)
        sums[pl.ds(start, reach), head_size:] += nn(low(probs), d_out)

        @pl.when((head == heads - 1) & (block == rows // ROWS - 1))
        def _():
            dkv_ref[...] = low(sums[...])

    return pl.pallas_call(
        body,
        out_shape=(
            jax.ShapeDtypeStruct((rows, columns), jnp.float32),
            jax.ShapeDtypeStruct(keyvals.shape, jnp.bfloat16),
        ),
        grid_spec=pltpu.PrefetchScalarGridSpec(
            num_scalar_prefetch=1,
            grid=(heads, rows // ROWS),
            in_specs=[
                pl.BlockSpec((ROWS, head_size), lambda h, i, info: (i, h)),
                pl.BlockSpec(keyvals.shape, lambda h, i, info: (0, 0)),
                pl.BlockSpec((ROWS, head_size), lambda h, i, info: (i, h)),
            ],
            out_specs=(
                pl.BlockSpec((ROWS, head_size), lambda h, i, info: (i, h)),
                pl.BlockSpec(keyvals.shape, lambda h, i, info: (0, 0)),
            ),
            scratch_shapes=[pltpu.VMEM(keyvals.shape, jnp.float32)],
        ),
        compiler_params=pltpu.CompilerParams(vmem_limit_bytes=VMEM_BYTES),
        cost_estimate=pl.CostEstimate(
            flops=10 * heads * rows * reach * head_size,
            bytes_accessed=8 * rows * columns + 4 * keyvals.size,
            transcendentals=heads * rows * reach,
        ),
        name="attention_backward",
    )(first_key[None].astype(jnp.int32), queries, keyvals, d_attended)


def gelu_tanh(values):
    return jax.nn.gelu(values, approximate=True)


def local(
    hidden,
    lengths,
    teacher,
    attn_gain,
    query_weight,
    kv_weight,
    out_weight,
    mlp_gain,
    gate_weight,
    up_weight,
    down_weight,
):
    tp_count = lax.axis_size("tp")
    ctx_count = lax.axis_size("ctx")
    fsdp_count = lax.axis_size("fsdp")
    tp_rank = lax.axis_index("tp")
    ctx_rank = lax.axis_index("ctx")
    fsdp_rank = lax.axis_index("fsdp")
    y_rank, core_rank = tp_rank // 2, tp_rank % 2
    hi_rank, lo_rank = ctx_rank // 2, ctx_rank % 2
    seq_count, rows, width = hidden.shape
    assert seq_count == 1 and tp_count == 4 and ctx_count == 4
    part_rows = rows // tp_count
    head_size = kv_weight.shape[1] // 2
    head_count = query_weight.shape[1] // head_size
    slot_count = -(-head_count // tp_count)
    slot_width = slot_count * head_size
    fuller = head_count - (slot_count - 1) * tp_count
    kv_width = 2 * head_size // tp_count

    def first_head_of(rank):
        return rank * (slot_count - 1) + jnp.minimum(rank, fuller)

    def slot_base_of(rank):
        return jnp.minimum(first_head_of(rank), head_count - slot_count)

    slot_heads = slot_base_of(tp_rank) + jnp.arange(slot_count)
    first_head = first_head_of(tp_rank)
    held_heads = slot_count - 1 + (tp_rank < fuller).astype(jnp.int32)
    live = ((slot_heads >= first_head) & (slot_heads < first_head + held_heads)).astype(jnp.int32)

    def over_tp(columns_of):
        blocks = [columns_of(tp_rank)]
        for bit in range(1, tp_count):
            blocks.append(flip(columns_of(tp_rank ^ bit), "tp", bit))
        return jnp.concatenate(swapped(blocks, tp_rank), axis=0)

    def over_fsdp(block):
        blocks = [block]
        for _ in range(1, fsdp_count):
            blocks.append(ring(blocks[-1], "fsdp"))
        return blocks

    def placed(by_ctx):
        pieces, slots = [], []
        for step, blocks in enumerate(by_ctx):
            for turn_at, block in enumerate(blocks):
                pieces.append(block)
                slots.append(
                    (fsdp_rank - turn_at) % fsdp_count * ctx_count
                    + (ctx_rank - step) % ctx_count
                )
        return place(pieces, slots).reshape(width, pieces[0].shape[1])

    def head_columns(weight):
        return lambda rank: lax.dynamic_slice_in_dim(
            weight, slot_base_of(rank) * head_size, slot_width, 1
        )

    unit_count = gate_weight.shape[1]
    half = -(-unit_count // 256) * 128
    rest = unit_count - half

    def near_halves(block):
        near, far = block[:, :half], jnp.pad(block[:, half:], ((0, 0), (0, half - rest)))
        mine = jnp.where(lo_rank == 0, near, far)
        theirs = jnp.where(lo_rank == 0, far, near)
        return mine, theirs

    def near_pair(halves):
        mine, theirs = halves
        return jnp.stack(swapped([mine, flip(theirs, "ctx", 1)], lo_rank))

    def quarters(pair):
        return jnp.split(pair.reshape(-1, half), 4)

    def far(pieces):
        if len(pieces) == 1:
            return [flip(pieces[0], "ctx", 2)]
        return jnp.split(flip(jnp.concatenate(pieces, axis=0), "ctx", 2), len(pieces))

    def mlp_placed(own, other):
        pieces, slots = [], []
        for far_bit, blocks in enumerate((own, other)):
            for turn_at, block in enumerate(blocks):
                pieces.append(block.reshape(-1, half))
                slots.append((fsdp_rank - turn_at) % fsdp_count * 2 + (hi_rank ^ far_bit))
        return place(pieces, slots).reshape(width, half)

    inputs_low = hidden[0]
    inputs = wide(inputs_low)
    inputs_part_low = lax.dynamic_slice_in_dim(inputs_low, tp_rank * part_rows, part_rows, 0)
    inputs_part = wide(inputs_part_low)
    scale_one = lax.rsqrt(jnp.mean(inputs * inputs, axis=-1, keepdims=True) + epsilon)
    positions = ctx_rank * rows + jnp.arange(rows)
    quarter = head_size // 4
    frequency = 10000.0 ** (-(jnp.arange(quarter).astype(jnp.float32) * 4.0 / head_size))
    angle = wide(positions)[:, None] * frequency[None, :]
    cosine, sine = jnp.cos(angle), jnp.sin(angle)

    def turn(values, cosine, sine):
        first, second = values[..., :quarter], values[..., quarter : 2 * quarter]
        return jnp.concatenate(
            [
                first * cosine - second * sine,
                second * cosine + first * sine,
                values[..., 2 * quarter :],
            ],
            axis=-1,
        )

    turning = tp_rank == 0
    kv_cosine, kv_sine = jnp.where(turning, cosine, 1.0), jnp.where(turning, sine, 0.0)
    query_scale = head_size ** (-0.5)
    reach_back = min((W - 2) // rows + 1, ctx_count - 1)
    first_key = (reach_back - jnp.minimum(ctx_rank, reach_back)) * rows

    at = Steps()
    gains = jnp.pad(jnp.stack([attn_gain, mlp_gain], axis=1), ((0, 0), (0, 126)))

    def qkv_columns(rank):
        kv = lax.dynamic_slice_in_dim(kv_weight, rank * kv_width, kv_width, 1)
        return jnp.concatenate([head_columns(query_weight)(rank), kv, gains], axis=1)

    def to_tp(columns_of):
        return [columns_of(tp_rank ^ bit) for bit in range(tp_count)]

    def flip_tp(blocks):
        return blocks[:1] + [flip(blocks[bit], "tp", bit) for bit in range(1, tp_count)]

    def from_tp(blocks):
        return jnp.concatenate(swapped(blocks, tp_rank), axis=0)

    def paired(mine, got):
        return jnp.stack(swapped([mine, got], lo_rank))

    at.qkv = to_tp(qkv_columns)
    at.gate_mine, at.gate_sent = near_halves(gate_weight)
    at.out_weight, at.up_weight, at.down_weight = out_weight, up_weight, down_weight
    at.next()
    at.qkv = flip_tp(at.qkv)
    at.gate_got = flip(at.gate_sent, "ctx", 1)
    at.next()
    at.qkv_0 = from_tp(at.drop("qkv")[0])
    at.gate_pair = paired(*at.drop("gate_mine", "gate_got"))
    at.next()
    at.qkv_x = [over_fsdp(at.qkv_0)]
    at.qkv_1 = ring(at.qkv_0, "ctx")
    at.out = to_tp(head_columns(at.drop("out_weight")[0]))
    at.next()
    at.qkv_x.append(over_fsdp(at.qkv_1))
    at.qkv_2 = ring(at.qkv_1, "ctx")
    at.up_mine, at.up_sent = near_halves(at.drop("up_weight")[0])
    at.down_mine, at.down_sent = near_halves(at.drop("down_weight")[0].T)
    at.next()
    at.qkv_x.append(over_fsdp(at.qkv_2))
    at.qkv_3 = ring(at.qkv_2, "ctx")
    at.out = flip_tp(at.out)
    at.next()
    at.out_0 = from_tp(at.drop("out")[0])
    at.drop("qkv_0", "qkv_1", "qkv_2", "gate_sent")
    at.next()
    at.qkv_x.append(over_fsdp(at.qkv_3))
    at.out_1 = ring(at.out_0, "ctx")
    at.next()

    qkv_part = placed(at.drop("qkv_x")[0])
    gain_attn = wide(qkv_part[:, slot_width + kv_width])
    gain_mlp = wide(qkv_part[:, slot_width + kv_width + 1])
    at.normed = low(inputs * scale_one * gain_attn)
    at.qkv_raw = nn(at.normed, qkv_part)
    at.gate_a = over_fsdp(at.gate_pair[0])
    at.out_2 = ring(at.out_1, "ctx")
    at.up_got = flip(at.up_sent, "ctx", 1)
    at.next()
    (qkv_raw,) = at.drop("qkv_raw")
    kv_raw = qkv_raw[:, slot_width : slot_width + kv_width]
    at.kv_own = low(turn(kv_raw, kv_cosine, kv_sine))
    query_raw = qkv_raw[:, :slot_width].reshape(rows, slot_count, head_size)
    queries = low(turn(query_raw, cosine[:, None, :], sine[:, None, :]) * query_scale)
    at.queries = queries.reshape(rows, slot_width)
    at.gate_b = over_fsdp(at.gate_pair[1])
    at.out_3 = ring(at.out_2, "ctx")
    at.next()
    normed = at.normed
    at.out_near = jnp.stack([at.out_0, at.out_1, at.out_2, at.out_3])
    at.next()
    out_x = over_fsdp(at.out_near)
    at.chunks = [shifted(at.kv_own, "ctx", by) for by in range(reach_back, 0, -1)]
    at.up_pair = paired(*at.drop("up_mine", "up_got"))
    at.next()
    at.kv_column = jnp.concatenate(at.drop("chunks")[0] + [at.kv_own], axis=0)
    at.gate_far = jnp.concatenate(quarters(at.gate_pair)[:2], axis=0)
    at.drop("out_0", "out_1", "out_2", "kv_own", "qkv_3")
    at.next()
    at.kv_over_y = flip(at.kv_column, "tp", 2)
    at.down_got = flip(at.down_sent, "ctx", 1)
    at.far_2 = flip(at.gate_far, "ctx", 2)
    at.out_x = out_x
    at.next()
    at.kv_pair = jnp.stack(at.drop("kv_column", "kv_over_y"))
    at.next()
    at.kv_other = flip(at.kv_pair, "tp", 1)
    at.down_pair = paired(*at.drop("down_mine", "down_got"))
    at.mixed_far = jnp.concatenate(quarters(at.gate_pair)[3:] + quarters(at.up_pair)[:2], axis=0)
    at.far_1 = far(quarters(at.gate_pair)[2:3])
    (out_x,) = at.drop("out_x")
    at.out_part = placed([[block[i] for block in out_x] for i in range(ctx_count)])
    at.next()
    kv_pair, kv_other = at.drop("kv_pair", "kv_other")
    at.keyvals = jnp.concatenate(
        swapped([kv_pair[0], kv_other[0], kv_pair[1], kv_other[1]], tp_rank), axis=1
    )
    at.drop("up_sent", "down_sent", "gate_far", "out_near")
    at.next()

    queries, keyvals = at.queries, at.keyvals
    at.attended = attention_forward(queries, keyvals, live, first_key, head_size)
    blocks = low(nt(at.attended, at.out_part)).reshape(2, 2, part_rows, -1)
    at.kept, at.sent = take(blocks, core_rank, 1), take(blocks, 1 - core_rank, 1)
    at.up_x = over_fsdp(at.up_pair)
    at.far_3 = flip(at.mixed_far, "ctx", 2)
    at.next()

    out_part = at.out_part
    quarter_rows = at.far_1[0].shape[0]
    at.got = flip(at.sent, "tp", 1)
    at.gate_other = jnp.concatenate(
        [at.far_2] + at.far_1 + [at.far_3[:quarter_rows]], axis=0
    ).reshape(at.gate_pair.shape)
    at.up_far = jnp.concatenate(quarters(at.up_pair)[2:], axis=0)
    at.next()
    summed = wide(at.kept) + wide(at.got)
    at.kept, at.sent = take(summed, y_rank), low(take(summed, 1 - y_rank))
    at.next()
    at.got = flip(at.sent, "tp", 2)
    at.gate_z = over_fsdp(at.gate_other)
    at.far_4 = flip(at.up_far, "ctx", 2)
    at.next()

    middle = part_rows // 2

    def gather_sides():
        at.over_y, at.over_z = flip(at.part, "tp", 2), flip(at.part, "ctx", 1)
        at.core_own = flip(at.part, "tp", 1)

    def between_sides_and_corners():
        at.to_z, at.to_y = at.over_y[:middle], at.over_z[middle:]
        at.sides = jnp.concatenate([at.over_y, at.over_z], axis=0)

    def gather_corners():
        at.corner_top = flip(at.to_z, "ctx", 1)
        at.corner_end = flip(at.to_y, "tp", 2)
        at.core_sides = flip(at.sides, "tp", 1)

    def between_corners_and_core():
        at.corner = jnp.concatenate(at.drop("corner_top", "corner_end"), axis=0)
        at.drop("to_z", "to_y", "over_y", "over_z")

    def gathered():
        return jnp.concatenate(
            at.drop("part", "sides", "corner", "core_own", "core_sides", "core_corner"), axis=0
        )

    def before_sum(partial):
        mine, theirs = partial.reshape(2, 4, part_rows, -1)
        at.mine, at.mine_corner = mine[:3], mine[3]
        at.theirs, at.theirs_corner = theirs[:3], theirs[3]

    def between_core_and_corners():
        corner = wide(at.drop("mine_corner")[0]) + wide(at.drop("got_corner")[0])
        at.to_z, at.to_y = low(corner[:middle]), low(corner[middle:])

    def sum_corners():
        at.corner_top = flip(at.to_z, "ctx", 1)
        at.corner_end = flip(at.to_y, "tp", 2)

    def between_corners_and_sides():
        sums, top, end = at.drop("sums", "corner_top", "corner_end")
        own, over_y, over_z = sums
        at.over_y = low(jnp.concatenate([over_y[:middle] + wide(top), over_y[middle:]], axis=0))
        at.over_z = low(jnp.concatenate([over_z[:middle], over_z[middle:] + wide(end)], axis=0))
        at.part = own
        at.drop("theirs", "theirs_corner", "to_z", "to_y")

    def sum_sides():
        at.got_y, at.got_z = flip(at.over_y, "tp", 2), flip(at.over_z, "ctx", 1)

    def summed():
        own, got_y, got_z = at.drop("part", "got_y", "got_z")
        at.drop("over_y", "over_z")
        return own + wide(got_y) + wide(got_z)

    residual = inputs_part + (at.kept + wide(at.got))
    at.drop("kept", "got", "sent")
    scale_two = lax.rsqrt(jnp.mean(residual * residual, axis=-1, keepdims=True) + epsilon)
    at.residual = residual
    at.part = low(residual * scale_two * gain_mlp)
    at.down_quarters = quarters(at.down_pair)
    at.next()
    residual = at.residual
    gather_sides()
    at.down_x = over_fsdp(at.down_pair)
    at.far_5 = flip(at.down_quarters[0], "ctx", 2)
    at.up_a, at.up_b = at.far_3[quarter_rows:], at.far_4
    gate_a, gate_b, gate_z = at.drop("gate_a", "gate_b", "gate_z")
    at.gate_full = mlp_placed([jnp.stack(pair) for pair in zip(gate_a, gate_b)], gate_z)
    at.next()
    between_sides_and_corners()
    at.next()
    gather_corners()
    at.up_a = over_fsdp(at.up_a)
    at.far_6 = flip(at.down_quarters[1], "ctx", 2)
    at.next()
    between_corners_and_core()
    at.next()
    at.core_corner = flip(at.corner, "tp", 1)
    at.next()
    at.normed_two = gathered()
    at.gate_proj = nn(at.normed_two, at.gate_full)
    at.up_b = over_fsdp(at.up_b)
    at.far_7 = flip(at.down_quarters[2], "ctx", 2)
    at.down_a = jnp.concatenate([at.far_5, at.far_6], axis=0)
    at.next()
    gate_full = at.gate_full
    up_a, up_b = at.drop("up_a", "up_b")
    up_z = [jnp.stack(pair) for pair in zip(up_a, up_b)]
    up_full = mlp_placed(at.drop("up_x")[0], up_z)
    at.up_proj = nn(at.normed_two, up_full)
    at.down_a = over_fsdp(at.down_a)
    at.far_8 = flip(at.down_quarters[3], "ctx", 2)
    at.next()
    at.down_b = jnp.concatenate([at.far_7, at.far_8], axis=0)
    at.next()
    gate_proj, up_proj = at.gate_proj, at.up_proj
    at.hidden_act = low(gelu_tanh(gate_proj) * up_proj)
    at.down_b = over_fsdp(at.down_b)
    at.next()
    at.drop("far_1", "far_2", "far_3", "far_4", "far_5", "far_6", "far_7", "gate_pair", "up_pair")
    at.drop("far_8", "gate_other", "up_far", "down_quarters", "mixed_far")
    at.drop("down_pair")
    down_x, down_a, down_b = at.drop("down_x", "down_a", "down_b")
    down_z = [jnp.stack(pair) for pair in zip(down_a, down_b)]
    down_full = mlp_placed(down_x, down_z)
    before_sum(low(nt(at.hidden_act, down_full)))
    at.next()
    at.got_corner = flip(at.theirs_corner, "tp", 1)
    at.next()
    between_core_and_corners()
    at.next()
    sum_corners()
    at.sums = wide(at.drop("mine")[0]) + wide(flip(at.theirs, "tp", 1))
    at.next()
    between_corners_and_sides()
    at.next()
    sum_sides()
    gate_proj, up_proj = at.drop("gate_proj", "up_proj")
    activated, gelu_back = jax.vjp(gelu_tanh, gate_proj)
    at.activated, at.slope = low(activated), low(gelu_back(up_proj)[0])
    at.next()
    at.ffn_parts = at.drop("part", "got_y", "got_z")
    at.drop("over_y", "over_z")
    my_length = lengths[fsdp_rank]
    part_positions = ctx_rank * rows + tp_rank * part_rows + jnp.arange(part_rows)
    valid = wide(part_positions < my_length)[:, None]
    count = wide(jnp.sum(lengths))
    d_scale = lengths.shape[0] * ctx_count * rows / count

    def outputs_of(residual, ffn_parts):
        own, got_y, got_z = ffn_parts
        output = (residual + (own + wide(got_y) + wide(got_z))) * valid
        return output, output - wide(teacher[0])

    at.part = low(valid * outputs_of(residual, at.ffn_parts)[1] * d_scale)
    at.next()
    output, mismatch = outputs_of(at.residual, at.drop("ffn_parts")[0])
    loss_part = jnp.sum(valid * mismatch * mismatch)
    at.d_output = valid * mismatch * d_scale
    at.output_low = low(output)
    gather_sides()
    at.next()
    between_sides_and_corners()
    at.next()
    gather_corners()
    at.next()
    between_corners_and_core()
    at.next()
    at.core_corner = flip(at.corner, "tp", 1)
    at.next()

    def terms(blocks_of, axis):
        count, rank = lax.axis_size(axis), lax.axis_index(axis)
        return [blocks_of((rank - step) % count) for step in range(1, count + 1)]

    def around(sent, axis):
        moving = ring(sent[0], axis)
        for term in sent[1:-1]:
            moving = ring(low(wide(moving) + wide(term)), axis)
        return moving

    def with_own(sent, arrived):
        return wide(sent[-1]) + wide(arrived)

    def far_and_own(grad):
        blocks = grad.reshape(fsdp_count, 2, 2, -1, half)
        return [
            terms(lambda owner: take(take(blocks, owner), high), "fsdp")
            for high in (1 - hi_rank, hi_rank)
        ]

    def blocks_of(grad):
        blocks = grad.reshape(fsdp_count, 2, 2, -1, half)
        return [
            terms(lambda owner: take(take(blocks, owner), high)[lo], "fsdp")
            for high in (1 - hi_rank, hi_rank)
            for lo in range(2)
        ]

    def near_split(mine):
        return wide(take(mine, lo_rank)), low(take(mine, 1 - lo_rank))

    def near_joined(kept, got):
        near, rest_of = swapped([kept, wide(got)], lo_rank)
        return jnp.concatenate([near, rest_of[:, :rest]], axis=1)

    at.d_ffn = gathered()
    at.down_terms = blocks_of(low(tn(at.d_ffn, at.hidden_act)))
    at.next()
    at.down_x = [around(at.down_terms[0], "fsdp")]
    d_hidden = nn(at.d_ffn, down_full)
    at.d_gate = low(d_hidden * wide(at.slope))
    at.d_up = low(d_hidden * wide(at.activated))
    at.next()
    at.drop("d_ffn", "hidden_act", "slope", "activated")
    at.down_x += [around(at.down_terms[1], "fsdp")]
    at.gate_terms = blocks_of(low(tn(at.normed_two, at.d_gate)))
    at.next()
    at.down_far = [low(with_own(at.down_terms[i], at.down_x[i])) for i in range(2)]
    at.next()
    at.down_x += [around(at.down_terms[2], "fsdp"), around(at.down_terms[3], "fsdp")]
    at.down_got_0 = flip(at.down_far[0], "ctx", 2)
    before_sum(low(nt(at.d_gate, gate_full) + nt(at.d_up, up_full)))
    at.next()
    at.got_corner = flip(at.theirs_corner, "tp", 1)
    at.next()
    between_core_and_corners()
    at.drop("d_gate")
    at.down_rest = jnp.split(at.down_far[1], 2)
    at.next()
    sum_corners()
    at.sums = wide(at.drop("mine")[0]) + wide(flip(at.theirs, "tp", 1))
    at.gate_got = [around(at.gate_terms[0], "fsdp")]
    at.down_got_1 = flip(at.down_rest[0], "ctx", 2)
    at.next()
    between_corners_and_sides()
    at.next()
    sum_sides()
    down_terms, down_x = at.drop("down_terms", "down_x")
    at.down_own = jnp.stack([low(with_own(down_terms[i], down_x[i])) for i in (2, 3)])
    at.gate_got += [around(at.gate_terms[1], "fsdp"), around(at.gate_terms[2], "fsdp")]
    at.down_got_2 = flip(at.down_rest[1], "ctx", 2)
    up_blocks = low(tn(at.normed_two, at.d_up)).reshape(fsdp_count, 2, 2, -1, half)
    at.up_first = terms(lambda owner: take(take(up_blocks, owner), 1 - hi_rank)[0], "fsdp")
    at.up_others = terms(
        lambda owner: jnp.concatenate(
            [take(take(up_blocks, owner), 1 - hi_rank)[1:], take(take(up_blocks, owner), hi_rank)]
        ),
        "fsdp",
    )
    at.next()
    at.drop("normed_two", "d_up", "down_far", "down_rest")
    at.gate_far = [low(with_own(at.gate_terms[i], at.gate_got[i])) for i in range(2)]
    d_normed_two = summed()
    scaled = gain_mlp * d_normed_two
    inner_two = jnp.mean(scaled * residual, axis=-1, keepdims=True)
    at.d_residual = at.d_output + scale_two * scaled - residual * scale_two**3 * inner_two
    at.gain_mlp_sums = jnp.sum(d_normed_two * residual * scale_two, axis=0)
    at.part = low(at.d_residual)
    at.next()
    at.over_y = flip(at.part, "tp", 2)
    got_0, got_1, got_2 = at.drop("down_got_0", "down_got_1", "down_got_2")
    down_got = jnp.stack([got_0, jnp.concatenate([got_1, got_2], axis=0)])
    at.down_kept, at.down_sent = near_split(wide(at.drop("down_own")[0]) + wide(down_got))
    at.gate_got += [around(at.gate_terms[3], "fsdp")]
    at.up_first_got = around(at.up_first, "fsdp")
    at.gate_far_0 = flip(at.gate_far[0], "ctx", 2)
    at.next()
    at.pair = jnp.stack(at.drop("part", "over_y"))
    at.next()
    at.other = flip(at.pair, "tp", 1)
    at.up_far = jnp.split(low(with_own(*at.drop("up_first", "up_first_got"))), 2)
    gate_terms, gate_got = at.drop("gate_terms", "gate_got")
    at.gate_own = jnp.stack([low(with_own(gate_terms[i], gate_got[i])) for i in (2, 3)])
    at.next()
    pair, other = at.drop("pair", "other")
    d_attn = swapped([pair[0], other[0], pair[1], other[1]], tp_rank)
    at.d_attn = jnp.concatenate(d_attn, axis=0)
    at.next()
    at.down_got = flip(at.down_sent, "ctx", 1)
    live_columns = jnp.repeat(live, head_size).astype(jnp.float32)
    d_attended = low(nn(at.d_attn, out_part) * live_columns)
    out_grad = low(tn(at.d_attn, at.attended))

    own_rows = attn_gain.shape[0]

    def split_sums(columns):
        rounded = low(columns)
        return jnp.concatenate([rounded, low(columns - wide(rounded))], axis=-1)

    def joined_sums(columns):
        return columns[..., :64] + columns[..., 64:]

    def to_tp_back(mine):
        blocks = low(mine).reshape(tp_count, own_rows, -1)
        return [take(blocks, tp_rank ^ bit) for bit in range(tp_count)]

    def by_rows(grad):
        return grad.reshape(fsdp_count, ctx_count, tp_count * own_rows, -1)

    def halves_of(grad):
        grad = by_rows(grad)
        turned = [take(grad, (ctx_rank - by) % ctx_count, 1) for by in range(1, ctx_count + 1)]
        pairs = [jnp.stack(turned[:2], axis=1), jnp.stack(turned[2:], axis=1)]
        return [terms(lambda owner: take(pair, owner), "fsdp") for pair in pairs]

    at.out_terms = halves_of(out_grad)
    at.d_queries, at.d_keyvals = attention_backward(
        queries, keyvals, d_attended, first_key, head_size
    )
    at.up_others_got = around(at.up_others, "fsdp")
    at.gate_far_1 = flip(at.gate_far[1], "ctx", 2)
    at.up_far_0 = flip(at.up_far[0], "ctx", 2)
    at.next()
    at.drop("attended", "d_attn", "down_sent")
    kv_blocks = jnp.stack(jnp.split(at.d_keyvals, tp_count, axis=1)).reshape(2, 2, -1, kv_width)
    at.kv_kept, at.kv_sent = take(kv_blocks, core_rank, 1), take(kv_blocks, 1 - core_rank, 1)
    at.drop("d_keyvals")
    at.next()
    at.kv_got = flip(at.kv_sent, "tp", 1)
    up_others, up_others_got = at.drop("up_others", "up_others_got")
    up_rest = jnp.split(low(wide(up_others[-1][0]) + wide(up_others_got[0])), 2)
    at.up_mixed = jnp.concatenate([at.up_far[1], up_rest[0]], axis=0)
    at.up_last = up_rest[1]
    at.up_own, at.up_own_got = up_others[-1][1:], up_others_got[1:]
    gate_far_got = jnp.stack(at.drop("gate_far_0", "gate_far_1"))
    at.gate_kept, at.gate_sent = near_split(wide(at.drop("gate_own")[0]) + wide(gate_far_got))
    at.drop("gate_far")
    at.next()
    kv_sum = wide(at.kv_kept) + wide(at.kv_got)
    at.kv_kept, at.kv_sent = take(kv_sum, y_rank), low(take(kv_sum, 1 - y_rank))
    at.next()
    at.kv_got = flip(at.kv_sent, "tp", 2)
    at.up_far_1 = flip(at.up_mixed, "ctx", 2)
    at.gate_near = flip(at.gate_sent, "ctx", 1)
    at.down_out = near_joined(*at.drop("down_kept", "down_got")).T
    at.up_own = low(wide(at.up_own) + wide(at.drop("up_own_got")[0]))
    at.out_got = [around(at.out_terms[0], "fsdp")]
    d_query_raw = turn(
        at.d_queries.reshape(rows, slot_count, head_size) * query_scale,
        cosine[:, None, :],
        -sine[:, None, :],
    )
    at.d_query_low = low(d_query_raw.reshape(rows, slot_width))
    at.query_terms = halves_of(low(tn(normed, at.d_query_low)))
    at.next()
    at.drop("d_queries", "kv_sent")
    kv_sum = (at.drop("kv_kept")[0] + wide(at.drop("kv_got")[0])).reshape(reach_back + 1, rows, -1)
    at.kv_low = [low(kv_sum[reach_back - by]) for by in range(1, reach_back + 1)]
    at.d_kv = kv_sum[reach_back]
    at.out_1 = low(with_own(at.out_terms[0], at.out_got[0]))
    at.next()
    at.kv_got = [shifted(at.kv_low[by - 1], "ctx", -by) for by in range(1, reach_back + 1)]
    at.out_got += [around(at.out_terms[1], "fsdp")]
    at.next()
    d_kv = at.d_kv
    for got in at.drop("kv_got")[0]:
        d_kv = d_kv + wide(got)
    d_kv_low = low(turn(d_kv, kv_cosine, -kv_sine))
    at.d_qkv = jnp.concatenate(
        [at.d_query_low, jnp.pad(d_kv_low, ((0, 0), (0, kv_width)))], axis=1
    )
    at.next()
    at.query_got = [around(at.query_terms[0], "fsdp")]
    at.up_far_2 = flip(at.up_last, "ctx", 2)
    at.out_z = ring(at.out_1[0], "ctx")
    at.partial = low(nt(at.d_qkv, qkv_part))
    at.next()
    partial = at.partial
    blocks = partial.reshape(2, 2, part_rows, -1)
    at.kept, at.sent = take(blocks, core_rank, 1), take(blocks, 1 - core_rank, 1)
    at.next()
    at.drop("d_query_low", "kv_low", "d_kv", "gate_sent")
    at.query_1 = low(with_own(at.query_terms[0], at.query_got[0]))
    at.out_2 = with_own(at.out_terms[1], at.out_got[1])
    at.out_z = low(wide(at.out_z) + wide(at.out_1[1]))
    at.got = flip(at.sent, "tp", 1)
    at.out_z = ring(at.out_z, "ctx")
    gain_attn_sums = jnp.sum(wide(at.partial) * inputs * scale_one, axis=0)
    sums = [gain_attn_sums, at.gain_mlp_sums, jnp.full(gain_attn_sums.shape, loss_part)]
    columns = jnp.pad(jnp.stack(sums, axis=1), ((0, 0), (0, 61)))
    kv_grad = jnp.concatenate([low(tn(normed, at.d_qkv[:, slot_width : slot_width + kv_width])), split_sums(columns)], axis=1)
    at.kv_terms = terms(lambda owner: take(by_rows(kv_grad), owner), "fsdp")
    at.next()
    summed_rows = wide(at.kept) + wide(at.got)
    at.kept, at.sent = take(summed_rows, y_rank), low(take(summed_rows, 1 - y_rank))
    at.out_z = low(wide(at.out_z) + at.out_2[0])
    at.next()
    at.got = flip(at.sent, "tp", 2)
    at.query_got += [around(at.query_terms[1], "fsdp")]
    got = at.drop("up_far_0", "up_far_1", "up_far_2")
    up_far_got = jnp.concatenate(got, axis=0).reshape(2, -1, half)
    at.up_kept, up_sent = near_split(wide(at.up_own) + wide(up_far_got))
    at.up_sent = jnp.split(up_sent, 2)
    at.gate_out = near_joined(*at.drop("gate_kept", "gate_near"))
    at.query_z = ring(at.query_1[0], "ctx")
    at.out_z = ring(at.out_z, "ctx")
    at.next()
    at.query_z = low(wide(at.query_z) + wide(at.query_1[1]))
    at.next()
    at.query_2 = with_own(at.query_terms[1], at.query_got[1])
    at.d_normed = at.kept + wide(at.got)
    at.drop("partial", "d_qkv")
    at.drop("query_1", "kept", "sent", "got", "up_far", "up_mixed", "up_last", "up_own")
    at.drop("query_terms", "query_got")
    at.drop("out_terms", "out_got")
    at.query_z = ring(at.query_z, "ctx")
    at.kv_got = around(at.kv_terms, "fsdp")
    at.up_near = flip(at.up_sent[0], "ctx", 1)
    at.out_back = to_tp_back(wide(at.out_z) + at.out_2[1])
    at.next()
    at.query_z = low(wide(at.query_z) + at.query_2[0])
    kv_mine = with_own(*at.drop("kv_terms", "kv_got"))
    kv_mine = jnp.concatenate(
        [low(kv_mine[..., :kv_width]), split_sums(joined_sums(kv_mine[..., kv_width:]))], axis=-1
    )
    at.kv_own = take(kv_mine, ctx_rank)
    at.kv_sent = [take(kv_mine, (ctx_rank + by) % ctx_count) for by in range(1, ctx_count)]

    at.next()
    at.drop("out_z", "out_2")
    at.out_back = flip_tp(at.out_back)
    at.query_z = ring(at.query_z, "ctx")
    at.kv_got = [ring(at.kv_sent[by - 1], "ctx", by) for by in range(1, ctx_count)]
    at.next()
    query_mine = low(wide(at.query_z) + at.query_2[1])
    kv_mine = sum([wide(got) for got in at.kv_got], wide(at.kv_own))
    kv_mine = jnp.concatenate(
        [low(kv_mine[:, :kv_width]), split_sums(joined_sums(kv_mine[:, kv_width:]))], axis=1
    )
    at.back = to_tp_back(jnp.concatenate([query_mine, kv_mine], axis=1))
    at.next()
    up_near = jnp.concatenate([at.up_near, flip(at.up_sent[1], "ctx", 1)], axis=0)
    at.drop("query_z", "query_2", "kv_got", "kv_own", "kv_sent", "up_sent")

    def whole_heads(parts):
        columns = []
        for rank, part in enumerate(parts):
            first = rank * (slot_count - 1) + min(rank, fuller)
            base = min(first, head_count - slot_count)
            held = slot_count - 1 + (1 if rank < fuller else 0)
            start = (first - base) * head_size
            columns.append(wide(part[:, start : start + held * head_size]))
        return jnp.concatenate(columns, axis=1)

    parts = swapped(flip_tp(at.back), tp_rank)
    query_grad = whole_heads([part[:, :slot_width] for part in parts])
    out_grad = whole_heads(swapped(at.out_back, tp_rank))
    kv_parts = [wide(part[:, slot_width:]) for part in parts]
    kv_grad = jnp.concatenate([part[:, :kv_width] for part in kv_parts], axis=1)
    sums = joined_sums(sum(part[:, kv_width:] for part in kv_parts))
    gain_attn_grad, gain_mlp_grad, loss_sum = sums[:, 0], sums[:, 1], sums[0, 2]
    down_grad, gate_grad = at.down_out, at.gate_out
    up_grad = near_joined(at.up_kept, up_near)
    loss = loss_sum / (count * width)
    d_normed, d_residual = at.d_normed, at.d_residual
    scale_part = lax.dynamic_slice_in_dim(scale_one, tp_rank * part_rows, part_rows, 0)
    scaled = gain_attn * d_normed
    inner_one = jnp.mean(scaled * inputs_part, axis=-1, keepdims=True)
    input_grad = d_residual + scale_part * scaled - inputs_part * scale_part**3 * inner_one
    return (
        at.output_low[None],
        loss,
        input_grad[None],
        gain_attn_grad,
        query_grad,
        kv_grad,
        out_grad,
        gain_mlp_grad,
        gate_grad,
        up_grad,
        down_grad,
    )


def solution(mesh):
    in_specs = (
        P("fsdp", "ctx", None),
        P(),
        P("fsdp", ("ctx", "tp"), None),
        P(("fsdp", "ctx", "tp")),
        P(("fsdp", "ctx", "tp"), None),
        P(("fsdp", "ctx", "tp"), None),
        P(("fsdp", "ctx", "tp"), None),
        P(("fsdp", "ctx", "tp")),
        P(("fsdp", "ctx"), "tp"),
        P(("fsdp", "ctx"), "tp"),
        P("tp", ("fsdp", "ctx")),
    )
    out_specs = (
        P("fsdp", ("ctx", "tp"), None),
        P(),
        P("fsdp", ("ctx", "tp"), None),
        P(("fsdp", "ctx", "tp")),
        P(("fsdp", "ctx", "tp"), None),
        P(("fsdp", "ctx", "tp"), None),
        P(("fsdp", "ctx", "tp"), None),
        P(("fsdp", "ctx", "tp")),
        P(("fsdp", "ctx"), "tp"),
        P(("fsdp", "ctx"), "tp"),
        P("tp", ("fsdp", "ctx")),
    )
    return jax.shard_map(local, mesh=mesh, in_specs=in_specs, out_specs=out_specs, check_vma=False)
```

```python
import jax
import jax.numpy as jnp
from jax import lax
from jax.experimental import pallas as pl
from jax.experimental.pallas import tpu as pltpu
from jax.sharding import PartitionSpec as P

W = 2048

epsilon = 1e-06
lowest = -1e30
ROWS = 256
VMEM_BYTES = 40 * 1024 * 1024


def flip(array, axis, bit):
    return lax.ppermute(array, axis, [(i, i ^ bit) for i in range(lax.axis_size(axis))])


def ring(array, axis, by=1):
    count = lax.axis_size(axis)
    return lax.ppermute(array, axis, [(i, (i + by) % count) for i in range(count)])


def shifted(array, axis, by):
    count = lax.axis_size(axis)
    pairs = [(i, i + by) for i in range(count) if 0 <= i + by < count]
    return lax.ppermute(array, axis, pairs)


class Steps:
    def next(self):
        self.__dict__.update(lax.optimization_barrier(dict(self.__dict__)))

    def drop(self, *names):
        return [self.__dict__.pop(name) for name in names]


def sync(*trees):
    return lax.optimization_barrier(trees)


def after(array, *others):
    return lax.optimization_barrier((array, others))[0]


def low(values):
    return values.astype(jnp.bfloat16)


def wide(values):
    return values.astype(jnp.float32)


def take(array, index, axis=0):
    return lax.dynamic_index_in_dim(array, index, axis, keepdims=False)


def swapped(blocks, rank):
    if len(blocks) == 2:
        odd = rank == 1
        return [jnp.where(odd, blocks[1], blocks[0]), jnp.where(odd, blocks[0], blocks[1])]
    first = swapped(blocks[:2], rank % 2) + swapped(blocks[2:], rank % 2)
    outer = rank // 2 == 1
    return [jnp.where(outer, first[i ^ 2], first[i]) for i in range(4)]


def place(pieces, slots):
    count = len(pieces)
    shape = pieces[0].shape

    def body(slots_ref, *refs):
        out_ref, held, came, left = refs[count:]
        into = [pltpu.make_async_copy(refs[k], held.at[k], came.at[k]) for k in range(count)]
        out_of = [
            pltpu.make_async_copy(held.at[k], out_ref.at[slots_ref[k]], left.at[k])
            for k in range(count)
        ]
        for copy in into:
            copy.start()
        for first, second in zip(into, out_of):
            first.wait()
            second.start()
        for copy in out_of:
            copy.wait()

    return pl.pallas_call(
        body,
        out_shape=jax.ShapeDtypeStruct((count,) + shape, pieces[0].dtype),
        grid_spec=pltpu.PrefetchScalarGridSpec(
            num_scalar_prefetch=1,
            grid=(1,),
            in_specs=[pl.BlockSpec(memory_space=pl.ANY)] * count,
            out_specs=pl.BlockSpec(memory_space=pl.ANY),
            scratch_shapes=[
                pltpu.VMEM((count,) + shape, pieces[0].dtype),
                pltpu.SemaphoreType.DMA((count,)),
                pltpu.SemaphoreType.DMA((count,)),
            ],
        ),
        compiler_params=pltpu.CompilerParams(vmem_limit_bytes=VMEM_BYTES),
        cost_estimate=pl.CostEstimate(
            flops=0, bytes_accessed=4 * count * pieces[0].size, transcendentals=0
        ),
        name="place",
    )(jnp.stack(slots).astype(jnp.int32), *pieces)


def nn(first, second):
    return lax.dot_general(
        first, second, (((1,), (0,)), ((), ())), preferred_element_type=jnp.float32
    )


def nt(first, second):
    return lax.dot_general(
        first, second, (((1,), (1,)), ((), ())), preferred_element_type=jnp.float32
    )


def tn(first, second):
    return lax.dot_general(
        first, second, (((0,), (0,)), ((), ())), preferred_element_type=jnp.float32
    )


def ring_sum(block_of, axis):
    count = lax.axis_size(axis)
    rank = lax.axis_index(axis)
    moving = None
    for step in range(1, count):
        term = block_of((rank - step) % count)
        moving = low(term if moving is None else wide(moving) + wide(term))
        moving = ring(moving, axis)
    own = wide(block_of(rank))
    return own if moving is None else own + wide(moving)


def attention_forward(queries, keyvals, live, first_key, head_size):
    rows, columns = queries.shape
    heads = columns // head_size
    reach = W + ROWS
    lead = keyvals.shape[0] - rows - W

    def body(info_ref, q_ref, kv_ref, o_ref):
        head, block = pl.program_id(0), pl.program_id(1)
        start = pl.multiple_of(lead + block * ROWS, ROWS)
        keys = kv_ref[pl.ds(start, reach), :head_size]
        vals = kv_ref[pl.ds(start, reach), head_size:]
        scores = nt(q_ref[...], keys)
        row = lax.broadcasted_iota(jnp.int32, scores.shape, 0)
        column = lax.broadcasted_iota(jnp.int32, scores.shape, 1)
        ahead = column - row
        allowed = (ahead > 0) & (ahead <= W) & (column >= info_ref[0] - start)
        scores = jnp.where(allowed, scores, lowest)
        peak = jnp.max(scores, axis=1, keepdims=True)
        shares = jnp.exp(scores - peak)
        total = jnp.sum(shares, axis=1, keepdims=True)
        probs = low(shares * (1.0 / total))
        mixed = nn(probs, vals)
        o_ref[...] = low(mixed * wide(info_ref[1 + head]))

    return pl.pallas_call(
        body,
        out_shape=jax.ShapeDtypeStruct((rows, columns), jnp.bfloat16),
        grid_spec=pltpu.PrefetchScalarGridSpec(
            num_scalar_prefetch=1,
            grid=(heads, rows // ROWS),
            in_specs=[
                pl.BlockSpec((ROWS, head_size), lambda h, i, info: (i, h)),
                pl.BlockSpec(keyvals.shape, lambda h, i, info: (0, 0)),
            ],
            out_specs=pl.BlockSpec((ROWS, head_size), lambda h, i, info: (i, h)),
        ),
        compiler_params=pltpu.CompilerParams(vmem_limit_bytes=VMEM_BYTES),
        cost_estimate=pl.CostEstimate(
            flops=4 * heads * rows * reach * head_size,
            bytes_accessed=4 * rows * columns + 2 * keyvals.size,
            transcendentals=heads * rows * reach,
        ),
        name="attention_forward",
    )(jnp.concatenate([first_key[None], live]).astype(jnp.int32), queries, keyvals)


def attention_backward(queries, keyvals, d_attended, first_key, head_size):
    rows, columns = queries.shape
    heads = columns // head_size
    reach = W + ROWS
    span = keyvals.shape[0]
    lead = span - rows - W

    def body(info_ref, q_ref, kv_ref, do_ref, dq_ref, dkv_ref, sums):
        head, block = pl.program_id(0), pl.program_id(1)

        @pl.when((head == 0) & (block == 0))
        def _():
            sums[...] = jnp.zeros_like(sums)

        start = pl.multiple_of(lead + block * ROWS, ROWS)
        keys = kv_ref[pl.ds(start, reach), :head_size]
        vals = kv_ref[pl.ds(start, reach), head_size:]
        query = q_ref[...]
        d_out = do_ref[...]
        scores = nt(keys, query)
        column = lax.broadcasted_iota(jnp.int32, scores.shape, 0)
        row = lax.broadcasted_iota(jnp.int32, scores.shape, 1)
        ahead = column - row
        allowed = (ahead > 0) & (ahead <= W) & (column >= info_ref[0] - start)
        scores = jnp.where(allowed, scores, lowest)
        peak = jnp.max(scores, axis=0, keepdims=True)
        shares = jnp.exp(scores - peak)
        total = jnp.sum(shares, axis=0, keepdims=True)
        probs = shares * (1.0 / total)
        d_probs = nt(vals, d_out)
        inner = jnp.sum(probs * d_probs, axis=0, keepdims=True)
        d_scores = low(probs * (d_probs - inner))
        dq_ref[...] = tn(d_scores, keys)
        sums[pl.ds(start, reach), :head_size] += nn(d_scores, query)
        sums[pl.ds(start, reach), head_size:] += nn(low(probs), d_out)

        @pl.when((head == heads - 1) & (block == rows // ROWS - 1))
        def _():
            dkv_ref[...] = low(sums[...])

    return pl.pallas_call(
        body,
        out_shape=(
            jax.ShapeDtypeStruct((rows, columns), jnp.float32),
            jax.ShapeDtypeStruct(keyvals.shape, jnp.bfloat16),
        ),
        grid_spec=pltpu.PrefetchScalarGridSpec(
            num_scalar_prefetch=1,
            grid=(heads, rows // ROWS),
            in_specs=[
                pl.BlockSpec((ROWS, head_size), lambda h, i, info: (i, h)),
                pl.BlockSpec(keyvals.shape, lambda h, i, info: (0, 0)),
                pl.BlockSpec((ROWS, head_size), lambda h, i, info: (i, h)),
            ],
            out_specs=(
                pl.BlockSpec((ROWS, head_size), lambda h, i, info: (i, h)),
                pl.BlockSpec(keyvals.shape, lambda h, i, info: (0, 0)),
            ),
            scratch_shapes=[pltpu.VMEM(keyvals.shape, jnp.float32)],
        ),
        compiler_params=pltpu.CompilerParams(vmem_limit_bytes=VMEM_BYTES),
        cost_estimate=pl.CostEstimate(
            flops=10 * heads * rows * reach * head_size,
            bytes_accessed=8 * rows * columns + 4 * keyvals.size,
            transcendentals=heads * rows * reach,
        ),
        name="attention_backward",
    )(first_key[None].astype(jnp.int32), queries, keyvals, d_attended)


def gelu_tanh(values):
    return jax.nn.gelu(values, approximate=True)


def local(
    hidden,
    lengths,
    teacher,
    attn_gain,
    query_weight,
    kv_weight,
    out_weight,
    mlp_gain,
    gate_weight,
    up_weight,
    down_weight,
):
    tp_count = lax.axis_size("tp")
    ctx_count = lax.axis_size("ctx")
    fsdp_count = lax.axis_size("fsdp")
    tp_rank = lax.axis_index("tp")
    ctx_rank = lax.axis_index("ctx")
    fsdp_rank = lax.axis_index("fsdp")
    y_rank, core_rank = tp_rank // 2, tp_rank % 2
    hi_rank, lo_rank = ctx_rank // 2, ctx_rank % 2
    seq_count, rows, width = hidden.shape
    assert seq_count == 1 and tp_count == 4 and ctx_count == 4
    part_rows = rows // tp_count
    head_size = kv_weight.shape[1] // 2
    head_count = query_weight.shape[1] // head_size
    slot_count = -(-head_count // tp_count)
    slot_width = slot_count * head_size
    fuller = head_count - (slot_count - 1) * tp_count
    kv_width = 2 * head_size // tp_count

    def first_head_of(rank):
        return rank * (slot_count - 1) + jnp.minimum(rank, fuller)

    def slot_base_of(rank):
        return jnp.minimum(first_head_of(rank), head_count - slot_count)

    slot_heads = slot_base_of(tp_rank) + jnp.arange(slot_count)
    first_head = first_head_of(tp_rank)
    held_heads = slot_count - 1 + (tp_rank < fuller).astype(jnp.int32)
    live = ((slot_heads >= first_head) & (slot_heads < first_head + held_heads)).astype(jnp.int32)

    def over_tp(columns_of):
        blocks = [columns_of(tp_rank)]
        for bit in range(1, tp_count):
            blocks.append(flip(columns_of(tp_rank ^ bit), "tp", bit))
        return jnp.concatenate(swapped(blocks, tp_rank), axis=0)

    def over_fsdp(block):
        blocks = [block]
        for _ in range(1, fsdp_count):
            blocks.append(ring(blocks[-1], "fsdp"))
        return blocks

    def placed(by_ctx):
        pieces, slots = [], []
        for step, blocks in enumerate(by_ctx):
            for turn_at, block in enumerate(blocks):
                pieces.append(block)
                slots.append(
                    (fsdp_rank - turn_at) % fsdp_count * ctx_count
                    + (ctx_rank - step) % ctx_count
                )
        return place(pieces, slots).reshape(width, pieces[0].shape[1])

    def head_columns(weight):
        return lambda rank: lax.dynamic_slice_in_dim(
            weight, slot_base_of(rank) * head_size, slot_width, 1
        )

    unit_count = gate_weight.shape[1]
    half = -(-unit_count // 256) * 128
    rest = unit_count - half

    def near_halves(block):
        near, far = block[:, :half], jnp.pad(block[:, half:], ((0, 0), (0, half - rest)))
        mine = jnp.where(lo_rank == 0, near, far)
        theirs = jnp.where(lo_rank == 0, far, near)
        return mine, theirs

    def near_pair(halves):
        mine, theirs = halves
        return jnp.stack(swapped([mine, flip(theirs, "ctx", 1)], lo_rank))

    def quarters(pair):
        return jnp.split(pair.reshape(-1, half), 4)

    def far(pieces):
        if len(pieces) == 1:
            return [flip(pieces[0], "ctx", 2)]
        return jnp.split(flip(jnp.concatenate(pieces, axis=0), "ctx", 2), len(pieces))

    def mlp_placed(own, other):
        pieces, slots = [], []
        for far_bit, blocks in enumerate((own, other)):
            for turn_at, block in enumerate(blocks):
                pieces.append(block.reshape(-1, half))
                slots.append((fsdp_rank - turn_at) % fsdp_count * 2 + (hi_rank ^ far_bit))
        return place(pieces, slots).reshape(width, half)

    inputs_low = hidden[0]
    inputs = wide(inputs_low)
    inputs_part_low = lax.dynamic_slice_in_dim(inputs_low, tp_rank * part_rows, part_rows, 0)
    inputs_part = wide(inputs_part_low)
    scale_one = lax.rsqrt(jnp.mean(inputs * inputs, axis=-1, keepdims=True) + epsilon)
    positions = ctx_rank * rows + jnp.arange(rows)
    quarter = head_size // 4
    frequency = 10000.0 ** (-(jnp.arange(quarter).astype(jnp.float32) * 4.0 / head_size))
    angle = wide(positions)[:, None] * frequency[None, :]
    cosine, sine = jnp.cos(angle), jnp.sin(angle)

    def turn(values, cosine, sine):
        first, second = values[..., :quarter], values[..., quarter : 2 * quarter]
        return jnp.concatenate(
            [
                first * cosine - second * sine,
                second * cosine + first * sine,
                values[..., 2 * quarter :],
            ],
            axis=-1,
        )

    turning = tp_rank == 0
    kv_cosine, kv_sine = jnp.where(turning, cosine, 1.0), jnp.where(turning, sine, 0.0)
    query_scale = head_size ** (-0.5)
    reach_back = min((W - 2) // rows + 1, ctx_count - 1)
    first_key = (reach_back - jnp.minimum(ctx_rank, reach_back)) * rows

    at = Steps()
    gains = jnp.pad(jnp.stack([attn_gain, mlp_gain], axis=1), ((0, 0), (0, 126)))

    def qkv_columns(rank):
        kv = lax.dynamic_slice_in_dim(kv_weight, rank * kv_width, kv_width, 1)
        return jnp.concatenate([head_columns(query_weight)(rank), kv, gains], axis=1)

    def to_tp(columns_of):
        return [columns_of(tp_rank ^ bit) for bit in range(tp_count)]

    def flip_tp(blocks):
        return blocks[:1] + [flip(blocks[bit], "tp", bit) for bit in range(1, tp_count)]

    def from_tp(blocks):
        return jnp.concatenate(swapped(blocks, tp_rank), axis=0)

    def paired(mine, got):
        return jnp.stack(swapped([mine, got], lo_rank))

    at.qkv = to_tp(qkv_columns)
    at.gate_mine, at.gate_sent = near_halves(gate_weight)
    at.out_weight, at.up_weight, at.down_weight = out_weight, up_weight, down_weight
    at.next()
    at.qkv = flip_tp(at.qkv)
    at.gate_got = flip(at.gate_sent, "ctx", 1)
    at.next()
    at.qkv_0 = from_tp(at.drop("qkv")[0])
    at.gate_pair = paired(*at.drop("gate_mine", "gate_got"))
    at.next()
    at.qkv_x = [over_fsdp(at.qkv_0)]
    at.qkv_1 = ring(at.qkv_0, "ctx")
    at.out = to_tp(head_columns(at.drop("out_weight")[0]))
    at.next()
    at.qkv_x.append(over_fsdp(at.qkv_1))
    at.qkv_2 = ring(at.qkv_1, "ctx")
    at.up_mine, at.up_sent = near_halves(at.drop("up_weight")[0])
    at.down_mine, at.down_sent = near_halves(at.drop("down_weight")[0].T)
    at.next()
    at.qkv_x.append(over_fsdp(at.qkv_2))
    at.qkv_3 = ring(at.qkv_2, "ctx")
    at.out = flip_tp(at.out)
    at.next()
    at.out_0 = from_tp(at.drop("out")[0])
    at.drop("qkv_0", "qkv_1", "qkv_2", "gate_sent")
    at.next()
    at.qkv_x.append(over_fsdp(at.qkv_3))
    at.out_1 = ring(at.out_0, "ctx")
    at.next()

    qkv_part = placed(at.drop("qkv_x")[0])
    gain_attn = wide(qkv_part[:, slot_width + kv_width])
    gain_mlp = wide(qkv_part[:, slot_width + kv_width + 1])
    at.normed = low(inputs * scale_one * gain_attn)
    at.qkv_raw = nn(at.normed, qkv_part)
    at.gate_a = over_fsdp(at.gate_pair[0])
    at.out_2 = ring(at.out_1, "ctx")
    at.far_1 = far(quarters(at.gate_pair)[:1])
    at.next()
    (qkv_raw,) = at.drop("qkv_raw")
    kv_raw = qkv_raw[:, slot_width : slot_width + kv_width]
    at.kv_own = low(turn(kv_raw, kv_cosine, kv_sine))
    query_raw = qkv_raw[:, :slot_width].reshape(rows, slot_count, head_size)
    queries = low(turn(query_raw, cosine[:, None, :], sine[:, None, :]) * query_scale)
    at.queries = queries.reshape(rows, slot_width)
    at.gate_b = over_fsdp(at.gate_pair[1])
    at.out_3 = ring(at.out_2, "ctx")
    at.next()
    normed = at.normed
    at.out_near = jnp.stack([at.out_0, at.out_1, at.out_2, at.out_3])
    at.next()
    out_x = over_fsdp(at.out_near)
    at.chunks = [shifted(at.kv_own, "ctx", by) for by in range(reach_back, 0, -1)]
    at.next()
    at.kv_column = jnp.concatenate(at.drop("chunks")[0] + [at.kv_own], axis=0)
    at.gate_far = jnp.concatenate(quarters(at.gate_pair)[1:3], axis=0)
    at.drop("out_0", "out_1", "out_2", "kv_own", "qkv_3")
    at.next()
    at.kv_over_y = flip(at.kv_column, "tp", 2)
    at.down_got = flip(at.down_sent, "ctx", 1)
    at.far_2 = flip(at.gate_far, "ctx", 2)
    at.out_x = out_x
    at.next()
    at.kv_pair = jnp.stack(at.drop("kv_column", "kv_over_y"))
    at.next()
    at.kv_other = flip(at.kv_pair, "tp", 1)
    at.down_pair = paired(*at.drop("down_mine", "down_got"))
    at.down_far = jnp.concatenate(quarters(at.down_pair)[:2], axis=0)
    at.far_0 = far(quarters(at.gate_pair)[3:])
    (out_x,) = at.drop("out_x")
    at.out_part = placed([[block[i] for block in out_x] for i in range(ctx_count)])
    at.next()
    kv_pair, kv_other = at.drop("kv_pair", "kv_other")
    at.keyvals = jnp.concatenate(
        swapped([kv_pair[0], kv_other[0], kv_pair[1], kv_other[1]], tp_rank), axis=1
    )
    at.drop("down_sent", "gate_far", "out_near")
    at.next()

    queries, keyvals = at.queries, at.keyvals
    at.attended = attention_forward(queries, keyvals, live, first_key, head_size)
    blocks = low(nt(at.attended, at.out_part)).reshape(2, 2, part_rows, -1)
    at.kept, at.sent = take(blocks, core_rank, 1), take(blocks, 1 - core_rank, 1)
    at.down_x = over_fsdp(at.down_pair)
    at.up_got = flip(at.up_sent, "ctx", 1)
    at.far_3 = flip(at.down_far, "ctx", 2)
    at.gate_other = jnp.concatenate(
        at.far_1 + [at.far_2] + at.far_0, axis=0
    ).reshape(at.gate_pair.shape)
    at.next()

    out_part = at.out_part
    at.got = flip(at.sent, "tp", 1)
    at.up_pair = paired(*at.drop("up_mine", "up_got"))
    at.up_far = jnp.concatenate(quarters(at.up_pair)[:2], axis=0)
    at.next()
    summed = wide(at.kept) + wide(at.got)
    at.kept, at.sent = take(summed, y_rank), low(take(summed, 1 - y_rank))
    at.next()
    at.got = flip(at.sent, "tp", 2)
    at.gate_z = over_fsdp(at.gate_other)
    at.far_4 = flip(at.up_far, "ctx", 2)
    at.next()

    middle = part_rows // 2

    def gather_sides():
        at.over_y, at.over_z = flip(at.part, "tp", 2), flip(at.part, "ctx", 1)
        at.core_own = flip(at.part, "tp", 1)

    def between_sides_and_corners():
        at.to_z, at.to_y = at.over_y[:middle], at.over_z[middle:]
        at.sides = jnp.concatenate([at.over_y, at.over_z], axis=0)

    def gather_corners():
        at.corner_top = flip(at.to_z, "ctx", 1)
        at.corner_end = flip(at.to_y, "tp", 2)
        at.core_sides = flip(at.sides, "tp", 1)

    def between_corners_and_core():
        at.corner = jnp.concatenate(at.drop("corner_top", "corner_end"), axis=0)
        at.drop("to_z", "to_y", "over_y", "over_z")

    def gathered():
        return jnp.concatenate(
            at.drop("part", "sides", "corner", "core_own", "core_sides", "core_corner"), axis=0
        )

    def before_sum(partial):
        mine, theirs = partial.reshape(2, 4, part_rows, -1)
        at.mine, at.mine_corner = mine[:3], mine[3]
        at.theirs, at.theirs_corner = theirs[:3], theirs[3]

    def between_core_and_corners():
        corner = wide(at.drop("mine_corner")[0]) + wide(at.drop("got_corner")[0])
        at.to_z, at.to_y = low(corner[:middle]), low(corner[middle:])

    def sum_corners():
        at.corner_top = flip(at.to_z, "ctx", 1)
        at.corner_end = flip(at.to_y, "tp", 2)

    def between_corners_and_sides():
        sums, top, end = at.drop("sums", "corner_top", "corner_end")
        own, over_y, over_z = sums
        at.over_y = low(jnp.concatenate([over_y[:middle] + wide(top), over_y[middle:]], axis=0))
        at.over_z = low(jnp.concatenate([over_z[:middle], over_z[middle:] + wide(end)], axis=0))
        at.part = own
        at.drop("theirs", "theirs_corner", "to_z", "to_y")

    def sum_sides():
        at.got_y, at.got_z = flip(at.over_y, "tp", 2), flip(at.over_z, "ctx", 1)

    def summed():
        own, got_y, got_z = at.drop("part", "got_y", "got_z")
        at.drop("over_y", "over_z")
        return own + wide(got_y) + wide(got_z)

    residual = inputs_part + (at.kept + wide(at.got))
    at.drop("kept", "got", "sent")
    scale_two = lax.rsqrt(jnp.mean(residual * residual, axis=-1, keepdims=True) + epsilon)
    at.residual = residual
    at.part = low(residual * scale_two * gain_mlp)
    at.down_quarters = quarters(at.down_pair)
    at.up_quarters = quarters(at.up_pair)
    at.next()
    residual = at.residual
    gather_sides()
    at.up_x = over_fsdp(at.up_pair)
    at.far_5 = flip(at.up_quarters[2], "ctx", 2)
    at.down_a = at.far_3
    gate_a, gate_b, gate_z = at.drop("gate_a", "gate_b", "gate_z")
    at.gate_full = mlp_placed([jnp.stack(pair) for pair in zip(gate_a, gate_b)], gate_z)
    at.next()
    between_sides_and_corners()
    at.next()
    gather_corners()
    at.up_a = over_fsdp(at.far_4)
    at.far_6 = flip(at.up_quarters[3], "ctx", 2)
    at.next()
    between_corners_and_core()
    at.up_b = jnp.concatenate([at.far_5, at.far_6], axis=0)
    at.next()
    at.core_corner = flip(at.corner, "tp", 1)
    at.next()
    at.normed_two = gathered()
    at.gate_proj = nn(at.normed_two, at.gate_full)
    at.up_b = over_fsdp(at.up_b)
    at.far_7 = flip(at.down_quarters[2], "ctx", 2)
    at.next()
    gate_full = at.gate_full
    up_a, up_b = at.drop("up_a", "up_b")
    up_z = [jnp.stack(pair) for pair in zip(up_a, up_b)]
    up_full = mlp_placed(at.drop("up_x")[0], up_z)
    at.up_proj = nn(at.normed_two, up_full)
    at.down_a = over_fsdp(at.down_a)
    at.far_8 = flip(at.down_quarters[3], "ctx", 2)
    at.next()
    at.down_b = jnp.concatenate([at.far_7, at.far_8], axis=0)
    at.next()
    gate_proj, up_proj = at.gate_proj, at.up_proj
    at.hidden_act = low(gelu_tanh(gate_proj) * up_proj)
    at.down_b = over_fsdp(at.down_b)
    at.next()
    at.drop("far_1", "far_2", "far_3", "far_4", "far_5", "far_6", "far_7", "gate_pair", "up_pair")
    at.drop("far_8", "gate_other", "up_far", "down_quarters", "up_quarters", "down_far", "up_sent", "far_0")
    at.drop("down_pair")
    down_x, down_a, down_b = at.drop("down_x", "down_a", "down_b")
    down_z = [jnp.stack(pair) for pair in zip(down_a, down_b)]
    down_full = mlp_placed(down_x, down_z)
    before_sum(low(nt(at.hidden_act, down_full)))
    at.next()
    at.got_corner = flip(at.theirs_corner, "tp", 1)
    at.next()
    between_core_and_corners()
    at.next()
    sum_corners()
    at.sums = wide(at.drop("mine")[0]) + wide(flip(at.theirs, "tp", 1))
    at.next()
    between_corners_and_sides()
    at.next()
    sum_sides()
    gate_proj, up_proj = at.drop("gate_proj", "up_proj")
    activated, gelu_back = jax.vjp(gelu_tanh, gate_proj)
    at.activated, at.slope = low(activated), low(gelu_back(up_proj)[0])
    at.next()
    at.ffn_parts = at.drop("part", "got_y", "got_z")
    at.drop("over_y", "over_z")
    my_length = lengths[fsdp_rank]
    part_positions = ctx_rank * rows + tp_rank * part_rows + jnp.arange(part_rows)
    valid = wide(part_positions < my_length)[:, None]
    count = wide(jnp.sum(lengths))
    d_scale = lengths.shape[0] * ctx_count * rows / count

    def outputs_of(residual, ffn_parts):
        own, got_y, got_z = ffn_parts
        output = (residual + (own + wide(got_y) + wide(got_z))) * valid
        return output, output - wide(teacher[0])

    at.part = low(valid * outputs_of(residual, at.ffn_parts)[1] * d_scale)
    at.next()
    output, mismatch = outputs_of(at.residual, at.drop("ffn_parts")[0])
    loss_part = jnp.sum(valid * mismatch * mismatch)
    at.d_output = valid * mismatch * d_scale
    at.output_low = low(output)
    gather_sides()
    at.next()
    between_sides_and_corners()
    at.next()
    gather_corners()
    at.next()
    between_corners_and_core()
    at.next()
    at.core_corner = flip(at.corner, "tp", 1)
    at.next()

    def terms(blocks_of, axis):
        count, rank = lax.axis_size(axis), lax.axis_index(axis)
        return [blocks_of((rank - step) % count) for step in range(1, count + 1)]

    def around(sent, axis):
        moving = ring(sent[0], axis)
        for term in sent[1:-1]:
            moving = ring(low(wide(moving) + wide(term)), axis)
        return moving

    def with_own(sent, arrived):
        return wide(sent[-1]) + wide(arrived)

    def far_and_own(grad):
        blocks = grad.reshape(fsdp_count, 2, 2, -1, half)
        return [
            terms(lambda owner: take(take(blocks, owner), high), "fsdp")
            for high in (1 - hi_rank, hi_rank)
        ]

    def blocks_of(grad):
        blocks = grad.reshape(fsdp_count, 2, 2, -1, half)
        return [
            terms(lambda owner: take(take(blocks, owner), high)[lo], "fsdp")
            for high in (1 - hi_rank, hi_rank)
            for lo in range(2)
        ]

    def near_split(mine):
        return wide(take(mine, lo_rank)), low(take(mine, 1 - lo_rank))

    def near_joined(kept, got):
        near, rest_of = swapped([kept, wide(got)], lo_rank)
        return jnp.concatenate([near, rest_of[:, :rest]], axis=1)

    at.d_ffn = gathered()
    at.down_terms = blocks_of(low(tn(at.d_ffn, at.hidden_act)))
    at.next()
    at.down_x = [around(at.down_terms[0], "fsdp")]
    d_hidden = nn(at.d_ffn, down_full)
    at.d_gate = low(d_hidden * wide(at.slope))
    at.d_up = low(d_hidden * wide(at.activated))
    at.next()
    at.drop("d_ffn", "hidden_act", "slope", "activated")
    at.down_x += [around(at.down_terms[1], "fsdp")]
    at.gate_terms = blocks_of(low(tn(at.normed_two, at.d_gate)))
    at.next()
    at.down_far = [low(with_own(at.down_terms[i], at.down_x[i])) for i in range(2)]
    at.next()
    at.down_x += [around(at.down_terms[2], "fsdp"), around(at.down_terms[3], "fsdp")]
    at.down_got_0 = flip(at.down_far[0], "ctx", 2)
    before_sum(low(nt(at.d_gate, gate_full) + nt(at.d_up, up_full)))
    at.next()
    at.got_corner = flip(at.theirs_corner, "tp", 1)
    at.next()
    between_core_and_corners()
    at.drop("d_gate")
    at.down_rest = jnp.split(at.down_far[1], 2)
    at.next()
    sum_corners()
    at.sums = wide(at.drop("mine")[0]) + wide(flip(at.theirs, "tp", 1))
    at.gate_got = [around(at.gate_terms[0], "fsdp")]
    at.down_got_1 = flip(at.down_rest[0], "ctx", 2)
    at.next()
    between_corners_and_sides()
    at.next()
    sum_sides()
    down_terms, down_x = at.drop("down_terms", "down_x")
    at.down_own = jnp.stack([low(with_own(down_terms[i], down_x[i])) for i in (2, 3)])
    at.gate_got += [around(at.gate_terms[1], "fsdp"), around(at.gate_terms[2], "fsdp")]
    at.down_got_2 = flip(at.down_rest[1], "ctx", 2)
    up_blocks = low(tn(at.normed_two, at.d_up)).reshape(fsdp_count, 2, 2, -1, half)
    at.up_first = terms(lambda owner: take(take(up_blocks, owner), 1 - hi_rank)[0], "fsdp")
    at.up_others = terms(
        lambda owner: jnp.concatenate(
            [take(take(up_blocks, owner), 1 - hi_rank)[1:], take(take(up_blocks, owner), hi_rank)]
        ),
        "fsdp",
    )
    at.next()
    at.drop("normed_two", "d_up", "down_far", "down_rest")
    at.gate_far = [low(with_own(at.gate_terms[i], at.gate_got[i])) for i in range(2)]
    d_normed_two = summed()
    scaled = gain_mlp * d_normed_two
    inner_two = jnp.mean(scaled * residual, axis=-1, keepdims=True)
    at.d_residual = at.d_output + scale_two * scaled - residual * scale_two**3 * inner_two
    at.gain_mlp_sums = jnp.sum(d_normed_two * residual * scale_two, axis=0)
    at.part = low(at.d_residual)
    at.next()
    at.over_y = flip(at.part, "tp", 2)
    got_0, got_1, got_2 = at.drop("down_got_0", "down_got_1", "down_got_2")
    down_got = jnp.stack([got_0, jnp.concatenate([got_1, got_2], axis=0)])
    at.down_kept, at.down_sent = near_split(wide(at.drop("down_own")[0]) + wide(down_got))
    at.gate_got += [around(at.gate_terms[3], "fsdp")]
    at.up_first_got = around(at.up_first, "fsdp")
    at.gate_far_0 = flip(at.gate_far[0], "ctx", 2)
    at.next()
    at.pair = jnp.stack(at.drop("part", "over_y"))
    at.next()
    at.other = flip(at.pair, "tp", 1)
    at.up_far = jnp.split(low(with_own(*at.drop("up_first", "up_first_got"))), 2)
    gate_terms, gate_got = at.drop("gate_terms", "gate_got")
    at.gate_own = jnp.stack([low(with_own(gate_terms[i], gate_got[i])) for i in (2, 3)])
    at.next()
    pair, other = at.drop("pair", "other")
    d_attn = swapped([pair[0], other[0], pair[1], other[1]], tp_rank)
    at.d_attn = jnp.concatenate(d_attn, axis=0)
    at.next()
    at.down_got = flip(at.down_sent, "ctx", 1)
    live_columns = jnp.repeat(live, head_size).astype(jnp.float32)
    d_attended = low(nn(at.d_attn, out_part) * live_columns)
    out_grad = low(tn(at.d_attn, at.attended))

    own_rows = attn_gain.shape[0]

    def split_sums(columns):
        rounded = low(columns)
        return jnp.concatenate([rounded, low(columns - wide(rounded))], axis=-1)

    def joined_sums(columns):
        return columns[..., :64] + columns[..., 64:]

    def to_tp_back(mine):
        blocks = low(mine).reshape(tp_count, own_rows, -1)
        return [take(blocks, tp_rank ^ bit) for bit in range(tp_count)]

    def by_rows(grad):
        return grad.reshape(fsdp_count, ctx_count, tp_count * own_rows, -1)

    def halves_of(grad):
        grad = by_rows(grad)
        turned = [take(grad, (ctx_rank - by) % ctx_count, 1) for by in range(1, ctx_count + 1)]
        pairs = [jnp.stack(turned[:2], axis=1), jnp.stack(turned[2:], axis=1)]
        return [terms(lambda owner: take(pair, owner), "fsdp") for pair in pairs]

    at.out_terms = halves_of(out_grad)
    at.d_queries, at.d_keyvals = attention_backward(
        queries, keyvals, d_attended, first_key, head_size
    )
    at.up_others_got = around(at.up_others, "fsdp")
    at.gate_far_1 = flip(at.gate_far[1], "ctx", 2)
    at.up_far_0 = flip(at.up_far[0], "ctx", 2)
    at.next()
    at.drop("attended", "d_attn", "down_sent")
    kv_blocks = jnp.stack(jnp.split(at.d_keyvals, tp_count, axis=1)).reshape(2, 2, -1, kv_width)
    at.kv_kept, at.kv_sent = take(kv_blocks, core_rank, 1), take(kv_blocks, 1 - core_rank, 1)
    at.drop("d_keyvals")
    at.next()
    at.kv_got = flip(at.kv_sent, "tp", 1)
    up_others, up_others_got = at.drop("up_others", "up_others_got")
    up_rest = jnp.split(low(wide(up_others[-1][0]) + wide(up_others_got[0])), 2)
    at.up_mixed = jnp.concatenate([at.up_far[1], up_rest[0]], axis=0)
    at.up_last = up_rest[1]
    at.up_own, at.up_own_got = up_others[-1][1:], up_others_got[1:]
    gate_far_got = jnp.stack(at.drop("gate_far_0", "gate_far_1"))
    at.gate_kept, at.gate_sent = near_split(wide(at.drop("gate_own")[0]) + wide(gate_far_got))
    at.drop("gate_far")
    at.next()
    kv_sum = wide(at.kv_kept) + wide(at.kv_got)
    at.kv_kept, at.kv_sent = take(kv_sum, y_rank), low(take(kv_sum, 1 - y_rank))
    at.next()
    at.kv_got = flip(at.kv_sent, "tp", 2)
    at.up_far_1 = flip(at.up_mixed, "ctx", 2)
    at.gate_near = flip(at.gate_sent, "ctx", 1)
    at.down_out = near_joined(*at.drop("down_kept", "down_got")).T
    at.up_own = low(wide(at.up_own) + wide(at.drop("up_own_got")[0]))
    at.out_got = [around(at.out_terms[0], "fsdp")]
    d_query_raw = turn(
        at.d_queries.reshape(rows, slot_count, head_size) * query_scale,
        cosine[:, None, :],
        -sine[:, None, :],
    )
    at.d_query_low = low(d_query_raw.reshape(rows, slot_width))
    at.query_terms = halves_of(low(tn(normed, at.d_query_low)))
    at.next()
    at.drop("d_queries", "kv_sent")
    kv_sum = (at.drop("kv_kept")[0] + wide(at.drop("kv_got")[0])).reshape(reach_back + 1, rows, -1)
    at.kv_low = [low(kv_sum[reach_back - by]) for by in range(1, reach_back + 1)]
    at.d_kv = kv_sum[reach_back]
    at.out_1 = low(with_own(at.out_terms[0], at.out_got[0]))
    at.next()
    at.kv_got = [shifted(at.kv_low[by - 1], "ctx", -by) for by in range(1, reach_back + 1)]
    at.out_got += [around(at.out_terms[1], "fsdp")]
    at.next()
    d_kv = at.d_kv
    for got in at.drop("kv_got")[0]:
        d_kv = d_kv + wide(got)
    d_kv_low = low(turn(d_kv, kv_cosine, -kv_sine))
    at.d_qkv = jnp.concatenate(
        [at.d_query_low, jnp.pad(d_kv_low, ((0, 0), (0, kv_width)))], axis=1
    )
    at.next()
    at.query_got = [around(at.query_terms[0], "fsdp")]
    at.up_far_2 = flip(at.up_last, "ctx", 2)
    at.out_z = ring(at.out_1[0], "ctx")
    at.partial = low(nt(at.d_qkv, qkv_part))
    at.next()
    partial = at.partial
    blocks = partial.reshape(2, 2, part_rows, -1)
    at.kept, at.sent = take(blocks, core_rank, 1), take(blocks, 1 - core_rank, 1)
    at.next()
    at.drop("d_query_low", "kv_low", "d_kv", "gate_sent")
    at.query_1 = low(with_own(at.query_terms[0], at.query_got[0]))
    at.out_2 = with_own(at.out_terms[1], at.out_got[1])
    at.out_z = low(wide(at.out_z) + wide(at.out_1[1]))
    at.got = flip(at.sent, "tp", 1)
    at.out_z = ring(at.out_z, "ctx")
    gain_attn_sums = jnp.sum(wide(at.partial) * inputs * scale_one, axis=0)
    sums = [gain_attn_sums, at.gain_mlp_sums, jnp.full(gain_attn_sums.shape, loss_part)]
    columns = jnp.pad(jnp.stack(sums, axis=1), ((0, 0), (0, 61)))
    kv_grad = jnp.concatenate([low(tn(normed, at.d_qkv[:, slot_width : slot_width + kv_width])), split_sums(columns)], axis=1)
    at.kv_terms = terms(lambda owner: take(by_rows(kv_grad), owner), "fsdp")
    at.next()
    summed_rows = wide(at.kept) + wide(at.got)
    at.kept, at.sent = take(summed_rows, y_rank), low(take(summed_rows, 1 - y_rank))
    at.out_z = low(wide(at.out_z) + at.out_2[0])
    at.next()
    at.got = flip(at.sent, "tp", 2)
    at.query_got += [around(at.query_terms[1], "fsdp")]
    got = at.drop("up_far_0", "up_far_1", "up_far_2")
    up_far_got = jnp.concatenate(got, axis=0).reshape(2, -1, half)
    at.up_kept, up_sent = near_split(wide(at.up_own) + wide(up_far_got))
    at.up_sent = jnp.split(up_sent, 2)
    at.gate_out = near_joined(*at.drop("gate_kept", "gate_near"))
    at.query_z = ring(at.query_1[0], "ctx")
    at.out_z = ring(at.out_z, "ctx")
    at.next()
    at.query_z = low(wide(at.query_z) + wide(at.query_1[1]))
    at.next()
    at.query_2 = with_own(at.query_terms[1], at.query_got[1])
    at.d_normed = at.kept + wide(at.got)
    at.drop("partial", "d_qkv")
    at.drop("query_1", "kept", "sent", "got", "up_far", "up_mixed", "up_last", "up_own")
    at.drop("query_terms", "query_got")
    at.drop("out_terms", "out_got")
    at.query_z = ring(at.query_z, "ctx")
    at.kv_got = around(at.kv_terms, "fsdp")
    at.up_near = flip(at.up_sent[0], "ctx", 1)
    at.out_back = to_tp_back(wide(at.out_z) + at.out_2[1])
    at.next()
    at.query_z = low(wide(at.query_z) + at.query_2[0])
    kv_mine = with_own(*at.drop("kv_terms", "kv_got"))
    kv_mine = jnp.concatenate(
        [low(kv_mine[..., :kv_width]), split_sums(joined_sums(kv_mine[..., kv_width:]))], axis=-1
    )
    at.kv_own = take(kv_mine, ctx_rank)
    at.kv_sent = [take(kv_mine, (ctx_rank + by) % ctx_count) for by in range(1, ctx_count)]

    at.next()
    at.drop("out_z", "out_2")
    at.out_back = flip_tp(at.out_back)
    at.query_z = ring(at.query_z, "ctx")
    at.kv_got = [ring(at.kv_sent[by - 1], "ctx", by) for by in range(1, ctx_count)]
    at.next()
    query_mine = low(wide(at.query_z) + at.query_2[1])
    kv_mine = sum([wide(got) for got in at.kv_got], wide(at.kv_own))
    kv_mine = jnp.concatenate(
        [low(kv_mine[:, :kv_width]), split_sums(joined_sums(kv_mine[:, kv_width:]))], axis=1
    )
    at.back = to_tp_back(jnp.concatenate([query_mine, kv_mine], axis=1))
    at.next()
    up_near = jnp.concatenate([at.up_near, flip(at.up_sent[1], "ctx", 1)], axis=0)
    at.drop("query_z", "query_2", "kv_got", "kv_own", "kv_sent", "up_sent")

    def whole_heads(parts):
        columns = []
        for rank, part in enumerate(parts):
            first = rank * (slot_count - 1) + min(rank, fuller)
            base = min(first, head_count - slot_count)
            held = slot_count - 1 + (1 if rank < fuller else 0)
            start = (first - base) * head_size
            columns.append(wide(part[:, start : start + held * head_size]))
        return jnp.concatenate(columns, axis=1)

    parts = swapped(flip_tp(at.back), tp_rank)
    query_grad = whole_heads([part[:, :slot_width] for part in parts])
    out_grad = whole_heads(swapped(at.out_back, tp_rank))
    kv_parts = [wide(part[:, slot_width:]) for part in parts]
    kv_grad = jnp.concatenate([part[:, :kv_width] for part in kv_parts], axis=1)
    sums = joined_sums(sum(part[:, kv_width:] for part in kv_parts))
    gain_attn_grad, gain_mlp_grad, loss_sum = sums[:, 0], sums[:, 1], sums[0, 2]
    down_grad, gate_grad = at.down_out, at.gate_out
    up_grad = near_joined(at.up_kept, up_near)
    loss = loss_sum / (count * width)
    d_normed, d_residual = at.d_normed, at.d_residual
    scale_part = lax.dynamic_slice_in_dim(scale_one, tp_rank * part_rows, part_rows, 0)
    scaled = gain_attn * d_normed
    inner_one = jnp.mean(scaled * inputs_part, axis=-1, keepdims=True)
    input_grad = d_residual + scale_part * scaled - inputs_part * scale_part**3 * inner_one
    return (
        at.output_low[None],
        loss,
        input_grad[None],
        gain_attn_grad,
        query_grad,
        kv_grad,
        out_grad,
        gain_mlp_grad,
        gate_grad,
        up_grad,
        down_grad,
    )


def solution(mesh):
    in_specs = (
        P("fsdp", "ctx", None),
        P(),
        P("fsdp", ("ctx", "tp"), None),
        P(("fsdp", "ctx", "tp")),
        P(("fsdp", "ctx", "tp"), None),
        P(("fsdp", "ctx", "tp"), None),
        P(("fsdp", "ctx", "tp"), None),
        P(("fsdp", "ctx", "tp")),
        P(("fsdp", "ctx"), "tp"),
        P(("fsdp", "ctx"), "tp"),
        P("tp", ("fsdp", "ctx")),
    )
    out_specs = (
        P("fsdp", ("ctx", "tp"), None),
        P(),
        P("fsdp", ("ctx", "tp"), None),
        P(("fsdp", "ctx", "tp")),
        P(("fsdp", "ctx", "tp"), None),
        P(("fsdp", "ctx", "tp"), None),
        P(("fsdp", "ctx", "tp"), None),
        P(("fsdp", "ctx", "tp")),
        P(("fsdp", "ctx"), "tp"),
        P(("fsdp", "ctx"), "tp"),
        P("tp", ("fsdp", "ctx")),
    )
    return jax.shard_map(local, mesh=mesh, in_specs=in_specs, out_specs=out_specs, check_vma=False)
```
